512 devices in a mesh: grp: 16 (over z), ty: 8 (over x, core), tx: 4 (over y).
Axes of the slice: x: 4, y: 4, z: 16, core: 2. Of those that a mesh axis runs over, the one named last changes fastest.
Arguments:
- images: float32 [4, 3, 8192, 512], P(None, None, ('grp', 'ty'), 'tx'), parts along dimension 2, may hold values from -16 to 16
- gains: float32 [4, 3], replicated, may hold values from 0.5 to 2
- labels: int32 [8192, 512], P(('grp', 'ty'), 'tx'), parts along dimension 0, may hold values from 0 to 3, as said below
Outputs:
- blended: float32 [3, 8192, 512], P(None, ('grp', 'ty'), 'tx'), parts along dimension 1
The draws below stay inside these ranges and needn't reach their ends.
There are 16 independent parts, one for each index of `grp`. The reference program is written for one: setup_inputs(seed, part) draws one part's arguments, and reference() takes and returns one part's arrays. A program takes and returns all parts, laid end to end along the dimension named above; an argument that names none is the same for every part. Nothing has to cross between parts.
Inputs may be any that keep to these rules, and one draw needn't show every extreme that they name: labels are constant on aligned 8 x 8 blocks of pixels.
All inputs are finite; a program needn't handle non-finite values.
Results may differ from the reference program's by a relative error of at most 0.0001.
Values sent between devices are 32-bit elements; how exact they have to be, the bound alone decides.
No kernel may reach another device: no remote copies, remote signals or barrier semaphores. Data moves between devices by JAX's collectives and lax.ppermute only.
A program may use at most 64 MiB of HBM per device.

```python
import math
import jax
import jax.numpy as jnp

EXPOSURES = 4
BANDS = 3
LEVELS = 6
ROWS = 512
COLS = 512


def wave_term(keys, rows, cols, index):
    shape_c = (EXPOSURES, BANDS, 1, 1)
    freq_r = jax.random.uniform(jax.random.fold_in(keys[0], index), shape_c, jnp.float32, 0.3, 2.0)
    freq_c = jax.random.uniform(jax.random.fold_in(keys[1], index), shape_c, jnp.float32, 0.3, 2.0)
    phase_r = jax.random.uniform(jax.random.fold_in(keys[2], index), shape_c, jnp.float32, -math.pi, math.pi)
    phase_c = jax.random.uniform(jax.random.fold_in(keys[3], index), shape_c, jnp.float32, -math.pi, math.pi)
    amps = jax.random.uniform(jax.random.fold_in(keys[4], index), shape_c, jnp.float32, 0.5, 1.5)
    along_rows = jnp.cos(2.0 * math.pi * freq_r * rows[None, None, :, None] + phase_r)
    along_cols = jnp.cos(2.0 * math.pi * freq_c * cols[None, None, None, :] + phase_c)
    return amps * along_rows * along_cols


def draw_images(key, part):
    key = jax.random.fold_in(key, 7)
    keys = jax.random.split(key, 9)
    rows = (jnp.arange(ROWS, dtype=jnp.float32) + 0.5) / ROWS
    cols = (jnp.arange(COLS, dtype=jnp.float32) + 0.5) / COLS
    shape_c = (EXPOSURES, BANDS, 1, 1)
    offset = jax.random.uniform(keys[5], shape_c, jnp.float32, -2.0, 2.0)
    slope_r = jax.random.uniform(keys[6], shape_c, jnp.float32, -2.0, 2.0)
    slope_c = jax.random.uniform(keys[7], shape_c, jnp.float32, -2.0, 2.0)
    smooth = offset + slope_r * (rows[None, None, :, None] - 0.5) + slope_c * (cols[None, None, None, :] - 0.5)
    smooth = smooth + wave_term(keys, rows, cols, 0) + wave_term(keys, rows, cols, 1)
    shape = (EXPOSURES, BANDS, ROWS, COLS)
    noise = jax.random.truncated_normal(keys[8], -4.0, 4.0, shape, jnp.float32)
    return smooth + noise


def draw_labels(key, part):
    key = jax.random.fold_in(key, 5)
    blocks = jax.random.randint(key, (ROWS // 8, COLS // 8), 0, EXPOSURES, dtype=jnp.int32)
    return jnp.repeat(jnp.repeat(blocks, 8, axis=0), 8, axis=1)


def setup_inputs(seed: int = 0, part: int = 0) -> dict:
    key_of = jax.random.split(jax.random.key(seed), 4)
    own_keys = jax.random.split(jax.random.fold_in(key_of[3], part), 4)
    return {
        "images": draw_images(jax.random.fold_in(jax.random.fold_in(key_of[3], part), 71), part),
        "gains": jnp.clip(jnp.exp(jax.random.uniform(key_of[1], (EXPOSURES, BANDS), jnp.float32, math.log(0.5), math.log(2.0))), 0.5, 2.0),
        "labels": draw_labels(jax.random.fold_in(jax.random.fold_in(key_of[3], part), 71), part),
    }


TAPS = (0.0625, 0.25, 0.375, 0.25, 0.0625)


def reduce_level(padded):
    height = (padded.shape[1] - 4) // 2
    width = (padded.shape[2] - 4) // 2
    across = TAPS[0] * padded[:, 0:2 * height:2, :]
    for offset in range(1, 5):
        across = across + TAPS[offset] * padded[:, offset:offset + 2 * height:2, :]
    result = TAPS[0] * across[:, :, 0:2 * width:2]
    for offset in range(1, 5):
        result = result + TAPS[offset] * across[:, :, offset:offset + 2 * width:2]
    return result


def expand_level(padded):
    channels = padded.shape[0]
    height = padded.shape[1] - 2
    width = padded.shape[2] - 2
    centre = padded[:, 1:-1, :]
    below = padded[:, :-2, :]
    above = padded[:, 2:, :]
    even_rows = (6.0 * centre + below + above) * 0.125
    odd_rows = (centre + above) * 0.5
    tall = jnp.stack([even_rows, odd_rows], axis=2).reshape(channels, 2 * height, width + 2)
    centre = tall[:, :, 1:-1]
    below = tall[:, :, :-2]
    above = tall[:, :, 2:]
    even_cols = (6.0 * centre + below + above) * 0.125
    odd_cols = (centre + above) * 0.5
    return jnp.stack([even_cols, odd_cols], axis=3).reshape(channels, 2 * height, 2 * width)


def blend_bands(masks, laplace):
    planes = laplace.reshape(masks.shape[0], -1, laplace.shape[1], laplace.shape[2])
    return jnp.sum(masks[:, None] * planes, axis=0)


def pad_by(values, width):
    return jnp.pad(values, ((0, 0), (width, width), (width, width)))


def reference(images, gains, labels):
    inner = EXPOSURES * BANDS
    gained = (images * gains[:, :, None, None]).reshape(inner, images.shape[2], images.shape[3])
    masks = (labels[None] == jnp.arange(EXPOSURES, dtype=jnp.int32)[:, None, None]).astype(jnp.float32)
    gauss = [jnp.concatenate([gained, masks], 0)]
    for level in range(LEVELS):
        gauss.append(reduce_level(pad_by(gauss[-1], 2)))
    result = blend_bands(gauss[LEVELS][inner:], gauss[LEVELS][:inner])
    for level in range(LEVELS - 1, -1, -1):
        laplace = gauss[level][:inner] - expand_level(pad_by(gauss[level + 1][:inner], 1))
        result = blend_bands(gauss[level][inner:], laplace) + expand_level(pad_by(result, 1))
    return result
```

```python
import jax
import jax.numpy as jnp
from jax import lax
from jax.experimental import pallas as pl
from jax.experimental.pallas import tpu as pltpu
from jax.sharding import PartitionSpec as P

EXPOSURES = 4
BANDS = 3
INNER = EXPOSURES * BANDS
PLANES = INNER + EXPOSURES
LANES = 128

SIDE = (64, 32, 16, 8, 4, 2, 1)
WIDE = (128, 64, 32, 16, 8, 4, 2)
ROWS = (64, 40, 24, 16, 8, 8, 8)
RIM = (0, 2, 3, 3, 3)
LEVEL_AT = (0, 0, 40, 64, 80)
PACKED = 88
PITCH_5 = 16
PITCH_6 = 8
AT_6 = 80
HALF = LANES // 2

f32 = jnp.float32
bf16 = jnp.bfloat16


def iota(shape, dim):
    return lax.broadcasted_iota(jnp.int32, shape, dim)


def reduce_weights(first):
    tap = iota((LANES, LANES), 0) - 2 * iota((LANES, LANES), 1) + first
    near = jnp.where((tap == 1) | (tap == 3), 0.25, 0.0)
    ends = jnp.where((tap == 0) | (tap == 4), 0.0625, 0.0)
    weights = jnp.where(tap == 2, 0.375, near + ends).astype(bf16)
    return jnp.concatenate([weights, weights], 0)


def expand_taps(source, target):
    half = jnp.bitwise_and(target, 1)
    away = 2 * source - target
    even = jnp.where(away == 0, 0.75, 0.0) + jnp.where((away == 2) | (away == -2), 0.125, 0.0)
    odd = jnp.where((away == 1) | (away == -1), 0.5, 0.0)
    return jnp.where(half == 1, odd, even)


def expand_weights(first):
    shape = (LANES, LANES)
    weights = expand_taps(iota(shape, 0) - 1, iota(shape, 1) - first).astype(bf16)
    return jnp.concatenate([weights, weights], 0)


def split_dot(values, weights):
    high = values.astype(bf16)
    low = (values - high.astype(f32)).astype(bf16)
    return jnp.dot(jnp.concatenate([high, low], 1), weights, preferred_element_type=f32)


def in_slab(level, row, col, rows, cols):
    shape = (ROWS[level], LANES)
    along, across = iota(shape, 0), iota(shape, 1)
    first = jnp.where(row == 0, 1, 0)
    last = jnp.where(row == rows - 1, SIDE[level] + 1, ROWS[level])
    left = jnp.where(col == 0, 1, 0)
    right = jnp.where(col == cols - 1, WIDE[level] + 1, LANES)
    return (along >= first) & (along < last) & (across >= left) & (across < right)


def expand_rows(source, target, count):
    before = source[:, 0:count, :]
    centre = source[:, 1 : count + 1, :]
    after = source[:, 2 : count + 2, :]
    target[:, pl.ds(0, count, stride=2), :] = (before + centre) * 0.5
    target[:, pl.ds(1, count, stride=2), :] = centre * 0.75 + (before + after) * 0.125


def expand_rows_tile(source, target, count):
    before = source[:, 0:count, :]
    centre = source[:, 1 : count + 1, :]
    after = source[:, 2 : count + 2, :]
    target[:, pl.ds(0, count, stride=2), :] = centre * 0.75 + (before + after) * 0.125
    target[:, pl.ds(1, count, stride=2), :] = (centre + after) * 0.5


def pairs_of(level):
    return {0: 32, 1: 20, 2: 12, 3: 6, 4: 4}[level]


def partial_kernel(
    grid, place, gains, images, labels, x1, x2, x3, x4, packed, send_a, send_b, patch,
    s0, s1, s2, s3, s4, s5, y5, y6, across, strips, turned, low, high,
):
    row, col = place[0], place[1]
    s0[:, 0:8, :] = jnp.zeros((PLANES, 8, LANES), f32)
    s0[:, 72:88, :] = jnp.zeros((PLANES, 16, LANES), f32)
    for e in range(EXPOSURES):
        for b in range(BANDS):
            s0[e * BANDS + b, 8:72, :] = images[e * BANDS + b] * gains[e, b]
        s0[INNER + e, 8:72, :] = jnp.where(labels[...] == e, 1.0, 0.0)

    def reduce(source, level, first, weights):
        count = ROWS[level]
        for p in range(PLANES):
            tap = [source[p, pl.ds(first + k, count, stride=2), :] for k in range(5)]
            total = tap[2] * 0.375 + (tap[1] + tap[3]) * 0.25 + (tap[0] + tap[4]) * 0.0625
            across[p * count : (p + 1) * count, :] = total
        result = split_dot(across[0 : PLANES * count, :], weights)
        inside = in_slab(level, row, col, *grid)
        return jnp.where(inside[None], result.reshape(PLANES, count, LANES), 0.0)

    def keep(store, result):
        count, depth = result.shape[1], store.shape[1]
        store[:, 0:8, :] = jnp.zeros((PLANES, 8, LANES), f32)
        store[:, 8 : 8 + count, :] = result
        if depth > 8 + count:
            store[:, 8 + count : depth, :] = jnp.zeros((PLANES, depth - 8 - count, LANES), f32)

    weights = reduce_weights(3)
    result = reduce(s0, 1, 4, reduce_weights(4))
    x1[...] = result
    keep(s1, result)
    for level, source, store, out in ((2, s1, s2, x2), (3, s2, s3, x3), (4, s3, s4, x4)):
        result = reduce(source, level, 5, weights)
        out[...] = result
        keep(store, result)
    result = reduce(s4, 5, 5, weights)
    y5[...] = result.reshape(PLANES * 8, LANES)
    keep(s5, result)
    y6[...] = reduce(s5, 6, 5, weights).reshape(PLANES * 8, LANES)

    coarse = jnp.zeros((PLANES, LANES), f32)
    for k in range(SIDE[5] + 3):
        line = y5[pl.ds(k, PLANES, stride=8), :]
        coarse = coarse + (pltpu.roll(line, PITCH_5 * k, 1) if k else line)
    for k in range(SIDE[6] + 3):
        coarse = coarse + pltpu.roll(y6[pl.ds(k, PLANES, stride=8), :], AT_6 + PITCH_6 * k, 1)
    patch[...] = coarse

    levels = (None, x1, x2, x3, x4)
    for level in range(1, 5):
        count, wide = ROWS[level], WIDE[level]
        lane = iota((count, LANES), 1)
        total = jnp.zeros((count, LANES), f32)
        for p in range(PLANES):
            plane = levels[level][p]
            at = 6 * p
            first = pltpu.roll(plane, at, 1) if at else plane
            last = pltpu.roll(plane, (at + 3 - wide) % LANES, 1)
            total = jnp.where((lane >= at) & (lane < at + 3), first, total)
            total = jnp.where((lane >= at + 3) & (lane < at + 6), last, total)
        strips[LEVEL_AT[level] : LEVEL_AT[level] + count, :] = total

    packed[...] = jnp.zeros((PACKED, LANES), f32)
    for here, there, count in packing():
        packed[here : here + count, :] = strips[there : there + count, :]

    for p in range(PLANES):
        turned[p] = pltpu.roll(x4[p], HALF, 1)
    for rim, at in ((low, (0, 0, 0, 0, 0)), (high, SIDE)):
        rim[0:PLANES, 0:2, :] = x1[:, at[1] : at[1] + 2, :]
        rim[0:PLANES, 2:5, :] = x2[:, at[2] : at[2] + 3, :]
        rim[0:PLANES, 5:8, :] = x3[:, at[3] : at[3] + 3, :] + turned[:, at[4] : at[4] + 3, :]
    for k in range(2):
        low[PLANES + k] = packed[8 * k : 8 * k + 8, :]
        high[PLANES + k] = packed[16 + 8 * k : 24 + 8 * k, :]
    odd = jnp.bitwise_and(row, 1) == 1
    send_a[...] = jnp.where(odd, low[...], high[...])
    send_b[...] = jnp.where(odd, high[...], low[...])


def packing():
    moves = []
    for start, last in ((0, False), (16, True)):
        here = start
        for level in range(1, 5):
            there = LEVEL_AT[level] + (SIDE[level] if last else 0)
            moves.append((here, there, RIM[level]))
            here += RIM[level]
    here = 32
    for level in range(1, 5):
        count = SIDE[level] - RIM[level]
        moves.append((here, LEVEL_AT[level] + RIM[level], count))
        here += count
    return moves


def fine_kernel(
    place, gains, images, labels, x1, x2, x3, x4, got_a, got_b, side_a, side_b,
    b0, b1, b2, b3, t4,
    t1, t2, t3, left, right, low, high, turned, across, spread,
):
    row_odd = jnp.bitwise_and(place[0], 1) == 1
    col_odd = jnp.bitwise_and(place[1], 1) == 1
    low[...] = jnp.where(row_odd, got_a[0:PLANES], got_b[0:PLANES])
    high[...] = jnp.where(row_odd, got_b[0:PLANES], got_a[0:PLANES])
    turned[0] = jnp.where(col_odd, side_a[...], side_b[...])
    turned[1] = jnp.where(col_odd, side_b[...], side_a[...])
    left[...] = jnp.zeros((PACKED, LANES), f32)
    right[...] = jnp.zeros((PACKED, LANES), f32)
    for here, there, count in packing():
        left[there : there + count, :] = turned[0, here : here + count, :]
        right[there : there + count, :] = turned[1, here : here + count, :]

    totals = (None, t1, t2, t3, t4)
    parts = (None, x1, x2, x3, x4)
    for level in range(1, 5):
        totals[level][...] = parts[level][...]
    for rim, at in ((low, (0, 0, 0, 0, 0)), (high, SIDE)):
        t1[:, at[1] : at[1] + 2, :] += rim[:, 0:2, :]
        t2[:, at[2] : at[2] + 3, :] += rim[:, 2:5, :]
        t3[:, at[3] : at[3] + 3, :] += rim[:, 5:8, :]
        for p in range(PLANES):
            rim[p] = pltpu.roll(rim[p], HALF, 1)
        t4[:, at[4] : at[4] + 3, :] += rim[:, 5:8, :]
    for level in range(1, 5):
        count, wide, at = ROWS[level], WIDE[level], LEVEL_AT[level]
        lane = iota((count, LANES), 1)
        from_left = left[at : at + count, :]
        from_right = right[at : at + count, :]
        for p in range(PLANES):
            first = pltpu.roll(from_left, (-6 * p - 3) % LANES, 1)
            last = pltpu.roll(from_right, (wide - 6 * p) % LANES, 1)
            last = jnp.where((lane >= wide) & (lane < wide + 3), last, 0.0)
            totals[level][p] = totals[level][p] + jnp.where(lane < 3, first, last)

    weights = expand_weights(1)
    for level in (3, 2, 1):
        above, count, out = totals[level + 1], ROWS[level + 1], (None, b1, b2, b3)[level]
        coarse = above[0:INNER].reshape(INNER * count, LANES)
        across[:, 0:count, :] = split_dot(coarse, weights).reshape(INNER, count, LANES)
        if level == 3:
            spread[:, 0 : ROWS[3], :] = jnp.zeros((INNER, ROWS[3], LANES), f32)
        expand_rows(across, spread, pairs_of(level))
        for b in range(BANDS):
            total = jnp.zeros((ROWS[level], LANES), f32)
            for e in range(EXPOSURES):
                p = e * BANDS + b
                laplace = totals[level][p] - spread[p, 0 : ROWS[level], :]
                total = total + totals[level][INNER + e] * laplace
            out[b] = total
    across[...] = split_dot(t1[0:INNER].reshape(INNER * ROWS[1], LANES), expand_weights(0)).reshape(
        INNER, ROWS[1], LANES
    )
    expand_rows_tile(across, spread, pairs_of(0))
    for b in range(BANDS):
        total = jnp.zeros((ROWS[0], LANES), f32)
        for e in range(EXPOSURES):
            p = e * BANDS + b
            laplace = images[p] * gains[e, b] - spread[p]
            total = total + jnp.where(labels[...] == e, laplace, 0.0)
        b0[b] = total


def collapse_kernel(
    grid, place, patches, b0, b1, b2, b3, t4, out,
    v5, v6, window, c4, c3, c2, c1, across, spread,
):
    rows, cols = grid
    row, col = place[0], place[1]
    lane = iota((PLANES, LANES), 1)
    zero = jnp.zeros((PLANES, LANES), f32)
    five, six = [zero, zero], zero
    for r in range(rows):
        for c in range(cols):
            at = (r * cols + c) * PLANES
            source = patches[at : at + PLANES, :]
            start = PITCH_5 * (SIDE[5] * r - 1) + WIDE[5] * c - 1
            stop = start + AT_6
            turned = pltpu.roll(source, start % LANES, 1)
            for k in range(2):
                begin, end = max(start - LANES * k, 0), min(stop - LANES * k, LANES)
                if begin < end:
                    five[k] = five[k] + jnp.where((lane >= begin) & (lane < end), turned, 0.0)
            start = PITCH_6 * (r - 1) + WIDE[6] * c - 1
            begin, end = max(start, 0), min(start + 4 * PITCH_6, PITCH_6 * rows)
            turned = pltpu.roll(source, (start - AT_6) % LANES, 1)
            six = six + jnp.where((lane >= begin) & (lane < end), turned, 0.0)

    def blend(planes, less):
        total = None
        for e in range(EXPOSURES):
            part = planes[e * BANDS : (e + 1) * BANDS, :]
            if less is not None:
                part = part - less[e * BANDS : (e + 1) * BANDS, :]
            part = part * planes[INNER + e : INNER + e + 1, :]
            total = part if total is None else total + part
        return total

    v6[...] = six
    top = blend(v6, None)
    v6[INNER : INNER + BANDS, :] = top
    v6[INNER + BANDS : PLANES, :] = jnp.zeros((1, LANES), f32)
    source, target = iota((LANES, 2 * LANES), 0), iota((LANES, 2 * LANES), 1)
    along = expand_taps(lax.shift_right_logical(source, 3), lax.shift_right_logical(target, 4))
    aside = expand_taps(jnp.bitwise_and(source, 7), jnp.bitwise_and(target, 15))
    weights = (along * aside).astype(bf16)
    weights = jnp.concatenate([weights, weights], 0)
    v5[:, 0:LANES] = five[0]
    v5[:, LANES : 2 * LANES] = five[1]
    window_5 = split_dot(v6[...], weights)
    spread_5 = spread
    spread_5[0, 0:PLANES, :] = window_5[:, 0:LANES]
    spread_5[1, 0:PLANES, :] = window_5[:, LANES : 2 * LANES]
    for k in range(2):
        planes = v5[:, LANES * k : LANES * k + LANES]
        less = spread_5[k, 0:PLANES, :]
        v5[INNER : INNER + BANDS, LANES * k : LANES * k + LANES] = (
            blend(planes, less) + less[INNER : INNER + BANDS, :]
        )
    v5[INNER + BANDS : PLANES, :] = jnp.zeros((1, 2 * LANES), f32)

    window[...] = jnp.zeros((PLANES * 8, LANES), f32)
    first, second = v5[:, 0:LANES], v5[:, LANES : 2 * LANES]
    where = lane + (WIDE[5] * col - 1)
    valid = (where >= 0) & (where < WIDE[5] * cols) & (lane < WIDE[5] + 3)
    for k in range(SIDE[5] + 3):
        line = SIDE[5] * row - 1 + k
        start = PITCH_5 * jnp.bitwise_and(line, 7) + WIDE[5] * col - 1
        turned = pltpu.roll(jnp.where(line < 8, first, second), jnp.bitwise_and(-start, LANES - 1), 1)
        held = valid & (line >= 0) & (line < SIDE[5] * rows)
        window[pl.ds(k, PLANES, stride=8), :] = jnp.where(held, turned, 0.0)

    weights = expand_weights(1)
    across[:, 0:8, :] = split_dot(window[...], weights).reshape(PLANES, 8, LANES)
    expand_rows(across, spread, pairs_of(4))
    inside = in_slab(4, row, col, rows, cols)
    for b in range(BANDS):
        total = spread[INNER + b, 0:8, :]
        for e in range(EXPOSURES):
            p = e * BANDS + b
            total = total + t4[INNER + e] * (t4[p] - spread[p, 0:8, :])
        c4[b] = jnp.where(inside, total, 0.0)
    c4[BANDS] = jnp.zeros((8, LANES), f32)

    for level, source, target, band in ((3, c4, c3, b3), (2, c3, c2, b2), (1, c2, c1, b1)):
        count, depth = ROWS[level + 1], ROWS[level]
        wide = split_dot(source[...].reshape(EXPOSURES * count, LANES), weights)
        across[0:EXPOSURES, 0:count, :] = wide.reshape(EXPOSURES, count, LANES)
        some = spread.at[0:EXPOSURES]
        if level == 3:
            some[:, 0:depth, :] = jnp.zeros((EXPOSURES, depth, LANES), f32)
        expand_rows(across.at[0:EXPOSURES], some, pairs_of(level))
        inside = in_slab(level, row, col, rows, cols)
        for b in range(BANDS):
            target[b] = jnp.where(inside, band[b] + spread[b, 0:depth, :], 0.0)
        target[BANDS] = jnp.zeros((depth, LANES), f32)
    wide = split_dot(c1[...].reshape(EXPOSURES * ROWS[1], LANES), expand_weights(0))
    across[0:EXPOSURES] = wide.reshape(EXPOSURES, ROWS[1], LANES)
    expand_rows_tile(across.at[0:BANDS], spread.at[0:BANDS], pairs_of(0))
    out[...] = b0[...] + spread[0:BANDS]


VMEM = pl.BlockSpec(memory_space=pltpu.VMEM)
SMEM = pl.BlockSpec(memory_space=pltpu.SMEM)
PARAMS = pltpu.CompilerParams(vmem_limit_bytes=32 * 1024 * 1024)


def floats(*shape):
    return jax.ShapeDtypeStruct(shape, f32)


def scratch(*shape):
    return pltpu.VMEM(shape, f32)


def swaps(size, first):
    return [p for i in range(first, size - 1, 2) for p in ((i, i + 1), (i + 1, i))]


def shards(images, gains, labels):
    rows, cols = lax.axis_size("ty"), lax.axis_size("tx")
    grid = (rows, cols)
    row, col = lax.axis_index("ty"), lax.axis_index("tx")
    place = jnp.stack([row, col]).astype(jnp.int32)
    images = images.reshape(INNER, ROWS[0], LANES)
    levels = [floats(PLANES, ROWS[level], LANES) for level in range(1, 5)]
    x1, x2, x3, x4, packed, send_a, send_b, patch = pl.pallas_call(
        lambda *refs: partial_kernel(grid, *refs),
        out_shape=[
            *levels,
            floats(PACKED, LANES),
            floats(PLANES + 2, 8, LANES),
            floats(PLANES + 2, 8, LANES),
            floats(PLANES, LANES),
        ],
        in_specs=[SMEM, SMEM, VMEM, VMEM],
        out_specs=[VMEM] * 8,
        scratch_shapes=[
            scratch(PLANES, 88, LANES),
            scratch(PLANES, 56, LANES),
            scratch(PLANES, 40, LANES),
            scratch(PLANES, 24, LANES),
            scratch(PLANES, 24, LANES),
            scratch(PLANES, 24, LANES),
            scratch(PLANES * 8, LANES),
            scratch(PLANES * 8, LANES),
            scratch(PLANES * ROWS[1], LANES),
            scratch(PACKED, LANES),
            scratch(PLANES, 8, LANES),
            scratch(PLANES + 2, 8, LANES),
            scratch(PLANES + 2, 8, LANES),
        ],
        compiler_params=PARAMS,
        name="partial_levels",
    )(place, gains, images, labels)
    patches = lax.all_gather(patch, ("ty", "tx"), axis=0, tiled=True)
    got_a = lax.ppermute(send_a, "ty", swaps(rows, 0))
    got_b = lax.ppermute(send_b, "ty", swaps(rows, 1))
    rim_a = got_a[PLANES:].reshape(16, LANES)
    rim_b = got_b[PLANES:].reshape(16, LANES)
    odd = row % 2 == 1
    rims = jnp.concatenate([jnp.where(odd, rim_a, rim_b), jnp.where(odd, rim_b, rim_a)], 0)
    whole = packed + jnp.pad(rims, ((0, PACKED - 32), (0, 0)))
    side_a = lax.ppermute(whole, "tx", swaps(cols, 0))
    side_b = lax.ppermute(whole, "tx", swaps(cols, 1))
    b0, b1, b2, b3, t4 = pl.pallas_call(
        fine_kernel,
        out_shape=[floats(BANDS, ROWS[level], LANES) for level in range(4)] + [levels[3]],
        in_specs=[SMEM, SMEM] + [VMEM] * 10,
        out_specs=[VMEM] * 5,
        scratch_shapes=[
            scratch(PLANES, ROWS[1], LANES),
            scratch(PLANES, ROWS[2], LANES),
            scratch(PLANES, ROWS[3], LANES),
            scratch(PACKED, LANES),
            scratch(PACKED, LANES),
            scratch(PLANES, 8, LANES),
            scratch(PLANES, 8, LANES),
            scratch(2, PACKED, LANES),
            scratch(INNER, ROWS[1], LANES),
            scratch(INNER, ROWS[0], LANES),
        ],
        compiler_params=PARAMS,
        name="fine_laplacians",
    )(place, gains, images, labels, x1, x2, x3, x4, got_a, got_b, side_a, side_b)
    return pl.pallas_call(
        lambda *refs: collapse_kernel(grid, *refs),
        out_shape=floats(BANDS, ROWS[0], LANES),
        in_specs=[SMEM] + [VMEM] * 6,
        out_specs=VMEM,
        scratch_shapes=[
            scratch(PLANES, 2 * LANES),
            scratch(PLANES, LANES),
            scratch(PLANES * 8, LANES),
            scratch(EXPOSURES, ROWS[4], LANES),
            scratch(EXPOSURES, ROWS[3], LANES),
            scratch(EXPOSURES, ROWS[2], LANES),
            scratch(EXPOSURES, ROWS[1], LANES),
            scratch(PLANES, ROWS[1], LANES),
            scratch(PLANES, ROWS[0], LANES),
        ],
        compiler_params=PARAMS,
        name="collapse",
    )(place, patches, b0, b1, b2, b3, t4)


def solution(mesh):
    placed = (P(None, None, ("grp", "ty"), "tx"), P(), P(("grp", "ty"), "tx"))
    return jax.shard_map(
        shards, mesh=mesh, in_specs=placed, out_specs=P(None, ("grp", "ty"), "tx"), check_vma=False
    )
```

```python
import jax
import jax.numpy as jnp
from jax import lax
from jax.experimental import pallas as pl
from jax.experimental.pallas import tpu as pltpu
from jax.sharding import PartitionSpec as P

EXPOSURES = 4
BANDS = 3
INNER = EXPOSURES * BANDS
PLANES = INNER + EXPOSURES
LANES = 128
HALF = LANES // 2

SIDE = (64, 32, 16, 8, 4, 2, 1)
WIDE = (128, 64, 32, 16, 8, 4, 2)
ROWS = (64, 40, 24, 16, 8, 8, 8)
PAIRS = (32, 20, 12, 6, 4)
SLOTS = 3
MOVES = (
    (1, 0, 0, 0), (1, 1, 1, 0),
    (2, 0, 0, 66), (2, 1, 1, 66), (2, 2, 2, 0),
    (3, 0, 2, 35), (3, 1, 2, 54), (3, 2, 2, 73),
    (4, 0, 2, 92), (4, 1, 2, 103), (4, 2, 2, 114),
)
STRIP_AT = (0, 0, 0, 24, 40)
STRIP = 48
PITCH_5 = 16
PITCH_6 = 8
AT_6 = 80
RIMS = 2 * SLOTS + 6
COARSE = 6

f32 = jnp.float32
bf16 = jnp.bfloat16


def iota(shape, dim):
    return lax.broadcasted_iota(jnp.int32, shape, dim)


def reduce_weights(first):
    tap = iota((LANES, LANES), 0) - 2 * iota((LANES, LANES), 1) + first
    near = jnp.where((tap == 1) | (tap == 3), 0.25, 0.0)
    ends = jnp.where((tap == 0) | (tap == 4), 0.0625, 0.0)
    weights = jnp.where(tap == 2, 0.375, near + ends).astype(bf16)
    return jnp.concatenate([weights, weights], 0)


def expand_taps(source, target):
    away = 2 * source - target
    even = jnp.where(away == 0, 0.75, 0.0) + jnp.where((away == 2) | (away == -2), 0.125, 0.0)
    odd = jnp.where((away == 1) | (away == -1), 0.5, 0.0)
    return jnp.where(jnp.bitwise_and(target, 1) == 1, odd, even)


def expand_weights(first):
    shape = (LANES, LANES)
    weights = expand_taps(iota(shape, 0) - 1, iota(shape, 1) - first).astype(bf16)
    return jnp.concatenate([weights, weights], 0)


def split_dot(values, weights):
    high = values.astype(bf16)
    low = (values - high.astype(f32)).astype(bf16)
    return jnp.dot(jnp.concatenate([high, low], 1), weights, preferred_element_type=f32)


def in_slab(level, row, col, rows, cols):
    shape = (ROWS[level], LANES)
    along, across = iota(shape, 0), iota(shape, 1)
    first = jnp.where(row == 0, 1, 0)
    last = jnp.where(row == rows - 1, SIDE[level] + 1, ROWS[level])
    left = jnp.where(col == 0, 1, 0)
    right = jnp.where(col == cols - 1, WIDE[level] + 1, LANES)
    return (along >= first) & (along < last) & (across >= left) & (across < right)


def expand_rows(source, target, count):
    before = source[:, 0:count, :]
    centre = source[:, 1 : count + 1, :]
    after = source[:, 2 : count + 2, :]
    target[:, pl.ds(0, count, stride=2), :] = (before + centre) * 0.5
    target[:, pl.ds(1, count, stride=2), :] = centre * 0.75 + (before + after) * 0.125


def expand_rows_tile(source, target, count):
    before = source[:, 0:count, :]
    centre = source[:, 1 : count + 1, :]
    after = source[:, 2 : count + 2, :]
    target[:, pl.ds(0, count, stride=2), :] = centre * 0.75 + (before + after) * 0.125
    target[:, pl.ds(1, count, stride=2), :] = (centre + after) * 0.5


def plane_of(level, p):
    return pl.ds(p * ROWS[level], ROWS[level])


def line_of(level, line):
    return pl.ds(line, PLANES, stride=ROWS[level])


def partial_kernel(
    rows, cols, images, gains, labels,
    x1, x2, x3, x4, send_a, send_b, strip_a, strip_b,
    s0, s1, s2, s3, s4, s5, y5, y6, across, label, gain, first_part, other_part, low, high, done,
):
    row, col = lax.axis_index("ty"), lax.axis_index("tx")
    s0[:, 0:8, :] = jnp.zeros((PLANES, 8, LANES), f32)
    s0[:, 72:88, :] = jnp.zeros((PLANES, 16, LANES), f32)
    copies = [pltpu.make_async_copy(labels, label, done.at[INNER])]
    copies.append(pltpu.make_async_copy(gains, gain, done.at[INNER + 1]))
    for p in range(INNER):
        copies.append(pltpu.make_async_copy(images.at[p], s0.at[p, pl.ds(8, 64)], done.at[p]))
    for copy in copies:
        copy.start()
    for store in (s1, s2, s3, s4, s5):
        depth = store.shape[1]
        store[:, 0:8, :] = jnp.zeros((PLANES, 8, LANES), f32)
        store[:, depth - 8 : depth, :] = jnp.zeros((PLANES, 8, LANES), f32)
    edge_weights, weights = reduce_weights(4), reduce_weights(3)

    def reduce_rows(source, level, first, planes, scales):
        count = ROWS[level]
        for p in planes:
            tap = [source[p, pl.ds(first + k, count, stride=2), :] for k in range(5)]
            total = tap[2] * 0.375 + (tap[1] + tap[3]) * 0.25 + (tap[0] + tap[4]) * 0.0625
            across[plane_of(level, p), :] = total if scales is None else total * scales[p]

    def reduce_columns(level, planes, weights):
        count, held = ROWS[level], planes[-1] + 1 - planes[0]
        inside = in_slab(level, row, col, rows, cols)
        values = across[pl.ds(planes[0] * count, held * count), :]
        result = split_dot(values, weights).reshape(held, count, LANES)
        return jnp.where(inside[None], result, 0.0)

    def finish(level, planes, result, store, out):
        count, held = ROWS[level], len(planes)
        if out is not None:
            out[pl.ds(planes[0] * count, held * count), :] = result.reshape(held * count, LANES)
        if store is not None:
            store[planes[0] : planes[0] + held, 8 : 8 + count, :] = result

    copies[0].wait()
    for e in range(EXPOSURES):
        s0[INNER + e, 8:72, :] = jnp.where(label[...] == e, 1.0, 0.0)
    planes = range(INNER, PLANES)
    reduce_rows(s0, 1, 4, planes, None)
    finish(1, planes, reduce_columns(1, planes, edge_weights), s1, x1)
    copies[1].wait()
    for e in range(EXPOSURES):
        planes = range(e * BANDS, (e + 1) * BANDS)
        scales = {e * BANDS + b: gain[e, b] for b in range(BANDS)}
        for p in planes:
            copies[2 + p].wait()
        reduce_rows(s0, 1, 4, planes, scales)
        finish(1, planes, reduce_columns(1, planes, edge_weights), s1, x1)
    planes = range(PLANES)
    stores = ((2, s1, s2, x2), (3, s2, s3, x3), (4, s3, s4, x4), (5, s4, s5, y5), (6, s5, None, y6))
    for level, source, store, out in stores:
        reduce_rows(source, level, 5, planes, None)
        finish(level, planes, reduce_columns(level, planes, weights), store, out)

    patch = jnp.zeros((PLANES, LANES), f32)
    for k in range(SIDE[5] + 3):
        line = y5[line_of(5, k), :]
        patch = patch + (pltpu.roll(line, PITCH_5 * k, 1) if k else line)
    for k in range(SIDE[6] + 3):
        patch = patch + pltpu.roll(y6[line_of(6, k), :], AT_6 + PITCH_6 * k, 1)
    lane = iota((PLANES, LANES), 1)
    start = PITCH_5 * (SIDE[5] * row - 1) + WIDE[5] * col - 1
    turned = pltpu.roll(patch, jnp.bitwise_and(start, LANES - 1), 1)
    coarse = []
    for k in range(2):
        away = lane + (LANES * k - start)
        coarse.append(jnp.where((away >= 0) & (away < AT_6), turned, 0.0))
    start = PITCH_6 * (row - 1) + WIDE[6] * col - 1
    turned = pltpu.roll(patch, jnp.bitwise_and(start - AT_6, LANES - 1), 1)
    away = lane - start
    held = (away >= 0) & (away < 4 * PITCH_6) & (lane < PITCH_6 * rows)
    coarse.append(jnp.where(held, turned, 0.0))
    for k in range(3):
        send_a[RIMS + 2 * k : RIMS + 2 * k + 2] = coarse[k].reshape(2, 8, LANES)

    levels = (None, x1, x2, x3, x4)
    for level in range(1, 5):
        count, wide = ROWS[level], WIDE[level]
        lane = iota((count, LANES), 1)
        before = jnp.zeros((count, LANES), f32)
        after = jnp.zeros((count, LANES), f32)
        for p in range(PLANES):
            plane = levels[level][plane_of(level, p), :]
            at = 3 * p if level == 1 else HALF + 3 * p
            here = (lane >= at) & (lane < at + 3)
            before = jnp.where(here, pltpu.roll(plane, at, 1) if at else plane, before)
            after = jnp.where(here, pltpu.roll(plane, (at - wide) % LANES, 1), after)
        before = jnp.where(col == 0, 0.0, before)
        after = jnp.where(col == cols - 1, 0.0, after)
        odd = jnp.bitwise_and(col, 1) == 1
        for k, strip in enumerate((jnp.where(odd, before, after), jnp.where(odd, after, before))):
            if level == 1:
                first_part[k] = strip
            else:
                other_part[k, pl.ds(STRIP_AT[level], count), :] = strip
    for k, strip in enumerate((strip_a, strip_b)):
        strip[0:5] = (first_part[k] + other_part[k, 0:40, :]).reshape(5, 8, LANES)
        strip[5] = other_part[k, 40:48, :]

    low[...] = jnp.zeros((RIMS, 8, LANES), f32)
    high[...] = jnp.zeros((RIMS, 8, LANES), f32)
    for rim, at in ((low, (0,) * 5), (high, SIDE)):
        slots = [None] * SLOTS
        for level, line, slot, lane in MOVES:
            values = levels[level][line_of(level, at[level] + line), :]
            values = pltpu.roll(values, lane, 1) if lane else values
            slots[slot] = values if slots[slot] is None else slots[slot] + values
        for k in range(SLOTS):
            rim[2 * k : 2 * k + 2] = slots[k].reshape(2, 8, LANES)
    for k in range(2):
        at = 2 * SLOTS + 3 * k
        low[at, 0:3, :] = other_part[k, 0:3, :]
        low[at + 1, 0:3, :] = other_part[k, 24:27, :]
        low[at + 1, 0:2, :] += first_part[k, 0:2, :]
        low[at + 2, 4:7, :] = other_part[k, 40:43, :]
        high[at, 0:3, :] = other_part[k, 16:19, :]
        high[at, 0:2, :] += first_part[k, 32:34, :]
        high[at + 1, 0:3, :] = other_part[k, 32:35, :]
        high[at + 2, 0:3, :] = other_part[k, 44:47, :]
    odd = jnp.bitwise_and(row, 1) == 1
    downward = jnp.where(row == 0, 0.0, low[...])
    upward = jnp.where(row == rows - 1, 0.0, high[...])
    send_a[0:RIMS] = jnp.where(odd, downward, upward)
    send_b[...] = jnp.where(odd, upward, downward)


def tables_kernel(after, inner, tile, top):
    inner[...] = expand_weights(1)
    tile[...] = expand_weights(0)
    source, target = iota((LANES, 2 * LANES), 0), iota((LANES, 2 * LANES), 1)
    along = expand_taps(lax.shift_right_logical(source, 3), lax.shift_right_logical(target, 4))
    aside = expand_taps(jnp.bitwise_and(source, 7), jnp.bitwise_and(target, 15))
    weights = (along * aside).astype(bf16)
    top[...] = jnp.concatenate([weights, weights], 0)


def fine_kernel(
    gains, images, labels, x1, x2, x3, x4, got_a, got_b, side_a, side_b, inner, tile,
    b0, b1, b2, b3, t4,
    t1, t2, t3, left, right, across, spread,
):
    row_odd = jnp.bitwise_and(lax.axis_index("ty"), 1) == 1
    col_odd = jnp.bitwise_and(lax.axis_index("tx"), 1) == 1
    left[...] = jnp.where(col_odd, side_a[0:6], side_b[0:6]).reshape(STRIP, LANES)
    right[...] = jnp.where(col_odd, side_b[0:6], side_a[0:6]).reshape(STRIP, LANES)

    totals = (None, t1, t2, t3, t4)
    parts = (None, x1, x2, x3, x4)
    for level in range(1, 5):
        count, wide, at = ROWS[level], WIDE[level], STRIP_AT[level]
        lane = iota((count, LANES), 1)
        from_left = left[at : at + count, :]
        from_right = right[at : at + count, :]
        start = 0 if level == 1 else HALF
        for p in range(PLANES):
            first = pltpu.roll(from_left, (-start - 3 * p) % LANES, 1) if start + p else from_left
            last = pltpu.roll(from_right, (wide - start - 3 * p) % LANES, 1)
            last = jnp.where((lane >= wide) & (lane < wide + 3), last, 0.0)
            place = plane_of(level, p)
            totals[level][place, :] = parts[level][place, :] + jnp.where(lane < 3, first, last)
    rims_a, rims_b = got_a[0 : 2 * SLOTS], got_b[0 : 2 * SLOTS]
    below = jnp.where(row_odd, rims_a, rims_b).reshape(SLOTS, PLANES, LANES)
    above = jnp.where(row_odd, rims_b, rims_a).reshape(SLOTS, PLANES, LANES)
    for rim, at in ((below, (0,) * 5), (above, SIDE)):
        for level, line, slot, lane in MOVES:
            values = rim[slot]
            values = pltpu.roll(values, LANES - lane, 1) if lane else values
            totals[level][line_of(level, at[level] + line), :] += values

    for level in (3, 2, 1):
        source, count, out = totals[level + 1], ROWS[level + 1], (None, b1, b2, b3)[level]
        wide = split_dot(source[0 : INNER * count, :], inner[...])
        across[:, 0:count, :] = wide.reshape(INNER, count, LANES)
        if level == 3:
            spread[:, 0 : ROWS[3], :] = jnp.zeros((INNER, ROWS[3], LANES), f32)
        expand_rows(across, spread, PAIRS[level])
        here = totals[level]
        for b in range(BANDS):
            total = jnp.zeros((ROWS[level], LANES), f32)
            for e in range(EXPOSURES):
                p = e * BANDS + b
                laplace = here[plane_of(level, p), :] - spread[p, 0 : ROWS[level], :]
                total = total + here[plane_of(level, INNER + e), :] * laplace
            out[b] = total
    across[...] = split_dot(t1[0 : INNER * ROWS[1], :], tile[...]).reshape(INNER, ROWS[1], LANES)
    expand_rows_tile(across, spread, PAIRS[0])
    for b in range(BANDS):
        total = jnp.zeros((ROWS[0], LANES), f32)
        for e in range(EXPOSURES):
            p = e * BANDS + b
            laplace = images[p] * gains[e, b] - spread[p]
            total = total + jnp.where(labels[...] == e, laplace, 0.0)
        b0[b] = total


def collapse_kernel(
    rows, cols, coarse, other, b0, b1, b2, b3, t4, inner, tile, top_weights, out,
    v5, v6, less_5, window, c4, c3, c2, c1, across, spread,
):
    row, col = lax.axis_index("ty"), lax.axis_index("tx")
    total = (coarse[...] + other[...]).reshape(3, PLANES, LANES)

    def blend(planes, less):
        total = None
        for e in range(EXPOSURES):
            part = planes[e * BANDS : (e + 1) * BANDS, :]
            if less is not None:
                part = part - less[e * BANDS : (e + 1) * BANDS, :]
            part = part * planes[INNER + e : INNER + e + 1, :]
            total = part if total is None else total + part
        return total

    v6[...] = total[2]
    v6[INNER : INNER + BANDS, :] = blend(total[2], None)
    less_5[...] = split_dot(v6[...], top_weights[...])
    for k in range(2):
        at = LANES * k
        less = less_5[:, at : at + LANES]
        v5[:, at : at + LANES] = total[k]
        v5[INNER : INNER + BANDS, at : at + LANES] = blend(total[k], less) + less[INNER : INNER + BANDS, :]

    window[...] = jnp.zeros((PLANES * 8, LANES), f32)
    lane = iota((PLANES, LANES), 1)
    first, second = v5[:, 0:LANES], v5[:, LANES : 2 * LANES]
    where = lane + (WIDE[5] * col - 1)
    valid = (where >= 0) & (where < WIDE[5] * cols) & (lane < WIDE[5] + 3)
    for k in range(SIDE[5] + 3):
        line = SIDE[5] * row - 1 + k
        start = PITCH_5 * jnp.bitwise_and(line, 7) + WIDE[5] * col - 1
        turned = pltpu.roll(jnp.where(line < 8, first, second), jnp.bitwise_and(-start, LANES - 1), 1)
        held = valid & (line >= 0) & (line < SIDE[5] * rows)
        window[line_of(5, k), :] = jnp.where(held, turned, 0.0)

    across[:, 0:8, :] = split_dot(window[...], inner[...]).reshape(PLANES, 8, LANES)
    expand_rows(across, spread, PAIRS[4])
    inside = in_slab(4, row, col, rows, cols)
    for b in range(BANDS):
        total = spread[INNER + b, 0:8, :]
        for e in range(EXPOSURES):
            p = e * BANDS + b
            laplace = t4[plane_of(4, p), :] - spread[p, 0:8, :]
            total = total + t4[plane_of(4, INNER + e), :] * laplace
        c4[b] = jnp.where(inside, total, 0.0)
    c4[BANDS] = jnp.zeros((8, LANES), f32)

    for level, source, target, band in ((3, c4, c3, b3), (2, c3, c2, b2), (1, c2, c1, b1)):
        count, depth = ROWS[level + 1], ROWS[level]
        wide = split_dot(source[...].reshape(EXPOSURES * count, LANES), inner[...])
        across[0:EXPOSURES, 0:count, :] = wide.reshape(EXPOSURES, count, LANES)
        if level == 3:
            spread[0:BANDS, 0:depth, :] = jnp.zeros((BANDS, depth, LANES), f32)
        expand_rows(across.at[0:BANDS], spread.at[0:BANDS], PAIRS[level])
        inside = in_slab(level, row, col, rows, cols)
        for b in range(BANDS):
            target[b] = jnp.where(inside, band[b] + spread[b, 0:depth, :], 0.0)
        target[BANDS] = jnp.zeros((depth, LANES), f32)
    wide = split_dot(c1[...].reshape(EXPOSURES * ROWS[1], LANES), tile[...])
    across[0:EXPOSURES] = wide.reshape(EXPOSURES, ROWS[1], LANES)
    expand_rows_tile(across.at[0:BANDS], spread.at[0:BANDS], PAIRS[0])
    out[...] = b0[...] + spread[0:BANDS]


VMEM = pl.BlockSpec(memory_space=pltpu.VMEM)
SMEM = pl.BlockSpec(memory_space=pltpu.SMEM)
HBM = pl.BlockSpec(memory_space=pltpu.HBM)
PARAMS = pltpu.CompilerParams(vmem_limit_bytes=32 * 1024 * 1024)


def floats(*shape):
    return jax.ShapeDtypeStruct(shape, f32)


def halves(*shape):
    return jax.ShapeDtypeStruct(shape, bf16)


def scratch(*shape):
    return pltpu.VMEM(shape, f32)


def swaps(size, first):
    return [(i, ((i - first) ^ 1) + first) for i in range(first, size - first)]


def around(size):
    return swaps(size, 1) + [(0, size - 1), (size - 1, 0)]


def shards(images, gains, labels):
    rows, cols = lax.axis_size("ty"), lax.axis_size("tx")
    images = images.reshape(INNER, ROWS[0], LANES)
    levels = [floats(PLANES * ROWS[level], LANES) for level in range(1, 5)]
    x1, x2, x3, x4, send_a, send_b, strip_a, strip_b = pl.pallas_call(
        lambda *refs: partial_kernel(rows, cols, *refs),
        out_shape=[
            *levels,
            floats(RIMS + COARSE, 8, LANES),
            floats(RIMS, 8, LANES),
            floats(6, 8, LANES),
            floats(6, 8, LANES),
        ],
        in_specs=[HBM] * 3,
        out_specs=[VMEM] * 8,
        scratch_shapes=[
            scratch(PLANES, 88, LANES),
            scratch(PLANES, 56, LANES),
            scratch(PLANES, 40, LANES),
            scratch(PLANES, 24, LANES),
            scratch(PLANES, 24, LANES),
            scratch(PLANES, 24, LANES),
            scratch(PLANES * 8, LANES),
            scratch(PLANES * 8, LANES),
            scratch(PLANES * ROWS[1], LANES),
            pltpu.VMEM((ROWS[0], LANES), jnp.int32),
            pltpu.SMEM((EXPOSURES, BANDS), f32),
            scratch(2, ROWS[1], LANES),
            scratch(2, STRIP, LANES),
            scratch(RIMS, 8, LANES),
            scratch(RIMS, 8, LANES),
            pltpu.SemaphoreType.DMA((INNER + 2,)),
        ],
        compiler_params=PARAMS,
        name="partial_levels",
    )(images, gains, labels)
    inner, tile, top = pl.pallas_call(
        tables_kernel,
        out_shape=[halves(2 * LANES, LANES), halves(2 * LANES, LANES), halves(2 * LANES, 2 * LANES)],
        in_specs=[VMEM],
        out_specs=[VMEM] * 3,
        compiler_params=PARAMS,
        name="expand_tables",
    )(strip_a)
    got_a = lax.ppermute(send_a, "ty", swaps(rows, 0))
    coarse = send_a[RIMS:] + got_a[RIMS:]
    got_b = lax.ppermute(jnp.concatenate([send_b, coarse], 0), "ty", around(rows))
    coarse = coarse + got_b[RIMS:]
    odd = lax.axis_index("ty") % 2 == 1
    rims_a, rims_b = got_a[2 * SLOTS : RIMS], got_b[2 * SLOTS : RIMS]
    below, above = jnp.where(odd, rims_a, rims_b), jnp.where(odd, rims_b, rims_a)
    strips = []
    for k, strip in enumerate((strip_a, strip_b)):
        low, high = below[3 * k : 3 * k + 3], above[3 * k : 3 * k + 3]
        none = jnp.zeros((1, 8, LANES), f32)
        rims = [low[0:1], none, high[0:1], low[1:2], high[1:2], low[2:3] + high[2:3]]
        strips.append(strip + jnp.concatenate(rims, 0))
    side_a = lax.ppermute(jnp.concatenate([strips[0], coarse], 0), "tx", swaps(cols, 0))
    coarse = coarse + side_a[6:]
    side_b = lax.ppermute(jnp.concatenate([strips[1], coarse], 0), "tx", around(cols))
    coarse = coarse + side_b[6:]
    other = lax.ppermute(coarse, "ty", [(i, (i + rows // 2) % rows) for i in range(rows)])
    b0, b1, b2, b3, t4 = pl.pallas_call(
        fine_kernel,
        out_shape=[floats(BANDS, ROWS[level], LANES) for level in range(4)] + [levels[3]],
        in_specs=[SMEM] + [VMEM] * 12,
        out_specs=[VMEM] * 5,
        scratch_shapes=[
            scratch(PLANES * ROWS[1], LANES),
            scratch(PLANES * ROWS[2], LANES),
            scratch(PLANES * ROWS[3], LANES),
            scratch(STRIP, LANES),
            scratch(STRIP, LANES),
            scratch(INNER, ROWS[1], LANES),
            scratch(INNER, ROWS[0], LANES),
        ],
        compiler_params=PARAMS,
        name="fine_laplacians",
    )(gains, images, labels, x1, x2, x3, x4, got_a, got_b, side_a, side_b, inner, tile)
    return pl.pallas_call(
        lambda *refs: collapse_kernel(rows, cols, *refs),
        out_shape=floats(BANDS, ROWS[0], LANES),
        in_specs=[VMEM] * 10,
        out_specs=VMEM,
        scratch_shapes=[
            scratch(PLANES, 2 * LANES),
            scratch(PLANES, LANES),
            scratch(PLANES, 2 * LANES),
            scratch(PLANES * 8, LANES),
            scratch(EXPOSURES, ROWS[4], LANES),
            scratch(EXPOSURES, ROWS[3], LANES),
            scratch(EXPOSURES, ROWS[2], LANES),
            scratch(EXPOSURES, ROWS[1], LANES),
            scratch(PLANES, ROWS[1], LANES),
            scratch(PLANES, ROWS[0], LANES),
        ],
        compiler_params=PARAMS,
        name="collapse",
    )(coarse, other, b0, b1, b2, b3, t4, inner, tile, top)


def solution(mesh):
    placed = (P(None, None, ("grp", "ty"), "tx"), P(), P(("grp", "ty"), "tx"))
    return jax.shard_map(
        shards, mesh=mesh, in_specs=placed, out_specs=P(None, ("grp", "ty"), "tx"), check_vma=False
    )
```

```python
import jax
import jax.numpy as jnp
from jax import lax
from jax.experimental import pallas as pl
from jax.experimental.pallas import tpu as pltpu
from jax.sharding import PartitionSpec as P

EXPOSURES = 4
BANDS = 3
INNER = EXPOSURES * BANDS
PLANES = INNER + EXPOSURES
LANES = 128
HALF = LANES // 2

SIDE = (64, 32, 16, 8, 4, 2, 1)
WIDE = (128, 64, 32, 16, 8, 4, 2)
ROWS = (64, 40, 24, 16, 8, 8, 8)
PAIRS = (32, 20, 12, 6, 4)
SLOTS = 3
MOVES = (
    (1, 0, 0, 0), (1, 1, 1, 0),
    (2, 0, 0, 66), (2, 1, 1, 66), (2, 2, 2, 0),
    (3, 0, 2, 35), (3, 1, 2, 54), (3, 2, 2, 73),
    (4, 0, 2, 92), (4, 1, 2, 103), (4, 2, 2, 114),
)
STRIP_AT = (0, 0, 0, 24, 40)
STRIP = 48
PITCH_5 = 8
PITCH_6 = 6
AT_6 = 40
RIMS = 2 * SLOTS + 6

f32 = jnp.float32
bf16 = jnp.bfloat16


def iota(shape, dim):
    return lax.broadcasted_iota(jnp.int32, shape, dim)


def reduce_weights(first):
    tap = iota((LANES, LANES), 0) - 2 * iota((LANES, LANES), 1) + first
    near = jnp.where((tap == 1) | (tap == 3), 0.25, 0.0)
    ends = jnp.where((tap == 0) | (tap == 4), 0.0625, 0.0)
    weights = jnp.where(tap == 2, 0.375, near + ends).astype(bf16)
    return jnp.concatenate([weights, weights], 0)


def expand_taps(source, target):
    away = 2 * source - target
    even = jnp.where(away == 0, 0.75, 0.0) + jnp.where((away == 2) | (away == -2), 0.125, 0.0)
    odd = jnp.where((away == 1) | (away == -1), 0.5, 0.0)
    return jnp.where(jnp.bitwise_and(target, 1) == 1, odd, even)


def expand_weights(first):
    shape = (LANES, LANES)
    weights = expand_taps(iota(shape, 0) - 1, iota(shape, 1) - first).astype(bf16)
    return jnp.concatenate([weights, weights], 0)


def split_dot(values, weights):
    high = values.astype(bf16)
    low = (values - high.astype(f32)).astype(bf16)
    return jnp.dot(jnp.concatenate([high, low], 1), weights, preferred_element_type=f32)


def in_slab(level, row, col, rows, cols):
    shape = (ROWS[level], LANES)
    along, across = iota(shape, 0), iota(shape, 1)
    first, last = 1 - SIDE[level] * row, 1 + SIDE[level] * (rows - row)
    left, right = 1 - WIDE[level] * col, 1 + WIDE[level] * (cols - col)
    return (along >= first) & (along < last) & (across >= left) & (across < right)


def expand_rows(source, target, count):
    before = source[:, 0:count, :]
    centre = source[:, 1 : count + 1, :]
    after = source[:, 2 : count + 2, :]
    target[:, pl.ds(0, count, stride=2), :] = (before + centre) * 0.5
    target[:, pl.ds(1, count, stride=2), :] = centre * 0.75 + (before + after) * 0.125


def expand_rows_tile(source, target, count):
    before = source[:, 0:count, :]
    centre = source[:, 1 : count + 1, :]
    after = source[:, 2 : count + 2, :]
    target[:, pl.ds(0, count, stride=2), :] = centre * 0.75 + (before + after) * 0.125
    target[:, pl.ds(1, count, stride=2), :] = (centre + after) * 0.5


def plane_of(level, p):
    return pl.ds(p * ROWS[level], ROWS[level])


def line_of(level, line):
    return pl.ds(line, PLANES, stride=ROWS[level])


def patch_places(shape, dim):
    lane = jnp.bitwise_and(iota(shape, dim), HALF - 1)
    row_5, col_5 = lax.shift_right_logical(lane, 3), jnp.bitwise_and(lane, PITCH_5 - 1)
    past = lane - AT_6
    row_6 = lax.shift_right_arithmetic(past * 43, 8)
    col_6 = past - PITCH_6 * row_6
    is_5 = (lane < AT_6) & (col_5 < WIDE[5] + 3)
    is_6 = (lane >= AT_6) & (col_6 < WIDE[6] + 3)
    return (is_5, row_5, col_5), (is_6, row_6, col_6)


def partial_kernel(
    rows, cols, images, gains, labels,
    s0, scale, x1, x2, x3, x4, send_a, send_b, strip_a, strip_b, patches,
    s1, s2, s3, s4, s5, y5, y6, across, label, gain, first_part, other_part, low, high, done,
):
    row, col = lax.axis_index("ty"), lax.axis_index("tx")
    s0[:, 0:8, :] = jnp.zeros((PLANES, 8, LANES), f32)
    s0[:, 72:88, :] = jnp.zeros((PLANES, 16, LANES), f32)
    copies = [pltpu.make_async_copy(labels, label, done.at[INNER])]
    copies.append(pltpu.make_async_copy(gains, gain, done.at[INNER + 1]))
    for p in range(INNER):
        copies.append(pltpu.make_async_copy(images.at[p], s0.at[p, pl.ds(8, 64)], done.at[p]))
    for copy in copies:
        copy.start()
    for store in (s1, s2, s3, s4, s5):
        depth = store.shape[1]
        store[:, 0:8, :] = jnp.zeros((PLANES, 8, LANES), f32)
        store[:, depth - 8 : depth, :] = jnp.zeros((PLANES, 8, LANES), f32)
    edge_weights, weights = reduce_weights(4), reduce_weights(3)

    def reduce_rows(source, level, first, planes, scales):
        count = ROWS[level]
        for p in planes:
            tap = [source[p, pl.ds(first + k, count, stride=2), :] for k in range(5)]
            total = tap[2] * 0.375 + (tap[1] + tap[3]) * 0.25 + (tap[0] + tap[4]) * 0.0625
            across[plane_of(level, p), :] = total if scales is None else total * scales[p]

    def reduce_columns(level, planes, weights):
        count, held = ROWS[level], planes[-1] + 1 - planes[0]
        inside = in_slab(level, row, col, rows, cols)
        values = across[pl.ds(planes[0] * count, held * count), :]
        result = split_dot(values, weights).reshape(held, count, LANES)
        return jnp.where(inside[None], result, 0.0)

    def finish(level, planes, result, store, out):
        count, held = ROWS[level], len(planes)
        if out is not None:
            out[pl.ds(planes[0] * count, held * count), :] = result.reshape(held * count, LANES)
        if store is not None:
            store[planes[0] : planes[0] + held, 8 : 8 + count, :] = result

    copies[0].wait()
    for e in range(EXPOSURES):
        s0[INNER + e, 8:72, :] = jnp.where(label[...] == e, 1.0, 0.0)
    planes = range(INNER, PLANES)
    reduce_rows(s0, 1, 4, planes, None)
    finish(1, planes, reduce_columns(1, planes, edge_weights), s1, x1)
    copies[1].wait()
    for p in range(INNER):
        scale[p] = jnp.full((8, LANES), gain[p // BANDS, p % BANDS], f32)
    for e in range(EXPOSURES):
        planes = range(e * BANDS, (e + 1) * BANDS)
        scales = {e * BANDS + b: gain[e, b] for b in range(BANDS)}
        for p in planes:
            copies[2 + p].wait()
        reduce_rows(s0, 1, 4, planes, scales)
        finish(1, planes, reduce_columns(1, planes, edge_weights), s1, x1)
    planes = range(PLANES)
    stores = ((2, s1, s2, x2), (3, s2, s3, x3), (4, s3, s4, x4), (5, s4, s5, y5), (6, s5, None, y6))
    for level, source, store, out in stores:
        reduce_rows(source, level, 5, planes, None)
        finish(level, planes, reduce_columns(level, planes, weights), store, out)

    patch = jnp.zeros((PLANES, LANES), f32)
    for k in range(SIDE[5] + 3):
        line = y5[line_of(5, k), :]
        patch = patch + (pltpu.roll(line, PITCH_5 * k, 1) if k else line)
    for k in range(SIDE[6] + 3):
        patch = patch + pltpu.roll(y6[line_of(6, k), :], AT_6 + PITCH_6 * k, 1)
    patch = patch[0:8, :] + pltpu.roll(patch[8:16, :], HALF, 1)
    (is_5, row_5, col_5), (is_6, row_6, col_6) = patch_places((8, LANES), 1)
    for r in range(rows):
        down = r - row
        rows_5 = is_5 & (row_5 + 2 * down >= 0) & (row_5 + 2 * down < SIDE[5] + 3)
        rows_6 = is_6 & (row_6 + down >= 0) & (row_6 + down < SIDE[6] + 3)
        for c in range(cols):
            over = c - col
            held = rows_5 & (col_5 + 4 * over >= 0) & (col_5 + 4 * over < WIDE[5] + 3)
            away = jnp.bitwise_and(-(2 * PITCH_5 * down + 4 * over), LANES - 1)
            block = jnp.where(held, pltpu.roll(patch, away, 1), 0.0)
            held = rows_6 & (col_6 + 2 * over >= 0) & (col_6 + 2 * over < WIDE[6] + 3)
            away = jnp.bitwise_and(-(PITCH_6 * down + 2 * over), LANES - 1)
            patches[r * cols + c] = jnp.where(held, pltpu.roll(patch, away, 1), block)

    levels = (None, x1, x2, x3, x4)
    for level in range(1, 5):
        count, wide = ROWS[level], WIDE[level]
        lane = iota((count, LANES), 1)
        before = jnp.zeros((count, LANES), f32)
        after = jnp.zeros((count, LANES), f32)
        for p in range(PLANES):
            plane = levels[level][plane_of(level, p), :]
            at = 3 * p if level == 1 else HALF + 3 * p
            here = (lane >= at) & (lane < at + 3)
            before = jnp.where(here, pltpu.roll(plane, at, 1) if at else plane, before)
            after = jnp.where(here, pltpu.roll(plane, (at - wide) % LANES, 1), after)
        before = jnp.where(col == 0, 0.0, before)
        after = jnp.where(col == cols - 1, 0.0, after)
        odd = jnp.bitwise_and(col, 1) == 1
        for k, strip in enumerate((jnp.where(odd, before, after), jnp.where(odd, after, before))):
            if level == 1:
                first_part[k] = strip
            else:
                other_part[k, pl.ds(STRIP_AT[level], count), :] = strip
    for k, strip in enumerate((strip_a, strip_b)):
        strip[0:5] = (first_part[k] + other_part[k, 0:40, :]).reshape(5, 8, LANES)
        strip[5] = other_part[k, 40:48, :]

    low[...] = jnp.zeros((RIMS, 8, LANES), f32)
    high[...] = jnp.zeros((RIMS, 8, LANES), f32)
    for rim, at in ((low, (0,) * 5), (high, SIDE)):
        slots = [None] * SLOTS
        for level, line, slot, lane in MOVES:
            values = levels[level][line_of(level, at[level] + line), :]
            values = pltpu.roll(values, lane, 1) if lane else values
            slots[slot] = values if slots[slot] is None else slots[slot] + values
        for k in range(SLOTS):
            rim[2 * k : 2 * k + 2] = slots[k].reshape(2, 8, LANES)
    for k in range(2):
        at = 2 * SLOTS + 3 * k
        low[at, 0:3, :] = other_part[k, 0:3, :]
        low[at + 1, 0:3, :] = other_part[k, 24:27, :]
        low[at + 1, 0:2, :] += first_part[k, 0:2, :]
        low[at + 2, 4:7, :] = other_part[k, 40:43, :]
        high[at, 0:3, :] = other_part[k, 16:19, :]
        high[at, 0:2, :] += first_part[k, 32:34, :]
        high[at + 1, 0:3, :] = other_part[k, 32:35, :]
        high[at + 2, 0:3, :] = other_part[k, 44:47, :]
    odd = jnp.bitwise_and(row, 1) == 1
    downward = jnp.where(row == 0, 0.0, low[...])
    upward = jnp.where(row == rows - 1, 0.0, high[...])
    send_a[...] = jnp.where(odd, downward, upward)
    send_b[...] = jnp.where(odd, upward, downward)


def tables_kernel(after, inner, tile, top):
    inner[...] = expand_weights(1)
    tile[...] = expand_weights(0)
    _, (is_6, row_6, col_6) = patch_places((LANES, LANES), 0)
    (is_5, row_5, col_5), _ = patch_places((LANES, LANES), 1)
    low = (iota((LANES, LANES), 0) < HALF) & (iota((LANES, LANES), 1) < HALF)
    taps = expand_taps(row_6 - 1, row_5 - 1) * expand_taps(col_6 - 1, col_5 - 1)
    weights = jnp.where(is_5 & is_6 & low, taps, 0.0).astype(bf16)
    top[...] = jnp.concatenate([weights, weights], 0)


def fine_kernel(
    s0, scale, x1, x2, x3, x4, got_a, got_b, side_a, side_b, inner, tile,
    b0, b1, b2, b3, t4,
    t1, t2, t3, left, right, across, spread,
):
    row_odd = jnp.bitwise_and(lax.axis_index("ty"), 1) == 1
    col_odd = jnp.bitwise_and(lax.axis_index("tx"), 1) == 1
    left[...] = jnp.where(col_odd, side_a[0:6], side_b[0:6]).reshape(STRIP, LANES)
    right[...] = jnp.where(col_odd, side_b[0:6], side_a[0:6]).reshape(STRIP, LANES)

    totals = (None, t1, t2, t3, t4)
    parts = (None, x1, x2, x3, x4)
    for level in range(1, 5):
        count, wide, at = ROWS[level], WIDE[level], STRIP_AT[level]
        lane = iota((count, LANES), 1)
        from_left = left[at : at + count, :]
        from_right = right[at : at + count, :]
        start = 0 if level == 1 else HALF
        for p in range(PLANES):
            first = pltpu.roll(from_left, (-start - 3 * p) % LANES, 1) if start + p else from_left
            last = pltpu.roll(from_right, (wide - start - 3 * p) % LANES, 1)
            last = jnp.where((lane >= wide) & (lane < wide + 3), last, 0.0)
            place = plane_of(level, p)
            totals[level][place, :] = parts[level][place, :] + jnp.where(lane < 3, first, last)
    rims_a, rims_b = got_a[0 : 2 * SLOTS], got_b[0 : 2 * SLOTS]
    below = jnp.where(row_odd, rims_a, rims_b).reshape(SLOTS, PLANES, LANES)
    above = jnp.where(row_odd, rims_b, rims_a).reshape(SLOTS, PLANES, LANES)
    for rim, at in ((below, (0,) * 5), (above, SIDE)):
        for level, line, slot, lane in MOVES:
            values = rim[slot]
            values = pltpu.roll(values, LANES - lane, 1) if lane else values
            totals[level][line_of(level, at[level] + line), :] += values

    for level in (3, 2, 1):
        source, count, out = totals[level + 1], ROWS[level + 1], (None, b1, b2, b3)[level]
        wide = split_dot(source[0 : INNER * count, :], inner[...])
        across[:, 0:count, :] = wide.reshape(INNER, count, LANES)
        if level == 3:
            spread[:, 0 : ROWS[3], :] = jnp.zeros((INNER, ROWS[3], LANES), f32)
        expand_rows(across, spread, PAIRS[level])
        here = totals[level]
        for b in range(BANDS):
            total = jnp.zeros((ROWS[level], LANES), f32)
            for e in range(EXPOSURES):
                p = e * BANDS + b
                laplace = here[plane_of(level, p), :] - spread[p, 0 : ROWS[level], :]
                total = total + here[plane_of(level, INNER + e), :] * laplace
            out[b] = total
    across[...] = split_dot(t1[0 : INNER * ROWS[1], :], tile[...]).reshape(INNER, ROWS[1], LANES)
    expand_rows_tile(across, spread, PAIRS[0])
    for b in range(BANDS):
        total = jnp.zeros((ROWS[0], LANES), f32)
        for e in range(EXPOSURES):
            p = e * BANDS + b
            laplace = s0[p, 8:72, :] * scale[p, 0:1, :] - spread[p]
            total = total + s0[INNER + e, 8:72, :] * laplace
        b0[b] = total


def collapse_kernel(
    rows, cols, patches, b0, b1, b2, b3, t4, inner, tile, top_weights, out,
    v5, window, c4, c3, c2, c1, across, spread,
):
    row, col = lax.axis_index("ty"), lax.axis_index("tx")
    total = patches[0]
    for k in range(1, rows * cols):
        total = total + patches[k]
    lane = iota((PLANES, LANES), 1)
    total = jnp.concatenate([total, pltpu.roll(total, HALF, 1)], 0)
    v5[...] = jnp.where(lane < HALF, total, 0.0)

    def blend(less):
        total = None
        for e in range(EXPOSURES):
            part = v5[e * BANDS : (e + 1) * BANDS, :]
            if less is not None:
                part = part - less[e * BANDS : (e + 1) * BANDS, :]
            part = part * v5[INNER + e : INNER + e + 1, :]
            total = part if total is None else total + part
        return total

    window[0:PLANES, :] = v5[...]
    window[INNER : INNER + BANDS, :] = blend(None)
    less = split_dot(window[0:PLANES, :], top_weights[...])
    (is_5, row_5, col_5), _ = patch_places((BANDS, LANES), 1)
    along, aside = row_5 + (SIDE[5] * row - 1), col_5 + (WIDE[5] * col - 1)
    held = is_5 & (along >= 0) & (along < SIDE[5] * rows) & (aside >= 0) & (aside < WIDE[5] * cols)
    v5[INNER : INNER + BANDS, :] = jnp.where(held, blend(less) + less[INNER : INNER + BANDS, :], 0.0)

    window[...] = jnp.zeros((PLANES * 8, LANES), f32)
    for k in range(SIDE[5] + 3):
        line = v5[...]
        line = pltpu.roll(line, LANES - PITCH_5 * k, 1) if k else line
        window[line_of(5, k), :] = jnp.where(lane < WIDE[5] + 3, line, 0.0)

    across[:, 0:8, :] = split_dot(window[...], inner[...]).reshape(PLANES, 8, LANES)
    expand_rows(across, spread, PAIRS[4])
    inside = in_slab(4, row, col, rows, cols)
    for b in range(BANDS):
        total = spread[INNER + b, 0:8, :]
        for e in range(EXPOSURES):
            p = e * BANDS + b
            laplace = t4[plane_of(4, p), :] - spread[p, 0:8, :]
            total = total + t4[plane_of(4, INNER + e), :] * laplace
        c4[b] = jnp.where(inside, total, 0.0)
    c4[BANDS] = jnp.zeros((8, LANES), f32)

    for level, source, target, band in ((3, c4, c3, b3), (2, c3, c2, b2), (1, c2, c1, b1)):
        count, depth = ROWS[level + 1], ROWS[level]
        wide = split_dot(source[...].reshape(EXPOSURES * count, LANES), inner[...])
        across[0:EXPOSURES, 0:count, :] = wide.reshape(EXPOSURES, count, LANES)
        if level == 3:
            spread[0:BANDS, 0:depth, :] = jnp.zeros((BANDS, depth, LANES), f32)
        expand_rows(across.at[0:BANDS], spread.at[0:BANDS], PAIRS[level])
        inside = in_slab(level, row, col, rows, cols)
        for b in range(BANDS):
            target[b] = jnp.where(inside, band[b] + spread[b, 0:depth, :], 0.0)
        target[BANDS] = jnp.zeros((depth, LANES), f32)
    wide = split_dot(c1[...].reshape(EXPOSURES * ROWS[1], LANES), tile[...])
    across[0:EXPOSURES] = wide.reshape(EXPOSURES, ROWS[1], LANES)
    expand_rows_tile(across.at[0:BANDS], spread.at[0:BANDS], PAIRS[0])
    out[...] = b0[...] + spread[0:BANDS]


VMEM = pl.BlockSpec(memory_space=pltpu.VMEM)
SMEM = pl.BlockSpec(memory_space=pltpu.SMEM)
HBM = pl.BlockSpec(memory_space=pltpu.HBM)
PARAMS = pltpu.CompilerParams(vmem_limit_bytes=32 * 1024 * 1024)


def floats(*shape):
    return jax.ShapeDtypeStruct(shape, f32)


def halves(*shape):
    return jax.ShapeDtypeStruct(shape, bf16)


def scratch(*shape):
    return pltpu.VMEM(shape, f32)


def swaps(size, first):
    return [(i, ((i - first) ^ 1) + first) for i in range(first, size - first)]


def shards(images, gains, labels):
    rows, cols = lax.axis_size("ty"), lax.axis_size("tx")
    images = images.reshape(INNER, ROWS[0], LANES)
    pinned = [pltpu.with_memory_space_constraint(x, pltpu.HBM) for x in (images, gains, labels)]
    levels = [floats(PLANES * ROWS[level], LANES) for level in range(1, 5)]
    s0, scale, x1, x2, x3, x4, send_a, send_b, strip_a, strip_b, patches = pl.pallas_call(
        lambda *refs: partial_kernel(rows, cols, *refs),
        out_shape=[
            floats(PLANES, 88, LANES),
            floats(INNER, 8, LANES),
            *levels,
            floats(RIMS, 8, LANES),
            floats(RIMS, 8, LANES),
            floats(6, 8, LANES),
            floats(6, 8, LANES),
            floats(rows * cols, 8, LANES),
        ],
        in_specs=[HBM] * 3,
        out_specs=[VMEM] * 11,
        scratch_shapes=[
            scratch(PLANES, 56, LANES),
            scratch(PLANES, 40, LANES),
            scratch(PLANES, 24, LANES),
            scratch(PLANES, 24, LANES),
            scratch(PLANES, 24, LANES),
            scratch(PLANES * 8, LANES),
            scratch(PLANES * 8, LANES),
            scratch(PLANES * ROWS[1], LANES),
            pltpu.VMEM((ROWS[0], LANES), jnp.int32),
            pltpu.SMEM((EXPOSURES, BANDS), f32),
            scratch(2, ROWS[1], LANES),
            scratch(2, STRIP, LANES),
            scratch(RIMS, 8, LANES),
            scratch(RIMS, 8, LANES),
            pltpu.SemaphoreType.DMA((INNER + 2,)),
        ],
        compiler_params=PARAMS,
        name="partial_levels",
    )(*pinned)
    got_a = lax.ppermute(send_a, "ty", swaps(rows, 0))
    got_b = lax.ppermute(send_b, "ty", swaps(rows, 1))
    inner, tile, top = pl.pallas_call(
        tables_kernel,
        out_shape=[halves(2 * LANES, LANES)] * 3,
        in_specs=[VMEM],
        out_specs=[VMEM] * 3,
        compiler_params=PARAMS,
        name="expand_tables",
    )(strip_a)
    patches = lax.all_to_all(patches, ("ty", "tx"), 0, 0, tiled=True)
    odd = lax.axis_index("ty") % 2 == 1
    rims_a, rims_b = got_a[2 * SLOTS :], got_b[2 * SLOTS :]
    below, above = jnp.where(odd, rims_a, rims_b), jnp.where(odd, rims_b, rims_a)
    strips = []
    for k, strip in enumerate((strip_a, strip_b)):
        low, high = below[3 * k : 3 * k + 3], above[3 * k : 3 * k + 3]
        none = jnp.zeros((1, 8, LANES), f32)
        rims = [low[0:1], none, high[0:1], low[1:2], high[1:2], low[2:3] + high[2:3]]
        strips.append(strip + jnp.concatenate(rims, 0))
    strips, inner, tile, top = lax.optimization_barrier((strips, inner, tile, top))
    side_a = lax.ppermute(strips[0], "tx", swaps(cols, 0))
    side_b = lax.ppermute(strips[1], "tx", swaps(cols, 1))
    b0, b1, b2, b3, t4 = pl.pallas_call(
        fine_kernel,
        out_shape=[floats(BANDS, ROWS[level], LANES) for level in range(4)] + [levels[3]],
        in_specs=[VMEM] * 12,
        out_specs=[VMEM] * 5,
        scratch_shapes=[
            scratch(PLANES * ROWS[1], LANES),
            scratch(PLANES * ROWS[2], LANES),
            scratch(PLANES * ROWS[3], LANES),
            scratch(STRIP, LANES),
            scratch(STRIP, LANES),
            scratch(INNER, ROWS[1], LANES),
            scratch(INNER, ROWS[0], LANES),
        ],
        compiler_params=PARAMS,
        name="fine_laplacians",
    )(s0, scale, x1, x2, x3, x4, got_a, got_b, side_a, side_b, inner, tile)
    return pl.pallas_call(
        lambda *refs: collapse_kernel(rows, cols, *refs),
        out_shape=floats(BANDS, ROWS[0], LANES),
        in_specs=[VMEM] * 9,
        out_specs=VMEM,
        scratch_shapes=[
            scratch(PLANES, LANES),
            scratch(PLANES * 8, LANES),
            scratch(EXPOSURES, ROWS[4], LANES),
            scratch(EXPOSURES, ROWS[3], LANES),
            scratch(EXPOSURES, ROWS[2], LANES),
            scratch(EXPOSURES, ROWS[1], LANES),
            scratch(PLANES, ROWS[1], LANES),
            scratch(PLANES, ROWS[0], LANES),
        ],
        compiler_params=PARAMS,
        name="collapse",
    )(patches, b0, b1, b2, b3, t4, inner, tile, top)


def solution(mesh):
    placed = (P(None, None, ("grp", "ty"), "tx"), P(), P(("grp", "ty"), "tx"))
    return jax.shard_map(
        shards, mesh=mesh, in_specs=placed, out_specs=P(None, ("grp", "ty"), "tx"), check_vma=False
    )
```

```python
import jax
import jax.numpy as jnp
from jax import lax
from jax.experimental import pallas as pl
from jax.experimental.pallas import tpu as pltpu
from jax.sharding import Mesh, PartitionSpec as P

EXPOSURES = 4
BANDS = 3
INNER = EXPOSURES * BANDS
PLANES = INNER + EXPOSURES
LANES = 128
HALF = LANES // 2

SIDE = (64, 32, 16, 8, 4, 2, 1)
WIDE = (128, 64, 32, 16, 8, 4, 2)
ROWS = (64, 40, 24, 16, 8, 8, 8)
PAIRS = (32, 20, 12, 6, 4)
SLOTS = 3
MOVES = (
    (1, 0, 0, 0), (1, 1, 1, 0),
    (2, 0, 0, 66), (2, 1, 1, 66), (2, 2, 2, 0),
    (3, 0, 2, 35), (3, 1, 2, 54), (3, 2, 2, 73),
    (4, 0, 2, 92), (4, 1, 2, 103), (4, 2, 2, 114),
)
STRIP_AT = (0, 0, 0, 24, 40)
STRIP = 48
PITCH_5 = 8
PITCH_6 = 6
AT_6 = 40
RIMS = 2 * SLOTS + 6
CORES = 2

f32 = jnp.float32
bf16 = jnp.bfloat16


def iota(shape, dim):
    return lax.broadcasted_iota(jnp.int32, shape, dim)


def reduce_weights(first):
    tap = iota((LANES, LANES), 0) - 2 * iota((LANES, LANES), 1) + first
    near = jnp.where((tap == 1) | (tap == 3), 0.25, 0.0)
    ends = jnp.where((tap == 0) | (tap == 4), 0.0625, 0.0)
    weights = jnp.where(tap == 2, 0.375, near + ends).astype(bf16)
    return jnp.concatenate([weights, weights], 0)


def expand_taps(source, target):
    away = 2 * source - target
    even = jnp.where(away == 0, 0.75, 0.0) + jnp.where((away == 2) | (away == -2), 0.125, 0.0)
    odd = jnp.where((away == 1) | (away == -1), 0.5, 0.0)
    return jnp.where(jnp.bitwise_and(target, 1) == 1, odd, even)


def expand_weights(first):
    shape = (LANES, LANES)
    weights = expand_taps(iota(shape, 0) - 1, iota(shape, 1) - first).astype(bf16)
    return jnp.concatenate([weights, weights], 0)


def split_dot(values, weights):
    high = values.astype(bf16)
    low = (values - high.astype(f32)).astype(bf16)
    return jnp.dot(jnp.concatenate([high, low], 1), weights, preferred_element_type=f32)


def in_slab(level, row, col, rows, cols):
    shape = (ROWS[level], LANES)
    along, across = iota(shape, 0), iota(shape, 1)
    first, last = 1 - SIDE[level] * row, 1 + SIDE[level] * (rows - row)
    left, right = 1 - WIDE[level] * col, 1 + WIDE[level] * (cols - col)
    return (along >= first) & (along < last) & (across >= left) & (across < right)


def expand_rows(source, target, count):
    before = source[:, 0:count, :]
    centre = source[:, 1 : count + 1, :]
    after = source[:, 2 : count + 2, :]
    target[:, pl.ds(0, count, stride=2), :] = (before + centre) * 0.5
    target[:, pl.ds(1, count, stride=2), :] = centre * 0.75 + (before + after) * 0.125


def expand_rows_tile(source, target, count):
    before = source[:, 0:count, :]
    centre = source[:, 1 : count + 1, :]
    after = source[:, 2 : count + 2, :]
    target[:, pl.ds(0, count, stride=2), :] = centre * 0.75 + (before + after) * 0.125
    target[:, pl.ds(1, count, stride=2), :] = (centre + after) * 0.5


def plane_of(level, p):
    return pl.ds(p * ROWS[level], ROWS[level])


def line_of(level, line):
    return pl.ds(line, PLANES, stride=ROWS[level])


def patch_places(shape, dim):
    lane = jnp.bitwise_and(iota(shape, dim), HALF - 1)
    row_5, col_5 = lax.shift_right_logical(lane, 3), jnp.bitwise_and(lane, PITCH_5 - 1)
    past = lane - AT_6
    row_6 = lax.shift_right_arithmetic(past * 43, 8)
    col_6 = past - PITCH_6 * row_6
    is_5 = (lane < AT_6) & (col_5 < WIDE[5] + 3)
    is_6 = (lane >= AT_6) & (col_6 < WIDE[6] + 3)
    return (is_5, row_5, col_5), (is_6, row_6, col_6)


def place_of(cores):
    return lax.axis_index("chip") * cores + lax.axis_index("core"), lax.axis_index("tx")


def partial_kernel(
    rows, cols, images, gains, labels,
    s0, scale, x1, x2, x3, x4, send_a, send_b, strip_a, strip_b,
    s1, s2, s3, s4, s5, y5, y6, label, gain, first_part, other_part, low, high, done,
):
    row, col = place_of(CORES)
    s0[:, 0:8, :] = jnp.zeros((PLANES, 8, LANES), f32)
    s0[:, 72:88, :] = jnp.zeros((PLANES, 16, LANES), f32)
    copies = [pltpu.make_async_copy(labels, label, done.at[INNER])]
    copies.append(pltpu.make_async_copy(gains, gain, done.at[INNER + 1]))
    for p in range(INNER):
        copies.append(pltpu.make_async_copy(images.at[p], s0.at[p, pl.ds(8, 64)], done.at[p]))
    for copy in copies:
        copy.start()
    for store in (s1, s2, s3, s4, s5):
        depth = store.shape[1]
        store[:, 0:8, :] = jnp.zeros((PLANES, 8, LANES), f32)
        store[:, depth - 8 : depth, :] = jnp.zeros((PLANES, 8, LANES), f32)
    edge_weights, weights = reduce_weights(4), reduce_weights(3)

    def reduce(source, level, first, planes, scales, weights):
        count, held, sums = ROWS[level], len(planes), []
        for p in planes:
            tap = [source[p, pl.ds(first + k, count, stride=2), :] for k in range(5)]
            total = tap[2] * 0.375 + (tap[1] + tap[3]) * 0.25 + (tap[0] + tap[4]) * 0.0625
            sums.append(total if scales is None else total * scales[p])
        result = split_dot(jnp.concatenate(sums, 0), weights).reshape(held, count, LANES)
        return jnp.where(in_slab(level, row, col, rows, cols)[None], result, 0.0)

    def finish(level, planes, result, store, out):
        count, held = ROWS[level], len(planes)
        if out is not None:
            out[pl.ds(planes[0] * count, held * count), :] = result.reshape(held * count, LANES)
        if store is not None:
            store[planes[0] : planes[0] + held, 8 : 8 + count, :] = result

    copies[0].wait()
    for e in range(EXPOSURES):
        s0[INNER + e, 8:72, :] = jnp.where(label[...] == e, 1.0, 0.0)
    planes = range(INNER, PLANES)
    finish(1, planes, reduce(s0, 1, 4, planes, None, edge_weights), s1, x1)
    copies[1].wait()
    for p in range(INNER):
        scale[p] = jnp.full((8, LANES), gain[p // BANDS, p % BANDS], f32)
    for e in range(EXPOSURES):
        planes = range(e * BANDS, (e + 1) * BANDS)
        scales = {e * BANDS + b: gain[e, b] for b in range(BANDS)}
        for p in planes:
            copies[2 + p].wait()
        finish(1, planes, reduce(s0, 1, 4, planes, scales, edge_weights), s1, x1)
    stores = ((2, s1, s2, x2), (3, s2, s3, x3), (4, s3, s4, x4), (5, s4, s5, y5), (6, s5, None, y6))
    for level, source, store, out in stores:
        held = {2: 4, 3: 8}.get(level, PLANES)
        for at in range(0, PLANES, held):
            planes = range(at, at + held)
            finish(level, planes, reduce(source, level, 5, planes, None, weights), store, out)

    patch = jnp.zeros((PLANES, LANES), f32)
    for k in range(SIDE[5] + 3):
        line = y5[line_of(5, k), :]
        patch = patch + (pltpu.roll(line, PITCH_5 * k, 1) if k else line)
    for k in range(SIDE[6] + 3):
        patch = patch + pltpu.roll(y6[line_of(6, k), :], AT_6 + PITCH_6 * k, 1)
    patch = patch[0:8, :] + pltpu.roll(patch[8:16, :], HALF, 1)
    send_a[RIMS] = patch

    levels = (None, x1, x2, x3, x4)
    odd = jnp.bitwise_and(col, 1) == 1
    for level in range(1, 5):
        count, wide = ROWS[level], WIDE[level]
        lane = iota((count, LANES), 1)
        before = jnp.zeros((count, LANES), f32)
        after = jnp.zeros((count, LANES), f32)
        for p in range(PLANES):
            plane = levels[level][plane_of(level, p), :]
            plane = pltpu.roll(plane, 3 * p, 1) if p else plane
            before = jnp.where((lane >= 3 * p) & (lane < 3 * p + 3), plane, before)
            after = jnp.where((lane >= wide + 3 * p) & (lane < wide + 3 * p + 3), plane, after)
        if level == 1:
            after = pltpu.roll(after, HALF, 1)
        else:
            before = pltpu.roll(before, HALF, 1)
            after = pltpu.roll(after, HALF - wide, 1)
        before = jnp.where(col == 0, 0.0, before)
        after = jnp.where(col == cols - 1, 0.0, after)
        for k, strip in enumerate((jnp.where(odd, before, after), jnp.where(odd, after, before))):
            if level == 1:
                first_part[k] = strip
            else:
                other_part[k, pl.ds(STRIP_AT[level], count), :] = strip
    for k, strip in enumerate((strip_a, strip_b)):
        strip[0:5] = (first_part[k] + other_part[k, 0:40, :]).reshape(5, 8, LANES)
        strip[5] = other_part[k, 40:48, :]

    low[...] = jnp.zeros((RIMS, 8, LANES), f32)
    high[...] = jnp.zeros((RIMS, 8, LANES), f32)
    for rim, at in ((low, (0,) * 5), (high, SIDE)):
        slots = [None] * SLOTS
        for level, line, slot, lane in MOVES:
            values = levels[level][line_of(level, at[level] + line), :]
            values = pltpu.roll(values, lane, 1) if lane else values
            slots[slot] = values if slots[slot] is None else slots[slot] + values
        for k in range(SLOTS):
            rim[2 * k : 2 * k + 2] = slots[k].reshape(2, 8, LANES)
    for k in range(2):
        at = 2 * SLOTS + 3 * k
        low[at, 0:3, :] = other_part[k, 0:3, :]
        low[at + 1, 0:3, :] = other_part[k, 24:27, :]
        low[at + 1, 0:2, :] += first_part[k, 0:2, :]
        low[at + 2, 4:7, :] = other_part[k, 40:43, :]
        high[at, 0:3, :] = other_part[k, 16:19, :]
        high[at, 0:2, :] += first_part[k, 32:34, :]
        high[at + 1, 0:3, :] = other_part[k, 32:35, :]
        high[at + 2, 0:3, :] = other_part[k, 44:47, :]
    odd = jnp.bitwise_and(row, 1) == 1
    downward = jnp.where(row == 0, 0.0, low[...])
    upward = jnp.where(row == rows - 1, 0.0, high[...])
    send_a[0:RIMS] = jnp.where(odd, downward, upward)
    send_b[...] = jnp.where(odd, upward, downward)


def coarse_kernel(rows, cols, own, other, patches):
    row, col = place_of(CORES)
    sources = ((own[RIMS], row), (other[RIMS], jnp.bitwise_xor(row, 1)))
    core = jnp.bitwise_and(row, 1)
    (is_5, row_5, col_5), (is_6, row_6, col_6) = patch_places((8, LANES), 1)
    for chip in range(rows // CORES):
        downs, held_5, held_6 = [], [], []
        for _, at in sources:
            down = CORES * chip + core - at
            downs.append(down)
            held_5.append(is_5 & (row_5 + 2 * down >= 0) & (row_5 + 2 * down < SIDE[5] + 3))
            held_6.append(is_6 & (row_6 + down >= 0) & (row_6 + down < SIDE[6] + 3))
        for c in range(cols):
            over = c - col
            cols_5 = (col_5 + 4 * over >= 0) & (col_5 + 4 * over < WIDE[5] + 3)
            cols_6 = (col_6 + 2 * over >= 0) & (col_6 + 2 * over < WIDE[6] + 3)
            block = jnp.zeros((8, LANES), f32)
            for (patch, _), down, rows_5, rows_6 in zip(sources, downs, held_5, held_6):
                away = jnp.bitwise_and(-(2 * PITCH_5 * down + 4 * over), LANES - 1)
                block = block + jnp.where(rows_5 & cols_5, pltpu.roll(patch, away, 1), 0.0)
                away = jnp.bitwise_and(-(PITCH_6 * down + 2 * over), LANES - 1)
                block = block + jnp.where(rows_6 & cols_6, pltpu.roll(patch, away, 1), 0.0)
            patches[chip * cols + c] = block


def tables_kernel(after, inner, tile, top):
    inner[...] = expand_weights(1)
    tile[...] = expand_weights(0)
    _, (is_6, row_6, col_6) = patch_places((LANES, LANES), 0)
    (is_5, row_5, col_5), _ = patch_places((LANES, LANES), 1)
    low = (iota((LANES, LANES), 0) < HALF) & (iota((LANES, LANES), 1) < HALF)
    taps = expand_taps(row_6 - 1, row_5 - 1) * expand_taps(col_6 - 1, col_5 - 1)
    weights = jnp.where(is_5 & is_6 & low, taps, 0.0).astype(bf16)
    top[...] = jnp.concatenate([weights, weights], 0)


def fine_kernel(
    s0, scale, x1, x2, x3, x4, got_a, got_b, side_a, side_b, inner, tile,
    b0, b1, b2, b3, t4,
    t1, t2, t3, left, right, across, spread,
):
    row_odd = lax.axis_index("core") == 1
    col_odd = jnp.bitwise_and(lax.axis_index("tx"), 1) == 1
    left[...] = jnp.where(col_odd, side_a[0:6], side_b[0:6]).reshape(STRIP, LANES)
    right[...] = jnp.where(col_odd, side_b[0:6], side_a[0:6]).reshape(STRIP, LANES)

    totals = (None, t1, t2, t3, t4)
    parts = (None, x1, x2, x3, x4)
    for level in range(1, 5):
        count, wide, at = ROWS[level], WIDE[level], STRIP_AT[level]
        lane = iota((count, LANES), 1)
        from_left = left[at : at + count, :]
        from_right = right[at : at + count, :]
        if level == 1:
            both = jnp.where(lane < HALF, from_left, pltpu.roll(from_right, HALF, 1))
            ends = jnp.bitwise_and(lane, HALF - 1) < 3
        for p in range(PLANES):
            place = plane_of(level, p)
            if level == 1:
                rim = jnp.where(ends, pltpu.roll(both, LANES - 3 * p, 1) if p else both, 0.0)
            else:
                first = pltpu.roll(from_left, HALF - 3 * p, 1)
                last = pltpu.roll(from_right, HALF + wide - 3 * p, 1)
                last = jnp.where((lane >= wide) & (lane < wide + 3), last, 0.0)
                rim = jnp.where(lane < 3, first, last)
            totals[level][place, :] = parts[level][place, :] + rim
    rims_a, rims_b = got_a[0 : 2 * SLOTS], got_b[0 : 2 * SLOTS]
    below = jnp.where(row_odd, rims_a, rims_b).reshape(SLOTS, PLANES, LANES)
    above = jnp.where(row_odd, rims_b, rims_a).reshape(SLOTS, PLANES, LANES)
    for rim, at in ((below, (0,) * 5), (above, SIDE)):
        for level, line, slot, lane in MOVES:
            values = rim[slot]
            values = pltpu.roll(values, LANES - lane, 1) if lane else values
            totals[level][line_of(level, at[level] + line), :] += values

    for level in (3, 2, 1):
        source, count, out = totals[level + 1], ROWS[level + 1], (None, b1, b2, b3)[level]
        wide = split_dot(source[0 : INNER * count, :], inner[...])
        across[:, 0:count, :] = wide.reshape(INNER, count, LANES)
        if level == 3:
            spread[:, 0 : ROWS[3], :] = jnp.zeros((INNER, ROWS[3], LANES), f32)
        expand_rows(across, spread, PAIRS[level])
        here = totals[level]
        for b in range(BANDS):
            total = jnp.zeros((ROWS[level], LANES), f32)
            for e in range(EXPOSURES):
                p = e * BANDS + b
                laplace = here[plane_of(level, p), :] - spread[p, 0 : ROWS[level], :]
                total = total + here[plane_of(level, INNER + e), :] * laplace
            out[b] = total
    across[...] = split_dot(t1[0 : INNER * ROWS[1], :], tile[...]).reshape(INNER, ROWS[1], LANES)
    expand_rows_tile(across, spread, PAIRS[0])
    for b in range(BANDS):
        total = jnp.zeros((ROWS[0], LANES), f32)
        for e in range(EXPOSURES):
            p = e * BANDS + b
            laplace = s0[p, 8:72, :] * scale[p, 0:1, :] - spread[p]
            total = total + s0[INNER + e, 8:72, :] * laplace
        b0[b] = total


def collapse_kernel(
    rows, cols, patches, b0, b1, b2, b3, t4, inner, tile, top_weights, out,
    v5, window, c4, c3, c2, c1, across, spread,
):
    row, col = place_of(CORES)
    total = patches[0]
    for k in range(1, rows // CORES * cols):
        total = total + patches[k]
    lane = iota((PLANES, LANES), 1)
    total = jnp.concatenate([total, pltpu.roll(total, HALF, 1)], 0)
    v5[...] = jnp.where(lane < HALF, total, 0.0)

    def blend(less):
        total = None
        for e in range(EXPOSURES):
            part = v5[e * BANDS : (e + 1) * BANDS, :]
            if less is not None:
                part = part - less[e * BANDS : (e + 1) * BANDS, :]
            part = part * v5[INNER + e : INNER + e + 1, :]
            total = part if total is None else total + part
        return total

    window[0:PLANES, :] = v5[...]
    window[INNER : INNER + BANDS, :] = blend(None)
    less = split_dot(window[0:PLANES, :], top_weights[...])
    (is_5, row_5, col_5), _ = patch_places((BANDS, LANES), 1)
    along, aside = row_5 + (SIDE[5] * row - 1), col_5 + (WIDE[5] * col - 1)
    held = is_5 & (along >= 0) & (along < SIDE[5] * rows) & (aside >= 0) & (aside < WIDE[5] * cols)
    v5[INNER : INNER + BANDS, :] = jnp.where(held, blend(less) + less[INNER : INNER + BANDS, :], 0.0)

    window[...] = jnp.zeros((PLANES * 8, LANES), f32)
    for k in range(SIDE[5] + 3):
        line = v5[...]
        line = pltpu.roll(line, LANES - PITCH_5 * k, 1) if k else line
        window[line_of(5, k), :] = jnp.where(lane < WIDE[5] + 3, line, 0.0)

    across[:, 0:8, :] = split_dot(window[...], inner[...]).reshape(PLANES, 8, LANES)
    expand_rows(across, spread, PAIRS[4])
    inside = in_slab(4, row, col, rows, cols)
    for b in range(BANDS):
        total = spread[INNER + b, 0:8, :]
        for e in range(EXPOSURES):
            p = e * BANDS + b
            laplace = t4[plane_of(4, p), :] - spread[p, 0:8, :]
            total = total + t4[plane_of(4, INNER + e), :] * laplace
        c4[b] = jnp.where(inside, total, 0.0)
    c4[BANDS] = jnp.zeros((8, LANES), f32)

    for level, source, target, band in ((3, c4, c3, b3), (2, c3, c2, b2), (1, c2, c1, b1)):
        count, depth = ROWS[level + 1], ROWS[level]
        wide = split_dot(source[...].reshape(EXPOSURES * count, LANES), inner[...])
        across[0:EXPOSURES, 0:count, :] = wide.reshape(EXPOSURES, count, LANES)
        if level == 3:
            spread[0:BANDS, 0:depth, :] = jnp.zeros((BANDS, depth, LANES), f32)
        expand_rows(across.at[0:BANDS], spread.at[0:BANDS], PAIRS[level])
        inside = in_slab(level, row, col, rows, cols)
        for b in range(BANDS):
            target[b] = jnp.where(inside, band[b] + spread[b, 0:depth, :], 0.0)
        target[BANDS] = jnp.zeros((depth, LANES), f32)
    wide = split_dot(c1[...].reshape(EXPOSURES * ROWS[1], LANES), tile[...])
    across[0:EXPOSURES] = wide.reshape(EXPOSURES, ROWS[1], LANES)
    expand_rows_tile(across.at[0:BANDS], spread.at[0:BANDS], PAIRS[0])
    out[...] = b0[...] + spread[0:BANDS]


VMEM = pl.BlockSpec(memory_space=pltpu.VMEM)
SMEM = pl.BlockSpec(memory_space=pltpu.SMEM)
HBM = pl.BlockSpec(memory_space=pltpu.HBM)
PARAMS = pltpu.CompilerParams(vmem_limit_bytes=32 * 1024 * 1024)


def floats(*shape):
    return jax.ShapeDtypeStruct(shape, f32)


def halves(*shape):
    return jax.ShapeDtypeStruct(shape, bf16)


def scratch(*shape):
    return pltpu.VMEM(shape, f32)


def swaps(size, first):
    return [(i, ((i - first) ^ 1) + first) for i in range(first, size - first)]


def shards(images, gains, labels):
    chips, cols = lax.axis_size("chip"), lax.axis_size("tx")
    rows = CORES * chips
    images = images.reshape(INNER, ROWS[0], LANES)
    pinned = [pltpu.with_memory_space_constraint(x, pltpu.HBM) for x in (images, gains, labels)]
    levels = [floats(PLANES * ROWS[level], LANES) for level in range(1, 5)]
    s0, scale, x1, x2, x3, x4, send_a, send_b, strip_a, strip_b = pl.pallas_call(
        lambda *refs: partial_kernel(rows, cols, *refs),
        out_shape=[
            floats(PLANES, 88, LANES),
            floats(INNER, 8, LANES),
            *levels,
            floats(RIMS + 1, 8, LANES),
            floats(RIMS, 8, LANES),
            floats(6, 8, LANES),
            floats(6, 8, LANES),
        ],
        in_specs=[HBM] * 3,
        out_specs=[VMEM] * 10,
        scratch_shapes=[
            scratch(PLANES, 56, LANES),
            scratch(PLANES, 40, LANES),
            scratch(PLANES, 24, LANES),
            scratch(PLANES, 24, LANES),
            scratch(PLANES, 24, LANES),
            scratch(PLANES * 8, LANES),
            scratch(PLANES * 8, LANES),
            pltpu.VMEM((ROWS[0], LANES), jnp.int32),
            pltpu.SMEM((EXPOSURES, BANDS), f32),
            scratch(2, ROWS[1], LANES),
            scratch(2, STRIP, LANES),
            scratch(RIMS, 8, LANES),
            scratch(RIMS, 8, LANES),
            pltpu.SemaphoreType.DMA((INNER + 2,)),
        ],
        compiler_params=PARAMS,
        name="partial_levels",
    )(*pinned)
    got_a = lax.ppermute(send_a, "core", swaps(CORES, 0))
    got_b = lax.ppermute(send_b, ("chip", "core"), swaps(rows, 1))
    inner, tile, top = pl.pallas_call(
        tables_kernel,
        out_shape=[halves(2 * LANES, LANES)] * 3,
        in_specs=[VMEM],
        out_specs=[VMEM] * 3,
        compiler_params=PARAMS,
        name="expand_tables",
    )(strip_a)
    patches = pl.pallas_call(
        lambda *refs: coarse_kernel(rows, cols, *refs),
        out_shape=floats(chips * cols, 8, LANES),
        in_specs=[VMEM] * 2,
        out_specs=VMEM,
        compiler_params=PARAMS,
        name="coarse_patches",
    )(send_a, got_a)
    odd = lax.axis_index("core") == 1
    rims_a, rims_b = got_a[2 * SLOTS : RIMS], got_b[2 * SLOTS :]
    below, above = jnp.where(odd, rims_a, rims_b), jnp.where(odd, rims_b, rims_a)
    strips = []
    for k, strip in enumerate((strip_a, strip_b)):
        low, high = below[3 * k : 3 * k + 3], above[3 * k : 3 * k + 3]
        none = jnp.zeros((1, 8, LANES), f32)
        rims = [low[0:1], none, high[0:1], low[1:2], high[1:2], low[2:3] + high[2:3]]
        strips.append(strip + jnp.concatenate(rims, 0))
    strips, inner, tile, top, _ = lax.optimization_barrier((strips, inner, tile, top, patches))
    patches = lax.all_to_all(patches, ("chip", "tx"), 0, 0, tiled=True)
    side_a = lax.ppermute(strips[0], "tx", swaps(cols, 0))
    side_b = lax.ppermute(strips[1], "tx", swaps(cols, 1))
    b0, b1, b2, b3, t4 = pl.pallas_call(
        fine_kernel,
        out_shape=[floats(BANDS, ROWS[level], LANES) for level in range(4)] + [levels[3]],
        in_specs=[VMEM] * 12,
        out_specs=[VMEM] * 5,
        scratch_shapes=[
            scratch(PLANES * ROWS[1], LANES),
            scratch(PLANES * ROWS[2], LANES),
            scratch(PLANES * ROWS[3], LANES),
            scratch(STRIP, LANES),
            scratch(STRIP, LANES),
            scratch(INNER, ROWS[1], LANES),
            scratch(INNER, ROWS[0], LANES),
        ],
        compiler_params=PARAMS,
        name="fine_laplacians",
    )(s0, scale, x1, x2, x3, x4, got_a, got_b, side_a, side_b, inner, tile)
    return pl.pallas_call(
        lambda *refs: collapse_kernel(rows, cols, *refs),
        out_shape=floats(BANDS, ROWS[0], LANES),
        in_specs=[VMEM] * 9,
        out_specs=VMEM,
        scratch_shapes=[
            scratch(PLANES, LANES),
            scratch(PLANES * 8, LANES),
            scratch(EXPOSURES, ROWS[4], LANES),
            scratch(EXPOSURES, ROWS[3], LANES),
            scratch(EXPOSURES, ROWS[2], LANES),
            scratch(EXPOSURES, ROWS[1], LANES),
            scratch(PLANES, ROWS[1], LANES),
            scratch(PLANES, ROWS[0], LANES),
        ],
        compiler_params=PARAMS,
        name="collapse",
    )(patches, b0, b1, b2, b3, t4, inner, tile, top)


def solution(mesh):
    groups, rows, cols = mesh.devices.shape
    devices = mesh.devices.reshape(groups, rows // CORES, CORES, cols)
    split = Mesh(devices, ("grp", "chip", "core", "tx"))
    down = ("grp", "chip", "core")
    return jax.shard_map(
        shards,
        mesh=split,
        in_specs=(P(None, None, down, "tx"), P(), P(down, "tx")),
        out_specs=P(None, down, "tx"),
        check_vma=False,
    )
```

```python
import jax
import jax.numpy as jnp
from jax import lax
from jax.experimental import pallas as pl
from jax.experimental.pallas import tpu as pltpu
from jax.sharding import Mesh, PartitionSpec as P

EXPOSURES = 4
BANDS = 3
INNER = EXPOSURES * BANDS
PLANES = INNER + EXPOSURES
LANES = 128
HALF = LANES // 2

SIDE = (64, 32, 16, 8, 4, 2, 1)
WIDE = (128, 64, 32, 16, 8, 4, 2)
ROWS = (64, 40, 24, 16, 8, 8, 8)
PAIRS = (32, 20, 12, 6, 4)
SLOTS = 3
MOVES = (
    (1, 0, 0, 0), (1, 1, 1, 0),
    (2, 0, 0, 66), (2, 1, 1, 66), (2, 2, 2, 0),
    (3, 0, 2, 35), (3, 1, 2, 54), (3, 2, 2, 73),
    (4, 0, 2, 92), (4, 1, 2, 103), (4, 2, 2, 114),
)
STRIP_AT = (0, 0, 0, 24, 40)
STRIP = 48
PITCH_5 = 8
PITCH_6 = 6
AT_6 = 40
RIMS = 2 * SLOTS + 6
CORES = 2
REACH_ROWS = 3
REACH_COLS = 2

f32 = jnp.float32
bf16 = jnp.bfloat16


def iota(shape, dim):
    return lax.broadcasted_iota(jnp.int32, shape, dim)


def reduce_weights(first):
    tap = iota((LANES, LANES), 0) - 2 * iota((LANES, LANES), 1) + first
    near = jnp.where((tap == 1) | (tap == 3), 0.25, 0.0)
    ends = jnp.where((tap == 0) | (tap == 4), 0.0625, 0.0)
    weights = jnp.where(tap == 2, 0.375, near + ends).astype(bf16)
    return jnp.concatenate([weights, weights], 0)


def expand_taps(source, target):
    away = 2 * source - target
    even = jnp.where(away == 0, 0.75, 0.0) + jnp.where((away == 2) | (away == -2), 0.125, 0.0)
    odd = jnp.where((away == 1) | (away == -1), 0.5, 0.0)
    return jnp.where(jnp.bitwise_and(target, 1) == 1, odd, even)


def expand_weights(first):
    shape = (LANES, LANES)
    weights = expand_taps(iota(shape, 0) - 1, iota(shape, 1) - first).astype(bf16)
    return jnp.concatenate([weights, weights], 0)


def split_dot(values, weights):
    high = values.astype(bf16)
    low = (values - high.astype(f32)).astype(bf16)
    return jnp.dot(jnp.concatenate([high, low], 1), weights, preferred_element_type=f32)


def in_slab(level, row, col, rows, cols):
    shape = (ROWS[level], LANES)
    along, across = iota(shape, 0), iota(shape, 1)
    first, last = 1 - SIDE[level] * row, 1 + SIDE[level] * (rows - row)
    left, right = 1 - WIDE[level] * col, 1 + WIDE[level] * (cols - col)
    return (along >= first) & (along < last) & (across >= left) & (across < right)


def expand_rows(source, target, count):
    before = source[:, 0:count, :]
    centre = source[:, 1 : count + 1, :]
    after = source[:, 2 : count + 2, :]
    target[:, pl.ds(0, count, stride=2), :] = (before + centre) * 0.5
    target[:, pl.ds(1, count, stride=2), :] = centre * 0.75 + (before + after) * 0.125


def expand_rows_tile(source, target, count):
    before = source[:, 0:count, :]
    centre = source[:, 1 : count + 1, :]
    after = source[:, 2 : count + 2, :]
    target[:, pl.ds(0, count, stride=2), :] = centre * 0.75 + (before + after) * 0.125
    target[:, pl.ds(1, count, stride=2), :] = (centre + after) * 0.5


def plane_of(level, p):
    return pl.ds(p * ROWS[level], ROWS[level])


def line_of(level, line):
    return pl.ds(line, PLANES, stride=ROWS[level])


def patch_places(shape, dim):
    lane = jnp.bitwise_and(iota(shape, dim), HALF - 1)
    row_5, col_5 = lax.shift_right_logical(lane, 3), jnp.bitwise_and(lane, PITCH_5 - 1)
    past = lane - AT_6
    row_6 = lax.shift_right_arithmetic(past * 43, 8)
    col_6 = past - PITCH_6 * row_6
    is_5 = (lane < AT_6) & (col_5 < WIDE[5] + 3)
    is_6 = (lane >= AT_6) & (col_6 < WIDE[6] + 3)
    return (is_5, row_5, col_5), (is_6, row_6, col_6)


def place_of(cores):
    return lax.axis_index("chip") * cores + lax.axis_index("core"), lax.axis_index("tx")


def partial_kernel(
    rows, cols, images, gains, labels,
    s0, scale, x1, x2, x3, x4, send_a, send_b, strip_a, strip_b, patch_out,
    s1, s2, s3, s4, s5, y5, y6, label, gain, first_part, other_part, low, high, done,
):
    row, col = place_of(CORES)
    copies = [
        pltpu.make_async_copy(labels, label, done.at[EXPOSURES]),
        pltpu.make_async_copy(gains, gain, done.at[EXPOSURES + 1]),
    ]
    for e in range(EXPOSURES):
        planes = pl.ds(e * BANDS, BANDS)
        copies.append(pltpu.make_async_copy(images.at[planes], s0.at[planes, pl.ds(8, 64)], done.at[e]))
    for copy in copies:
        copy.start()
    s0[:, 0:8, :] = jnp.zeros((PLANES, 8, LANES), f32)
    s0[:, 72:88, :] = jnp.zeros((PLANES, 16, LANES), f32)
    for store in (s1, s2, s3, s4, s5):
        depth = store.shape[1]
        store[:, 0:8, :] = jnp.zeros((PLANES, 8, LANES), f32)
        store[:, depth - 8 : depth, :] = jnp.zeros((PLANES, 8, LANES), f32)
    edge_weights, weights = reduce_weights(4), reduce_weights(3)

    def reduce(source, level, first, planes, scales, weights):
        count, held, sums = ROWS[level], len(planes), []
        for p in planes:
            tap = [source[p, pl.ds(first + k, count, stride=2), :] for k in range(5)]
            total = tap[2] * 0.375 + (tap[1] + tap[3]) * 0.25 + (tap[0] + tap[4]) * 0.0625
            sums.append(total if scales is None else total * scales[p])
        result = split_dot(jnp.concatenate(sums, 0), weights).reshape(held, count, LANES)
        return jnp.where(in_slab(level, row, col, rows, cols)[None], result, 0.0)

    def finish(level, planes, result, store, out):
        count, held = ROWS[level], len(planes)
        if out is not None:
            out[pl.ds(planes[0] * count, held * count), :] = result.reshape(held * count, LANES)
        if store is not None:
            store[planes[0] : planes[0] + held, 8 : 8 + count, :] = result

    copies[0].wait()
    for e in range(EXPOSURES):
        s0[INNER + e, 8:72, :] = jnp.where(label[...] == e, 1.0, 0.0)
    planes = range(INNER, PLANES)
    finish(1, planes, reduce(s0, 1, 4, planes, None, edge_weights), s1, x1)
    copies[1].wait()
    for p in range(INNER):
        scale[p] = jnp.full((8, LANES), gain[p // BANDS, p % BANDS], f32)
    for e in range(EXPOSURES):
        planes = range(e * BANDS, (e + 1) * BANDS)
        scales = {e * BANDS + b: gain[e, b] for b in range(BANDS)}
        copies[2 + e].wait()
        finish(1, planes, reduce(s0, 1, 4, planes, scales, edge_weights), s1, x1)
    stores = ((2, s1, s2, x2), (3, s2, s3, x3), (4, s3, s4, x4), (5, s4, s5, y5), (6, s5, None, y6))
    for level, source, store, out in stores:
        held = {2: 4, 3: 8}.get(level, PLANES)
        for at in range(0, PLANES, held):
            planes = range(at, at + held)
            finish(level, planes, reduce(source, level, 5, planes, None, weights), store, out)

    patch = jnp.zeros((PLANES, LANES), f32)
    for k in range(SIDE[5] + 3):
        line = y5[line_of(5, k), :]
        patch = patch + (pltpu.roll(line, PITCH_5 * k, 1) if k else line)
    for k in range(SIDE[6] + 3):
        patch = patch + pltpu.roll(y6[line_of(6, k), :], AT_6 + PITCH_6 * k, 1)
    patch = patch[0:8, :] + pltpu.roll(patch[8:16, :], HALF, 1)
    patch_out[...] = patch

    levels = (None, x1, x2, x3, x4)
    odd = jnp.bitwise_and(col, 1) == 1
    for level in range(1, 5):
        count, wide = ROWS[level], WIDE[level]
        lane = iota((count, LANES), 1)
        before = jnp.zeros((count, LANES), f32)
        after = jnp.zeros((count, LANES), f32)
        for p in range(PLANES):
            plane = levels[level][plane_of(level, p), :]
            plane = pltpu.roll(plane, 3 * p, 1) if p else plane
            before = jnp.where((lane >= 3 * p) & (lane < 3 * p + 3), plane, before)
            after = jnp.where((lane >= wide + 3 * p) & (lane < wide + 3 * p + 3), plane, after)
        if level == 1:
            after = pltpu.roll(after, HALF, 1)
        else:
            before = pltpu.roll(before, HALF, 1)
            after = pltpu.roll(after, HALF - wide, 1)
        before = jnp.where(col == 0, 0.0, before)
        after = jnp.where(col == cols - 1, 0.0, after)
        for k, strip in enumerate((jnp.where(odd, before, after), jnp.where(odd, after, before))):
            if level == 1:
                first_part[k] = strip
            else:
                other_part[k, pl.ds(STRIP_AT[level], count), :] = strip
    for k, strip in enumerate((strip_a, strip_b)):
        strip[0:5] = (first_part[k] + other_part[k, 0:40, :]).reshape(5, 8, LANES)
        strip[5] = other_part[k, 40:48, :]

    low[...] = jnp.zeros((RIMS, 8, LANES), f32)
    high[...] = jnp.zeros((RIMS, 8, LANES), f32)
    for rim, at in ((low, (0,) * 5), (high, SIDE)):
        slots = [None] * SLOTS
        for level, line, slot, lane in MOVES:
            values = levels[level][line_of(level, at[level] + line), :]
            values = pltpu.roll(values, lane, 1) if lane else values
            slots[slot] = values if slots[slot] is None else slots[slot] + values
        for k in range(SLOTS):
            rim[2 * k : 2 * k + 2] = slots[k].reshape(2, 8, LANES)
    for k in range(2):
        at = 2 * SLOTS + 3 * k
        low[at, 0:3, :] = other_part[k, 0:3, :]
        low[at + 1, 0:3, :] = other_part[k, 24:27, :]
        low[at + 1, 0:2, :] += first_part[k, 0:2, :]
        low[at + 2, 4:7, :] = other_part[k, 40:43, :]
        high[at, 0:3, :] = other_part[k, 16:19, :]
        high[at, 0:2, :] += first_part[k, 32:34, :]
        high[at + 1, 0:3, :] = other_part[k, 32:35, :]
        high[at + 2, 0:3, :] = other_part[k, 44:47, :]
    odd = jnp.bitwise_and(row, 1) == 1
    downward = jnp.where(row == 0, 0.0, low[...])
    upward = jnp.where(row == rows - 1, 0.0, high[...])
    send_a[...] = jnp.where(odd, downward, upward)
    send_b[...] = jnp.where(odd, upward, downward)


def coarse_kernel(rows, cols, patch, rims, patches, send, slots):
    row, col = place_of(CORES)
    send[...] = rims[...]
    slots[...] = jnp.zeros(slots.shape, f32)
    width = cols + 2 * REACH_COLS
    (is_5, row_5, col_5), (is_6, row_6, col_6) = patch_places((8, LANES), 1)
    values = patch[...]
    for down in range(-REACH_ROWS, REACH_ROWS + 1):
        for over in range(-REACH_COLS, REACH_COLS + 1):
            along, aside = row_6 + down, col_6 + 2 * over
            held = is_6 & (along >= 0) & (along < SIDE[6] + 3) & (aside >= 0) & (aside < WIDE[6] + 3)
            away = -(PITCH_6 * down + 2 * over) % LANES
            block = jnp.where(held, pltpu.roll(values, away, 1) if away else values, 0.0)
            if abs(down) < REACH_ROWS and abs(over) < REACH_COLS:
                along, aside = row_5 + 2 * down, col_5 + 4 * over
                held = is_5 & (along >= 0) & (along < SIDE[5] + 3) & (aside >= 0) & (aside < WIDE[5] + 3)
                away = -(2 * PITCH_5 * down + 4 * over) % LANES
                block = jnp.where(held, pltpu.roll(values, away, 1) if away else values, block)
            slots[(row + (down + REACH_ROWS)) * width + col + (over + REACH_COLS)] = block
    for r in range(rows):
        for c in range(cols):
            patches[r * cols + c] = slots[(r + REACH_ROWS) * width + c + REACH_COLS]


def tables_kernel(after, inner, tile, top):
    inner[...] = expand_weights(1)
    tile[...] = expand_weights(0)
    _, (is_6, row_6, col_6) = patch_places((LANES, LANES), 0)
    (is_5, row_5, col_5), _ = patch_places((LANES, LANES), 1)
    low = (iota((LANES, LANES), 0) < HALF) & (iota((LANES, LANES), 1) < HALF)
    taps = expand_taps(row_6 - 1, row_5 - 1) * expand_taps(col_6 - 1, col_5 - 1)
    weights = jnp.where(is_5 & is_6 & low, taps, 0.0).astype(bf16)
    top[...] = jnp.concatenate([weights, weights], 0)


def add_side(totals, parts, strip, on_left, held):
    held[...] = strip[...].reshape(STRIP, LANES)
    for level in range(1, 5):
        count, wide, at = ROWS[level], WIDE[level], STRIP_AT[level]
        lane = iota((count, LANES), 1)
        start = 0 if level == 1 else HALF
        rim = held[at : at + count, :]
        rim = jnp.where((lane >= start) & (lane < start + 3 * PLANES), rim, 0.0)
        rim = jnp.where(on_left, rim, pltpu.roll(rim, wide, 1))
        first = jnp.where(on_left, 0, wide)
        inside = (lane >= first) & (lane < first + 3)
        for p in range(PLANES):
            away = -(start + 3 * p) % LANES
            place = plane_of(level, p)
            part = jnp.where(inside, pltpu.roll(rim, away, 1) if away else rim, 0.0)
            totals[level][place, :] = parts[level][place, :] + part


def rims_kernel(x1, x2, x3, x4, got_a, got_b, side, t1, t2, t3, t4, held):
    row_odd = lax.axis_index("core") == 1
    col_odd = jnp.bitwise_and(lax.axis_index("tx"), 1) == 1
    totals = (None, t1, t2, t3, t4)
    add_side(totals, (None, x1, x2, x3, x4), side, col_odd, held)
    rims_a, rims_b = got_a[0 : 2 * SLOTS], got_b[0 : 2 * SLOTS]
    below = jnp.where(row_odd, rims_a, rims_b).reshape(SLOTS, PLANES, LANES)
    above = jnp.where(row_odd, rims_b, rims_a).reshape(SLOTS, PLANES, LANES)
    for rim, at in ((below, (0,) * 5), (above, SIDE)):
        for level, line, slot, lane in MOVES:
            values = rim[slot]
            values = pltpu.roll(values, LANES - lane, 1) if lane else values
            totals[level][line_of(level, at[level] + line), :] += values


def fine_kernel(
    s0, scale, x1, x2, x3, x4, side, inner, tile,
    b0, b1, b2, b3, t4,
    t1, t2, t3, held, across, spread,
):
    col_odd = jnp.bitwise_and(lax.axis_index("tx"), 1) == 1
    totals = (None, t1, t2, t3, t4)
    add_side(totals, (None, x1, x2, x3, x4), side, jnp.logical_not(col_odd), held)

    for level in (3, 2, 1):
        source, count, out = totals[level + 1], ROWS[level + 1], (None, b1, b2, b3)[level]
        wide = split_dot(source[0 : INNER * count, :], inner[...])
        across[:, 0:count, :] = wide.reshape(INNER, count, LANES)
        if level == 3:
            spread[:, 0 : ROWS[3], :] = jnp.zeros((INNER, ROWS[3], LANES), f32)
        expand_rows(across, spread, PAIRS[level])
        here = totals[level]
        for b in range(BANDS):
            total = jnp.zeros((ROWS[level], LANES), f32)
            for e in range(EXPOSURES):
                p = e * BANDS + b
                laplace = here[plane_of(level, p), :] - spread[p, 0 : ROWS[level], :]
                total = total + here[plane_of(level, INNER + e), :] * laplace
            out[b] = total
    across[...] = split_dot(t1[0 : INNER * ROWS[1], :], tile[...]).reshape(INNER, ROWS[1], LANES)
    expand_rows_tile(across, spread, PAIRS[0])
    for b in range(BANDS):
        total = jnp.zeros((ROWS[0], LANES), f32)
        for e in range(EXPOSURES):
            p = e * BANDS + b
            laplace = s0[p, 8:72, :] * scale[p, 0:1, :] - spread[p]
            total = total + s0[INNER + e, 8:72, :] * laplace
        b0[b] = total


def collapse_kernel(
    rows, cols, patches, b0, b1, b2, b3, t4, inner, tile, top_weights, out,
    v5, window, c4, c3, c2, c1, across, spread,
):
    row, col = place_of(CORES)
    total = patches[0]
    for k in range(1, rows * cols):
        total = total + patches[k]
    lane = iota((PLANES, LANES), 1)
    total = jnp.concatenate([total, pltpu.roll(total, HALF, 1)], 0)
    v5[...] = jnp.where(lane < HALF, total, 0.0)

    def blend(less):
        total = None
        for e in range(EXPOSURES):
            part = v5[e * BANDS : (e + 1) * BANDS, :]
            if less is not None:
                part = part - less[e * BANDS : (e + 1) * BANDS, :]
            part = part * v5[INNER + e : INNER + e + 1, :]
            total = part if total is None else total + part
        return total

    window[0:PLANES, :] = v5[...]
    window[INNER : INNER + BANDS, :] = blend(None)
    less = split_dot(window[0:PLANES, :], top_weights[...])
    (is_5, row_5, col_5), _ = patch_places((BANDS, LANES), 1)
    along, aside = row_5 + (SIDE[5] * row - 1), col_5 + (WIDE[5] * col - 1)
    held = is_5 & (along >= 0) & (along < SIDE[5] * rows) & (aside >= 0) & (aside < WIDE[5] * cols)
    v5[INNER : INNER + BANDS, :] = jnp.where(held, blend(less) + less[INNER : INNER + BANDS, :], 0.0)

    window[...] = jnp.zeros((PLANES * 8, LANES), f32)
    for k in range(SIDE[5] + 3):
        line = v5[...]
        line = pltpu.roll(line, LANES - PITCH_5 * k, 1) if k else line
        window[line_of(5, k), :] = jnp.where(lane < WIDE[5] + 3, line, 0.0)

    across[:, 0:8, :] = split_dot(window[...], inner[...]).reshape(PLANES, 8, LANES)
    expand_rows(across, spread, PAIRS[4])
    inside = in_slab(4, row, col, rows, cols)
    for b in range(BANDS):
        total = spread[INNER + b, 0:8, :]
        for e in range(EXPOSURES):
            p = e * BANDS + b
            laplace = t4[plane_of(4, p), :] - spread[p, 0:8, :]
            total = total + t4[plane_of(4, INNER + e), :] * laplace
        c4[b] = jnp.where(inside, total, 0.0)
    c4[BANDS] = jnp.zeros((8, LANES), f32)

    for level, source, target, band in ((3, c4, c3, b3), (2, c3, c2, b2), (1, c2, c1, b1)):
        count, depth = ROWS[level + 1], ROWS[level]
        wide = split_dot(source[...].reshape(EXPOSURES * count, LANES), inner[...])
        across[0:EXPOSURES, 0:count, :] = wide.reshape(EXPOSURES, count, LANES)
        if level == 3:
            spread[0:BANDS, 0:depth, :] = jnp.zeros((BANDS, depth, LANES), f32)
        expand_rows(across.at[0:BANDS], spread.at[0:BANDS], PAIRS[level])
        inside = in_slab(level, row, col, rows, cols)
        for b in range(BANDS):
            target[b] = jnp.where(inside, band[b] + spread[b, 0:depth, :], 0.0)
        target[BANDS] = jnp.zeros((depth, LANES), f32)
    wide = split_dot(c1[...].reshape(EXPOSURES * ROWS[1], LANES), tile[...])
    across[0:EXPOSURES] = wide.reshape(EXPOSURES, ROWS[1], LANES)
    expand_rows_tile(across.at[0:BANDS], spread.at[0:BANDS], PAIRS[0])
    out[...] = b0[...] + spread[0:BANDS]


VMEM = pl.BlockSpec(memory_space=pltpu.VMEM)
SMEM = pl.BlockSpec(memory_space=pltpu.SMEM)
HBM = pl.BlockSpec(memory_space=pltpu.HBM)
PARAMS = pltpu.CompilerParams(vmem_limit_bytes=32 * 1024 * 1024)


def floats(*shape):
    return jax.ShapeDtypeStruct(shape, f32)


def halves(*shape):
    return jax.ShapeDtypeStruct(shape, bf16)


def scratch(*shape):
    return pltpu.VMEM(shape, f32)


def swaps(size, first):
    return [(i, ((i - first) ^ 1) + first) for i in range(first, size - first)]


def shards(images, gains, labels):
    chips, cols = lax.axis_size("chip"), lax.axis_size("tx")
    rows = CORES * chips
    images = images.reshape(INNER, ROWS[0], LANES)
    pinned = [pltpu.with_memory_space_constraint(x, pltpu.HBM) for x in (images, gains, labels)]
    levels = [floats(PLANES * ROWS[level], LANES) for level in range(1, 5)]
    s0, scale, x1, x2, x3, x4, send_a, send_b, strip_a, strip_b, patch = pl.pallas_call(
        lambda *refs: partial_kernel(rows, cols, *refs),
        out_shape=[
            floats(PLANES, 88, LANES),
            floats(INNER, 8, LANES),
            *levels,
            floats(RIMS, 8, LANES),
            floats(RIMS, 8, LANES),
            floats(6, 8, LANES),
            floats(6, 8, LANES),
            floats(8, LANES),
        ],
        in_specs=[HBM] * 3,
        out_specs=[VMEM] * 11,
        scratch_shapes=[
            scratch(PLANES, 56, LANES),
            scratch(PLANES, 40, LANES),
            scratch(PLANES, 24, LANES),
            scratch(PLANES, 24, LANES),
            scratch(PLANES, 24, LANES),
            scratch(PLANES * 8, LANES),
            scratch(PLANES * 8, LANES),
            pltpu.VMEM((ROWS[0], LANES), jnp.int32),
            pltpu.SMEM((EXPOSURES, BANDS), f32),
            scratch(2, ROWS[1], LANES),
            scratch(2, STRIP, LANES),
            scratch(RIMS, 8, LANES),
            scratch(RIMS, 8, LANES),
            pltpu.SemaphoreType.DMA((EXPOSURES + 2,)),
        ],
        compiler_params=PARAMS,
        name="partial_levels",
    )(*pinned)
    got_b = lax.ppermute(send_b, ("chip", "core"), swaps(rows, 1))
    patches, send_a = pl.pallas_call(
        lambda *refs: coarse_kernel(rows, cols, *refs),
        out_shape=[floats(rows * cols, 8, LANES), floats(RIMS, 8, LANES)],
        in_specs=[VMEM] * 2,
        out_specs=[VMEM] * 2,
        scratch_shapes=[scratch((rows + 2 * REACH_ROWS) * (cols + 2 * REACH_COLS), 8, LANES)],
        compiler_params=PARAMS,
        name="coarse_patches",
    )(patch, send_a)
    got_a = lax.ppermute(send_a, "core", swaps(CORES, 0))
    inner, tile, top = pl.pallas_call(
        tables_kernel,
        out_shape=[halves(2 * LANES, LANES)] * 3,
        in_specs=[VMEM],
        out_specs=[VMEM] * 3,
        compiler_params=PARAMS,
        name="expand_tables",
    )(strip_a)
    odd = lax.axis_index("core") == 1
    rims_a, rims_b = got_a[2 * SLOTS :], got_b[2 * SLOTS :]
    below, above = jnp.where(odd, rims_a, rims_b), jnp.where(odd, rims_b, rims_a)
    strips = []
    for k, strip in enumerate((strip_a, strip_b)):
        low, high = below[3 * k : 3 * k + 3], above[3 * k : 3 * k + 3]
        none = jnp.zeros((1, 8, LANES), f32)
        rims = [low[0:1], none, high[0:1], low[1:2], high[1:2], low[2:3] + high[2:3]]
        strips.append(strip + jnp.concatenate(rims, 0))
    strips, inner, tile, top, _ = lax.optimization_barrier((strips, inner, tile, top, patches))
    patches = lax.all_to_all(patches, ("chip", "core", "tx"), 0, 0, tiled=True)
    side_a = lax.ppermute(strips[0], "tx", swaps(cols, 0))
    side_b = lax.ppermute(strips[1], "tx", swaps(cols, 1))
    x1, x2, x3, x4 = pl.pallas_call(
        rims_kernel,
        out_shape=levels,
        in_specs=[VMEM] * 7,
        out_specs=[VMEM] * 4,
        scratch_shapes=[scratch(STRIP, LANES)],
        compiler_params=PARAMS,
        name="add_rims",
    )(x1, x2, x3, x4, got_a, got_b, side_a)
    b0, b1, b2, b3, t4 = pl.pallas_call(
        fine_kernel,
        out_shape=[floats(BANDS, ROWS[level], LANES) for level in range(4)] + [levels[3]],
        in_specs=[VMEM] * 9,
        out_specs=[VMEM] * 5,
        scratch_shapes=[
            scratch(PLANES * ROWS[1], LANES),
            scratch(PLANES * ROWS[2], LANES),
            scratch(PLANES * ROWS[3], LANES),
            scratch(STRIP, LANES),
            scratch(INNER, ROWS[1], LANES),
            scratch(INNER, ROWS[0], LANES),
        ],
        compiler_params=PARAMS,
        name="fine_laplacians",
    )(s0, scale, x1, x2, x3, x4, side_b, inner, tile)
    return pl.pallas_call(
        lambda *refs: collapse_kernel(rows, cols, *refs),
        out_shape=floats(BANDS, ROWS[0], LANES),
        in_specs=[VMEM] * 9,
        out_specs=VMEM,
        scratch_shapes=[
            scratch(PLANES, LANES),
            scratch(PLANES * 8, LANES),
            scratch(EXPOSURES, ROWS[4], LANES),
            scratch(EXPOSURES, ROWS[3], LANES),
            scratch(EXPOSURES, ROWS[2], LANES),
            scratch(EXPOSURES, ROWS[1], LANES),
            scratch(PLANES, ROWS[1], LANES),
            scratch(PLANES, ROWS[0], LANES),
        ],
        compiler_params=PARAMS,
        name="collapse",
    )(patches, b0, b1, b2, b3, t4, inner, tile, top)


def solution(mesh):
    groups, rows, cols = mesh.devices.shape
    devices = mesh.devices.reshape(groups, rows // CORES, CORES, cols)
    split = Mesh(devices, ("grp", "chip", "core", "tx"))
    down = ("grp", "chip", "core")
    return jax.shard_map(
        shards,
        mesh=split,
        in_specs=(P(None, None, down, "tx"), P(), P(down, "tx")),
        out_specs=P(None, down, "tx"),
        check_vma=False,
    )
```

```python
import jax
import jax.numpy as jnp
from jax import lax
from jax.experimental import pallas as pl
from jax.experimental.pallas import tpu as pltpu
from jax.sharding import Mesh, PartitionSpec as P

EXPOSURES = 4
BANDS = 3
INNER = EXPOSURES * BANDS
PLANES = INNER + EXPOSURES
LANES = 128
HALF = LANES // 2

SIDE = (64, 32, 16, 8, 4, 2, 1)
WIDE = (128, 64, 32, 16, 8, 4, 2)
ROWS = (64, 40, 24, 16, 8, 8, 8)
PAIRS = (32, 20, 12, 6, 4)
SLOTS = 3
MOVES = (
    (1, 0, 0, 0), (1, 1, 1, 0),
    (2, 0, 0, 66), (2, 1, 1, 66), (2, 2, 2, 0),
    (3, 0, 2, 35), (3, 1, 2, 54), (3, 2, 2, 73),
    (4, 0, 2, 92), (4, 1, 2, 103), (4, 2, 2, 114),
)
STRIP_AT = (0, 0, 0, 24, 40)
STRIP = 48
PITCH_5 = 8
PITCH_6 = 6
AT_6 = 40
RIMS = 2 * SLOTS + 6
CORES = 2
REACH_ROWS = 3
REACH_COLS = 2

f32 = jnp.float32
bf16 = jnp.bfloat16


def iota(shape, dim):
    return lax.broadcasted_iota(jnp.int32, shape, dim)


def reduce_weights(first):
    tap = iota((LANES, LANES), 0) - 2 * iota((LANES, LANES), 1) + first
    near = jnp.where((tap == 1) | (tap == 3), 0.25, 0.0)
    ends = jnp.where((tap == 0) | (tap == 4), 0.0625, 0.0)
    weights = jnp.where(tap == 2, 0.375, near + ends).astype(bf16)
    return jnp.concatenate([weights, weights], 0)


def expand_taps(source, target):
    away = 2 * source - target
    even = jnp.where(away == 0, 0.75, 0.0) + jnp.where((away == 2) | (away == -2), 0.125, 0.0)
    odd = jnp.where((away == 1) | (away == -1), 0.5, 0.0)
    return jnp.where(jnp.bitwise_and(target, 1) == 1, odd, even)


def expand_weights(first):
    shape = (LANES, LANES)
    weights = expand_taps(iota(shape, 0) - 1, iota(shape, 1) - first).astype(bf16)
    return jnp.concatenate([weights, weights], 0)


def split_dot(values, weights):
    high = values.astype(bf16)
    low = (values - high.astype(f32)).astype(bf16)
    return jnp.dot(jnp.concatenate([high, low], 1), weights, preferred_element_type=f32)


def in_slab(level, row, col, rows, cols):
    shape = (ROWS[level], LANES)
    along, across = iota(shape, 0), iota(shape, 1)
    first, last = 1 - SIDE[level] * row, 1 + SIDE[level] * (rows - row)
    left, right = 1 - WIDE[level] * col, 1 + WIDE[level] * (cols - col)
    return (along >= first) & (along < last) & (across >= left) & (across < right)


def expand_rows(source, target, count):
    before = source[:, 0:count, :]
    centre = source[:, 1 : count + 1, :]
    after = source[:, 2 : count + 2, :]
    target[:, pl.ds(0, count, stride=2), :] = (before + centre) * 0.5
    target[:, pl.ds(1, count, stride=2), :] = centre * 0.75 + (before + after) * 0.125


def expand_rows_tile(source, target, count):
    before = source[:, 0:count, :]
    centre = source[:, 1 : count + 1, :]
    after = source[:, 2 : count + 2, :]
    target[:, pl.ds(0, count, stride=2), :] = centre * 0.75 + (before + after) * 0.125
    target[:, pl.ds(1, count, stride=2), :] = (centre + after) * 0.5


def plane_of(level, p):
    return pl.ds(p * ROWS[level], ROWS[level])


def line_of(level, line):
    return pl.ds(line, PLANES, stride=ROWS[level])


def patch_places(shape, dim):
    lane = jnp.bitwise_and(iota(shape, dim), HALF - 1)
    row_5, col_5 = lax.shift_right_logical(lane, 3), jnp.bitwise_and(lane, PITCH_5 - 1)
    past = lane - AT_6
    row_6 = lax.shift_right_arithmetic(past * 43, 8)
    col_6 = past - PITCH_6 * row_6
    is_5 = (lane < AT_6) & (col_5 < WIDE[5] + 3)
    is_6 = (lane >= AT_6) & (col_6 < WIDE[6] + 3)
    return (is_5, row_5, col_5), (is_6, row_6, col_6)


def place_of(cores):
    return lax.axis_index("chip") * cores + lax.axis_index("core"), lax.axis_index("tx")


def partial_kernel(
    rows, cols, images, gains, labels,
    s0, scale, x1, x2, x3, x4, send_a, send_b, strip_a, strip_b, patches,
    s1, s2, s3, s4, s5, y5, y6, label, gain, first_part, other_part, low, high, slots, done, sent,
):
    row, col = place_of(CORES)
    copies = [
        pltpu.make_async_copy(labels, label, done.at[EXPOSURES]),
        pltpu.make_async_copy(gains, gain, done.at[EXPOSURES + 1]),
    ]
    for e in range(EXPOSURES):
        planes = pl.ds(e * BANDS, BANDS)
        copies.append(pltpu.make_async_copy(images.at[planes], s0.at[planes, pl.ds(8, 64)], done.at[e]))
    for copy in copies:
        copy.start()
    s0[:, 0:8, :] = jnp.zeros((PLANES, 8, LANES), f32)
    s0[:, 72:88, :] = jnp.zeros((PLANES, 16, LANES), f32)
    slots[...] = jnp.zeros(slots.shape, f32)
    for store in (s1, s2, s3, s4, s5):
        depth = store.shape[1]
        store[:, 0:8, :] = jnp.zeros((PLANES, 8, LANES), f32)
        store[:, depth - 8 : depth, :] = jnp.zeros((PLANES, 8, LANES), f32)
    edge_weights, weights = reduce_weights(4), reduce_weights(3)

    def reduce(source, level, first, planes, scales, weights):
        count, held, sums = ROWS[level], len(planes), []
        for p in planes:
            tap = [source[p, pl.ds(first + k, count, stride=2), :] for k in range(5)]
            total = tap[2] * 0.375 + (tap[1] + tap[3]) * 0.25 + (tap[0] + tap[4]) * 0.0625
            sums.append(total if scales is None else total * scales[p])
        result = split_dot(jnp.concatenate(sums, 0), weights).reshape(held, count, LANES)
        return jnp.where(in_slab(level, row, col, rows, cols)[None], result, 0.0)

    def finish(level, planes, result, store, out):
        count, held = ROWS[level], len(planes)
        if out is not None:
            out[pl.ds(planes[0] * count, held * count), :] = result.reshape(held * count, LANES)
        if store is not None:
            store[planes[0] : planes[0] + held, 8 : 8 + count, :] = result

    copies[0].wait()
    for e in range(EXPOSURES):
        s0[INNER + e, 8:72, :] = jnp.where(label[...] == e, 1.0, 0.0)
    planes = range(INNER, PLANES)
    finish(1, planes, reduce(s0, 1, 4, planes, None, edge_weights), s1, x1)
    copies[1].wait()
    for p in range(INNER):
        scale[p] = jnp.full((8, LANES), gain[p // BANDS, p % BANDS], f32)
    for e in range(EXPOSURES):
        planes = range(e * BANDS, (e + 1) * BANDS)
        scales = {e * BANDS + b: gain[e, b] for b in range(BANDS)}
        copies[2 + e].wait()
        finish(1, planes, reduce(s0, 1, 4, planes, scales, edge_weights), s1, x1)
    stores = ((2, s1, s2, x2), (3, s2, s3, x3), (4, s3, s4, x4), (5, s4, s5, y5), (6, s5, None, y6))
    for level, source, store, out in stores:
        held = {2: 4, 3: 8}.get(level, PLANES)
        for at in range(0, PLANES, held):
            planes = range(at, at + held)
            finish(level, planes, reduce(source, level, 5, planes, None, weights), store, out)

    patch = jnp.zeros((PLANES, LANES), f32)
    for k in range(SIDE[5] + 3):
        line = y5[line_of(5, k), :]
        patch = patch + (pltpu.roll(line, PITCH_5 * k, 1) if k else line)
    for k in range(SIDE[6] + 3):
        patch = patch + pltpu.roll(y6[line_of(6, k), :], AT_6 + PITCH_6 * k, 1)
    patch = patch[0:8, :] + pltpu.roll(patch[8:16, :], HALF, 1)
    width = cols + 2 * REACH_COLS
    (is_5, row_5, col_5), (is_6, row_6, col_6) = patch_places((8, LANES), 1)
    for down in range(-REACH_ROWS, REACH_ROWS + 1):
        for over in range(-REACH_COLS, REACH_COLS + 1):
            along, aside = row_6 + down, col_6 + 2 * over
            held = is_6 & (along >= 0) & (along < SIDE[6] + 3) & (aside >= 0) & (aside < WIDE[6] + 3)
            away = -(PITCH_6 * down + 2 * over) % LANES
            block = jnp.where(held, pltpu.roll(patch, away, 1) if away else patch, 0.0)
            if abs(down) < REACH_ROWS and abs(over) < REACH_COLS:
                along, aside = row_5 + 2 * down, col_5 + 4 * over
                held = is_5 & (along >= 0) & (along < SIDE[5] + 3) & (aside >= 0) & (aside < WIDE[5] + 3)
                away = -(2 * PITCH_5 * down + 4 * over) % LANES
                block = jnp.where(held, pltpu.roll(patch, away, 1) if away else patch, block)
            slots[(row + (down + REACH_ROWS)) * width + col + (over + REACH_COLS)] = block
    sends = []
    for r in range(rows):
        source = slots.at[pl.ds((r + REACH_ROWS) * width + REACH_COLS, cols)]
        sends.append(pltpu.make_async_copy(source, patches.at[pl.ds(r * cols, cols)], sent.at[r]))
        sends[r].start()

    levels = (None, x1, x2, x3, x4)
    odd = jnp.bitwise_and(col, 1) == 1
    for level in range(1, 5):
        count, wide = ROWS[level], WIDE[level]
        lane = iota((count, LANES), 1)
        before = jnp.zeros((count, LANES), f32)
        after = jnp.zeros((count, LANES), f32)
        for p in range(PLANES):
            plane = levels[level][plane_of(level, p), :]
            plane = pltpu.roll(plane, 3 * p, 1) if p else plane
            before = jnp.where((lane >= 3 * p) & (lane < 3 * p + 3), plane, before)
            after = jnp.where((lane >= wide + 3 * p) & (lane < wide + 3 * p + 3), plane, after)
        if level == 1:
            after = pltpu.roll(after, HALF, 1)
        else:
            before = pltpu.roll(before, HALF, 1)
            after = pltpu.roll(after, HALF - wide, 1)
        before = jnp.where(col == 0, 0.0, before)
        after = jnp.where(col == cols - 1, 0.0, after)
        for k, strip in enumerate((jnp.where(odd, before, after), jnp.where(odd, after, before))):
            if level == 1:
                first_part[k] = strip
            else:
                other_part[k, pl.ds(STRIP_AT[level], count), :] = strip
    for k, strip in enumerate((strip_a, strip_b)):
        strip[0:5] = (first_part[k] + other_part[k, 0:40, :]).reshape(5, 8, LANES)
        strip[5] = other_part[k, 40:48, :]

    low[...] = jnp.zeros((RIMS, 8, LANES), f32)
    high[...] = jnp.zeros((RIMS, 8, LANES), f32)
    for rim, at in ((low, (0,) * 5), (high, SIDE)):
        slots = [None] * SLOTS
        for level, line, slot, lane in MOVES:
            values = levels[level][line_of(level, at[level] + line), :]
            values = pltpu.roll(values, lane, 1) if lane else values
            slots[slot] = values if slots[slot] is None else slots[slot] + values
        for k in range(SLOTS):
            rim[2 * k : 2 * k + 2] = slots[k].reshape(2, 8, LANES)
    for k in range(2):
        at = 2 * SLOTS + 3 * k
        low[at, 0:3, :] = other_part[k, 0:3, :]
        low[at + 1, 0:3, :] = other_part[k, 24:27, :]
        low[at + 1, 0:2, :] += first_part[k, 0:2, :]
        low[at + 2, 4:7, :] = other_part[k, 40:43, :]
        high[at, 0:3, :] = other_part[k, 16:19, :]
        high[at, 0:2, :] += first_part[k, 32:34, :]
        high[at + 1, 0:3, :] = other_part[k, 32:35, :]
        high[at + 2, 0:3, :] = other_part[k, 44:47, :]
    odd = jnp.bitwise_and(row, 1) == 1
    downward = jnp.where(row == 0, 0.0, low[...])
    upward = jnp.where(row == rows - 1, 0.0, high[...])
    send_a[...] = jnp.where(odd, downward, upward)
    send_b[...] = jnp.where(odd, upward, downward)
    for copy in sends:
        copy.wait()


def tables_kernel(rims, inner, tile, top, send):
    send[...] = rims[...]
    inner[...] = expand_weights(1)
    tile[...] = expand_weights(0)
    _, (is_6, row_6, col_6) = patch_places((LANES, LANES), 0)
    (is_5, row_5, col_5), _ = patch_places((LANES, LANES), 1)
    low = (iota((LANES, LANES), 0) < HALF) & (iota((LANES, LANES), 1) < HALF)
    taps = expand_taps(row_6 - 1, row_5 - 1) * expand_taps(col_6 - 1, col_5 - 1)
    weights = jnp.where(is_5 & is_6 & low, taps, 0.0).astype(bf16)
    top[...] = jnp.concatenate([weights, weights], 0)


def add_side(totals, parts, strip, on_left, held):
    held[...] = strip[...].reshape(STRIP, LANES)
    for level in range(1, 5):
        count, wide, at = ROWS[level], WIDE[level], STRIP_AT[level]
        lane = iota((count, LANES), 1)
        start = 0 if level == 1 else HALF
        rim = held[at : at + count, :]
        rim = jnp.where((lane >= start) & (lane < start + 3 * PLANES), rim, 0.0)
        rim = jnp.where(on_left, rim, pltpu.roll(rim, wide, 1))
        first = jnp.where(on_left, 0, wide)
        inside = (lane >= first) & (lane < first + 3)
        for p in range(PLANES):
            away = -(start + 3 * p) % LANES
            place = plane_of(level, p)
            part = jnp.where(inside, pltpu.roll(rim, away, 1) if away else rim, 0.0)
            totals[level][place, :] = parts[level][place, :] + part


def rims_kernel(x1, x2, x3, x4, got_a, got_b, side, t1, t2, t3, t4, held):
    row_odd = lax.axis_index("core") == 1
    col_odd = jnp.bitwise_and(lax.axis_index("tx"), 1) == 1
    totals = (None, t1, t2, t3, t4)
    add_side(totals, (None, x1, x2, x3, x4), side, col_odd, held)
    rims_a, rims_b = got_a[0 : 2 * SLOTS], got_b[0 : 2 * SLOTS]
    below = jnp.where(row_odd, rims_a, rims_b).reshape(SLOTS, PLANES, LANES)
    above = jnp.where(row_odd, rims_b, rims_a).reshape(SLOTS, PLANES, LANES)
    for rim, at in ((below, (0,) * 5), (above, SIDE)):
        for level, line, slot, lane in MOVES:
            values = rim[slot]
            values = pltpu.roll(values, LANES - lane, 1) if lane else values
            totals[level][line_of(level, at[level] + line), :] += values


def fine_kernel(
    s0, scale, x1, x2, x3, x4, side, inner, tile,
    b0, b1, b2, b3, t4,
    t1, t2, t3, held, across, spread,
):
    col_odd = jnp.bitwise_and(lax.axis_index("tx"), 1) == 1
    totals = (None, t1, t2, t3, t4)
    add_side(totals, (None, x1, x2, x3, x4), side, jnp.logical_not(col_odd), held)

    for level in (3, 2, 1):
        source, count, out = totals[level + 1], ROWS[level + 1], (None, b1, b2, b3)[level]
        wide = split_dot(source[0 : INNER * count, :], inner[...])
        across[:, 0:count, :] = wide.reshape(INNER, count, LANES)
        if level == 3:
            spread[:, 0 : ROWS[3], :] = jnp.zeros((INNER, ROWS[3], LANES), f32)
        expand_rows(across, spread, PAIRS[level])
        here = totals[level]
        for b in range(BANDS):
            total = jnp.zeros((ROWS[level], LANES), f32)
            for e in range(EXPOSURES):
                p = e * BANDS + b
                laplace = here[plane_of(level, p), :] - spread[p, 0 : ROWS[level], :]
                total = total + here[plane_of(level, INNER + e), :] * laplace
            out[b] = total
    across[...] = split_dot(t1[0 : INNER * ROWS[1], :], tile[...]).reshape(INNER, ROWS[1], LANES)
    expand_rows_tile(across, spread, PAIRS[0])
    for b in range(BANDS):
        total = jnp.zeros((ROWS[0], LANES), f32)
        for e in range(EXPOSURES):
            p = e * BANDS + b
            laplace = s0[p, 8:72, :] * scale[p, 0:1, :] - spread[p]
            total = total + s0[INNER + e, 8:72, :] * laplace
        b0[b] = total


def collapse_kernel(
    rows, cols, patches, b0, b1, b2, b3, t4, inner, tile, top_weights, out,
    v5, window, c4, c3, c2, c1, across, spread,
):
    row, col = place_of(CORES)
    total = patches[0]
    for k in range(1, rows * cols):
        total = total + patches[k]
    lane = iota((PLANES, LANES), 1)
    total = jnp.concatenate([total, pltpu.roll(total, HALF, 1)], 0)
    v5[...] = jnp.where(lane < HALF, total, 0.0)

    def blend(less):
        total = None
        for e in range(EXPOSURES):
            part = v5[e * BANDS : (e + 1) * BANDS, :]
            if less is not None:
                part = part - less[e * BANDS : (e + 1) * BANDS, :]
            part = part * v5[INNER + e : INNER + e + 1, :]
            total = part if total is None else total + part
        return total

    window[0:PLANES, :] = v5[...]
    window[INNER : INNER + BANDS, :] = blend(None)
    less = split_dot(window[0:PLANES, :], top_weights[...])
    (is_5, row_5, col_5), _ = patch_places((BANDS, LANES), 1)
    along, aside = row_5 + (SIDE[5] * row - 1), col_5 + (WIDE[5] * col - 1)
    held = is_5 & (along >= 0) & (along < SIDE[5] * rows) & (aside >= 0) & (aside < WIDE[5] * cols)
    v5[INNER : INNER + BANDS, :] = jnp.where(held, blend(less) + less[INNER : INNER + BANDS, :], 0.0)

    window[...] = jnp.zeros((PLANES * 8, LANES), f32)
    for k in range(SIDE[5] + 3):
        line = v5[...]
        line = pltpu.roll(line, LANES - PITCH_5 * k, 1) if k else line
        window[line_of(5, k), :] = jnp.where(lane < WIDE[5] + 3, line, 0.0)

    across[:, 0:8, :] = split_dot(window[...], inner[...]).reshape(PLANES, 8, LANES)
    expand_rows(across, spread, PAIRS[4])
    inside = in_slab(4, row, col, rows, cols)
    for b in range(BANDS):
        total = spread[INNER + b, 0:8, :]
        for e in range(EXPOSURES):
            p = e * BANDS + b
            laplace = t4[plane_of(4, p), :] - spread[p, 0:8, :]
            total = total + t4[plane_of(4, INNER + e), :] * laplace
        c4[b] = jnp.where(inside, total, 0.0)
    c4[BANDS] = jnp.zeros((8, LANES), f32)

    for level, source, target, band in ((3, c4, c3, b3), (2, c3, c2, b2), (1, c2, c1, b1)):
        count, depth = ROWS[level + 1], ROWS[level]
        wide = split_dot(source[...].reshape(EXPOSURES * count, LANES), inner[...])
        across[0:EXPOSURES, 0:count, :] = wide.reshape(EXPOSURES, count, LANES)
        if level == 3:
            spread[0:BANDS, 0:depth, :] = jnp.zeros((BANDS, depth, LANES), f32)
        expand_rows(across.at[0:BANDS], spread.at[0:BANDS], PAIRS[level])
        inside = in_slab(level, row, col, rows, cols)
        for b in range(BANDS):
            target[b] = jnp.where(inside, band[b] + spread[b, 0:depth, :], 0.0)
        target[BANDS] = jnp.zeros((depth, LANES), f32)
    wide = split_dot(c1[...].reshape(EXPOSURES * ROWS[1], LANES), tile[...])
    across[0:EXPOSURES] = wide.reshape(EXPOSURES, ROWS[1], LANES)
    expand_rows_tile(across.at[0:BANDS], spread.at[0:BANDS], PAIRS[0])
    out[...] = b0[...] + spread[0:BANDS]


VMEM = pl.BlockSpec(memory_space=pltpu.VMEM)
SMEM = pl.BlockSpec(memory_space=pltpu.SMEM)
HBM = pl.BlockSpec(memory_space=pltpu.HBM)
PARAMS = pltpu.CompilerParams(vmem_limit_bytes=32 * 1024 * 1024)


def floats(*shape):
    return jax.ShapeDtypeStruct(shape, f32)


def halves(*shape):
    return jax.ShapeDtypeStruct(shape, bf16)


def scratch(*shape):
    return pltpu.VMEM(shape, f32)


def swaps(size, first):
    return [(i, ((i - first) ^ 1) + first) for i in range(first, size - first)]


def shards(images, gains, labels):
    chips, cols = lax.axis_size("chip"), lax.axis_size("tx")
    rows = CORES * chips
    images = images.reshape(INNER, ROWS[0], LANES)
    pinned = [pltpu.with_memory_space_constraint(x, pltpu.HBM) for x in (images, gains, labels)]
    levels = [floats(PLANES * ROWS[level], LANES) for level in range(1, 5)]
    s0, scale, x1, x2, x3, x4, send_a, send_b, strip_a, strip_b, patches = pl.pallas_call(
        lambda *refs: partial_kernel(rows, cols, *refs),
        out_shape=[
            floats(PLANES, 88, LANES),
            floats(INNER, 8, LANES),
            *levels,
            floats(RIMS, 8, LANES),
            floats(RIMS, 8, LANES),
            floats(6, 8, LANES),
            floats(6, 8, LANES),
            floats(rows * cols, 8, LANES),
        ],
        in_specs=[HBM] * 3,
        out_specs=[VMEM] * 10 + [HBM],
        scratch_shapes=[
            scratch(PLANES, 56, LANES),
            scratch(PLANES, 40, LANES),
            scratch(PLANES, 24, LANES),
            scratch(PLANES, 24, LANES),
            scratch(PLANES, 24, LANES),
            scratch(PLANES * 8, LANES),
            scratch(PLANES * 8, LANES),
            pltpu.VMEM((ROWS[0], LANES), jnp.int32),
            pltpu.SMEM((EXPOSURES, BANDS), f32),
            scratch(2, ROWS[1], LANES),
            scratch(2, STRIP, LANES),
            scratch(RIMS, 8, LANES),
            scratch(RIMS, 8, LANES),
            scratch((rows + 2 * REACH_ROWS) * (cols + 2 * REACH_COLS), 8, LANES),
            pltpu.SemaphoreType.DMA((EXPOSURES + 2,)),
            pltpu.SemaphoreType.DMA((rows,)),
        ],
        compiler_params=PARAMS,
        name="partial_levels",
    )(*pinned)
    got_b = lax.ppermute(send_b, ("chip", "core"), swaps(rows, 1))
    inner, tile, top, send_a = pl.pallas_call(
        tables_kernel,
        out_shape=[halves(2 * LANES, LANES)] * 3 + [floats(RIMS, 8, LANES)],
        in_specs=[VMEM],
        out_specs=[VMEM] * 4,
        compiler_params=PARAMS,
        name="expand_tables",
    )(send_a)
    got_a = lax.ppermute(send_a, "core", swaps(CORES, 0))
    odd = lax.axis_index("core") == 1
    rims_a, rims_b = got_a[2 * SLOTS :], got_b[2 * SLOTS :]
    below, above = jnp.where(odd, rims_a, rims_b), jnp.where(odd, rims_b, rims_a)
    strips = []
    for k, strip in enumerate((strip_a, strip_b)):
        low, high = below[3 * k : 3 * k + 3], above[3 * k : 3 * k + 3]
        none = jnp.zeros((1, 8, LANES), f32)
        rims = [low[0:1], none, high[0:1], low[1:2], high[1:2], low[2:3] + high[2:3]]
        strips.append(strip + jnp.concatenate(rims, 0))
    patches = lax.all_to_all(patches, ("chip", "core", "tx"), 0, 0, tiled=True)
    side_a = lax.ppermute(strips[0], "tx", swaps(cols, 0))
    side_b = lax.ppermute(strips[1], "tx", swaps(cols, 1))
    x1, x2, x3, x4 = pl.pallas_call(
        rims_kernel,
        out_shape=levels,
        in_specs=[VMEM] * 7,
        out_specs=[VMEM] * 4,
        scratch_shapes=[scratch(STRIP, LANES)],
        compiler_params=PARAMS,
        name="add_rims",
    )(x1, x2, x3, x4, got_a, got_b, side_a)
    b0, b1, b2, b3, t4 = pl.pallas_call(
        fine_kernel,
        out_shape=[floats(BANDS, ROWS[level], LANES) for level in range(4)] + [levels[3]],
        in_specs=[VMEM] * 9,
        out_specs=[VMEM] * 5,
        scratch_shapes=[
            scratch(PLANES * ROWS[1], LANES),
            scratch(PLANES * ROWS[2], LANES),
            scratch(PLANES * ROWS[3], LANES),
            scratch(STRIP, LANES),
            scratch(INNER, ROWS[1], LANES),
            scratch(INNER, ROWS[0], LANES),
        ],
        compiler_params=PARAMS,
        name="fine_laplacians",
    )(s0, scale, x1, x2, x3, x4, side_b, inner, tile)
    return pl.pallas_call(
        lambda *refs: collapse_kernel(rows, cols, *refs),
        out_shape=floats(BANDS, ROWS[0], LANES),
        in_specs=[VMEM] * 9,
        out_specs=VMEM,
        scratch_shapes=[
            scratch(PLANES, LANES),
            scratch(PLANES * 8, LANES),
            scratch(EXPOSURES, ROWS[4], LANES),
            scratch(EXPOSURES, ROWS[3], LANES),
            scratch(EXPOSURES, ROWS[2], LANES),
            scratch(EXPOSURES, ROWS[1], LANES),
            scratch(PLANES, ROWS[1], LANES),
            scratch(PLANES, ROWS[0], LANES),
        ],
        compiler_params=PARAMS,
        name="collapse",
    )(patches, b0, b1, b2, b3, t4, inner, tile, top)


def solution(mesh):
    groups, rows, cols = mesh.devices.shape
    devices = mesh.devices.reshape(groups, rows // CORES, CORES, cols)
    split = Mesh(devices, ("grp", "chip", "core", "tx"))
    down = ("grp", "chip", "core")
    return jax.shard_map(
        shards,
        mesh=split,
        in_specs=(P(None, None, down, "tx"), P(), P(down, "tx")),
        out_specs=P(None, down, "tx"),
        check_vma=False,
    )
```

```python
import jax
import jax.numpy as jnp
from jax import lax
from jax.experimental import pallas as pl
from jax.experimental.pallas import tpu as pltpu
from jax.sharding import Mesh, PartitionSpec as P

EXPOSURES = 4
BANDS = 3
INNER = EXPOSURES * BANDS
PLANES = INNER + EXPOSURES
LANES = 128
HALF = LANES // 2

SIDE = (64, 32, 16, 8, 4, 2, 1)
WIDE = (128, 64, 32, 16, 8, 4, 2)
ROWS = (64, 40, 24, 16, 8, 8, 8)
PAIRS = (32, 20, 12, 6, 4)
SLOTS = 3
MOVES = (
    (1, 0, 0, 0), (1, 1, 1, 0),
    (2, 0, 0, 66), (2, 1, 1, 66), (2, 2, 2, 0),
    (3, 0, 2, 35), (3, 1, 2, 54), (3, 2, 2, 73),
    (4, 0, 2, 92), (4, 1, 2, 103), (4, 2, 2, 114),
)
STRIP_AT = (0, 0, 0, 24, 40)
STRIP = 48
PITCH_5 = 8
PITCH_6 = 6
AT_6 = 40
RIMS = 2 * SLOTS + 6
CORES = 2
REACH_ROWS = 3
REACH_COLS = 2

f32 = jnp.float32
bf16 = jnp.bfloat16


def iota(shape, dim):
    return lax.broadcasted_iota(jnp.int32, shape, dim)


def reduce_weights(first):
    tap = iota((LANES, LANES), 0) - 2 * iota((LANES, LANES), 1) + first
    near = jnp.where((tap == 1) | (tap == 3), 0.25, 0.0)
    ends = jnp.where((tap == 0) | (tap == 4), 0.0625, 0.0)
    weights = jnp.where(tap == 2, 0.375, near + ends).astype(bf16)
    return jnp.concatenate([weights, weights], 0)


def expand_taps(source, target):
    away = 2 * source - target
    even = jnp.where(away == 0, 0.75, 0.0) + jnp.where((away == 2) | (away == -2), 0.125, 0.0)
    odd = jnp.where((away == 1) | (away == -1), 0.5, 0.0)
    return jnp.where(jnp.bitwise_and(target, 1) == 1, odd, even)


def expand_weights(first):
    shape = (LANES, LANES)
    weights = expand_taps(iota(shape, 0) - 1, iota(shape, 1) - first).astype(bf16)
    return jnp.concatenate([weights, weights], 0)


def split_dot(values, weights):
    high = values.astype(bf16)
    low = (values - high.astype(f32)).astype(bf16)
    return jnp.dot(jnp.concatenate([high, low], 1), weights, preferred_element_type=f32)


def split_dot_2(values, weights):
    high = values.astype(bf16)
    low = (values - high.astype(f32)).astype(bf16)
    return jnp.dot(jnp.concatenate([high, low, high], 1), weights, preferred_element_type=f32)


def in_slab(level, row, col, rows, cols):
    shape = (ROWS[level], LANES)
    along, across = iota(shape, 0), iota(shape, 1)
    first, last = 1 - SIDE[level] * row, 1 + SIDE[level] * (rows - row)
    left, right = 1 - WIDE[level] * col, 1 + WIDE[level] * (cols - col)
    return (along >= first) & (along < last) & (across >= left) & (across < right)


def expand_rows(source, target, count):
    before = source[:, 0:count, :]
    centre = source[:, 1 : count + 1, :]
    after = source[:, 2 : count + 2, :]
    target[:, pl.ds(0, count, stride=2), :] = (before + centre) * 0.5
    target[:, pl.ds(1, count, stride=2), :] = centre * 0.75 + (before + after) * 0.125


def expand_rows_tile(source, target, count):
    before = source[:, 0:count, :]
    centre = source[:, 1 : count + 1, :]
    after = source[:, 2 : count + 2, :]
    target[:, pl.ds(0, count, stride=2), :] = centre * 0.75 + (before + after) * 0.125
    target[:, pl.ds(1, count, stride=2), :] = (centre + after) * 0.5


def plane_of(level, p):
    return pl.ds(p * ROWS[level], ROWS[level])


def line_of(level, line):
    return pl.ds(line, PLANES, stride=ROWS[level])


def patch_places(shape, dim):
    lane = jnp.bitwise_and(iota(shape, dim), HALF - 1)
    row_5, col_5 = lax.shift_right_logical(lane, 3), jnp.bitwise_and(lane, PITCH_5 - 1)
    past = lane - AT_6
    row_6 = lax.shift_right_arithmetic(past * 43, 8)
    col_6 = past - PITCH_6 * row_6
    is_5 = (lane < AT_6) & (col_5 < WIDE[5] + 3)
    is_6 = (lane >= AT_6) & (col_6 < WIDE[6] + 3)
    return (is_5, row_5, col_5), (is_6, row_6, col_6)


def place_of(cores):
    return lax.axis_index("chip") * cores + lax.axis_index("core"), lax.axis_index("tx")


def partial_kernel(
    rows, cols, images, gains, labels,
    s0, scale, x1, x2, x3, x4, send_a, send_b, strip_a, strip_b, patches,
    s1, s2, s3, s4, s5, y5, y6, label, gain, first_part, other_part, low, high, slots, done, sent,
):
    row, col = place_of(CORES)
    copies = [
        pltpu.make_async_copy(labels, label, done.at[EXPOSURES]),
        pltpu.make_async_copy(gains, gain, done.at[EXPOSURES + 1]),
    ]
    for e in range(EXPOSURES):
        planes = pl.ds(e * BANDS, BANDS)
        copies.append(pltpu.make_async_copy(images.at[planes], s0.at[planes, pl.ds(8, 64)], done.at[e]))
    for copy in copies:
        copy.start()
    s0[:, 0:8, :] = jnp.zeros((PLANES, 8, LANES), f32)
    s0[:, 72:88, :] = jnp.zeros((PLANES, 16, LANES), f32)
    slots[...] = jnp.zeros(slots.shape, f32)
    for store in (s1, s2, s3, s4, s5):
        depth = store.shape[1]
        store[:, 0:8, :] = jnp.zeros((PLANES, 8, LANES), f32)
        store[:, depth - 8 : depth, :] = jnp.zeros((PLANES, 8, LANES), f32)
    edge_weights, weights = reduce_weights(4), reduce_weights(3)

    def reduce(source, level, first, planes, scales, weights):
        count, held, sums = ROWS[level], len(planes), []
        for p in planes:
            tap = [source[p, pl.ds(first + k, count, stride=2), :] for k in range(5)]
            total = tap[2] * 0.375 + (tap[1] + tap[3]) * 0.25 + (tap[0] + tap[4]) * 0.0625
            sums.append(total if scales is None else total * scales[p])
        result = split_dot(jnp.concatenate(sums, 0), weights).reshape(held, count, LANES)
        return jnp.where(in_slab(level, row, col, rows, cols)[None], result, 0.0)

    def finish(level, planes, result, store, out):
        count, held = ROWS[level], len(planes)
        if out is not None:
            out[pl.ds(planes[0] * count, held * count), :] = result.reshape(held * count, LANES)
        if store is not None:
            store[planes[0] : planes[0] + held, 8 : 8 + count, :] = result

    copies[0].wait()
    for e in range(EXPOSURES):
        s0[INNER + e, 8:72, :] = jnp.where(label[...] == e, 1.0, 0.0)
    planes = range(INNER, PLANES)
    finish(1, planes, reduce(s0, 1, 4, planes, None, edge_weights), s1, x1)
    copies[1].wait()
    for p in range(INNER):
        scale[p] = jnp.full((8, LANES), gain[p // BANDS, p % BANDS], f32)
    for e in range(EXPOSURES):
        planes = range(e * BANDS, (e + 1) * BANDS)
        scales = {e * BANDS + b: gain[e, b] for b in range(BANDS)}
        copies[2 + e].wait()
        finish(1, planes, reduce(s0, 1, 4, planes, scales, edge_weights), s1, x1)
    stores = ((2, s1, s2, x2), (3, s2, s3, x3), (4, s3, s4, x4), (5, s4, s5, y5), (6, s5, None, y6))
    for level, source, store, out in stores:
        held = {2: 4, 3: 8}.get(level, PLANES)
        for at in range(0, PLANES, held):
            planes = range(at, at + held)
            finish(level, planes, reduce(source, level, 5, planes, None, weights), store, out)

    patch = jnp.zeros((PLANES, LANES), f32)
    for k in range(SIDE[5] + 3):
        line = y5[line_of(5, k), :]
        patch = patch + (pltpu.roll(line, PITCH_5 * k, 1) if k else line)
    for k in range(SIDE[6] + 3):
        patch = patch + pltpu.roll(y6[line_of(6, k), :], AT_6 + PITCH_6 * k, 1)
    patch = patch[0:8, :] + pltpu.roll(patch[8:16, :], HALF, 1)
    width = cols + 2 * REACH_COLS
    (is_5, row_5, col_5), (is_6, row_6, col_6) = patch_places((8, LANES), 1)
    for down in range(-REACH_ROWS, REACH_ROWS + 1):
        for over in range(-REACH_COLS, REACH_COLS + 1):
            along, aside = row_6 + down, col_6 + 2 * over
            held = is_6 & (along >= 0) & (along < SIDE[6] + 3) & (aside >= 0) & (aside < WIDE[6] + 3)
            away = -(PITCH_6 * down + 2 * over) % LANES
            block = jnp.where(held, pltpu.roll(patch, away, 1) if away else patch, 0.0)
            if abs(down) < REACH_ROWS and abs(over) < REACH_COLS:
                along, aside = row_5 + 2 * down, col_5 + 4 * over
                held = is_5 & (along >= 0) & (along < SIDE[5] + 3) & (aside >= 0) & (aside < WIDE[5] + 3)
                away = -(2 * PITCH_5 * down + 4 * over) % LANES
                block = jnp.where(held, pltpu.roll(patch, away, 1) if away else patch, block)
            slots[(row + (down + REACH_ROWS)) * width + col + (over + REACH_COLS)] = block
    sends = []
    for r in range(rows):
        source = slots.at[pl.ds((r + REACH_ROWS) * width + REACH_COLS, cols)]
        sends.append(pltpu.make_async_copy(source, patches.at[pl.ds(r * cols, cols)], sent.at[r]))
        sends[r].start()

    levels = (None, x1, x2, x3, x4)
    odd = jnp.bitwise_and(col, 1) == 1
    for level in range(1, 5):
        count, wide = ROWS[level], WIDE[level]
        lane = iota((count, LANES), 1)
        before = jnp.zeros((count, LANES), f32)
        after = jnp.zeros((count, LANES), f32)
        for p in range(PLANES):
            plane = levels[level][plane_of(level, p), :]
            plane = pltpu.roll(plane, 3 * p, 1) if p else plane
            before = jnp.where((lane >= 3 * p) & (lane < 3 * p + 3), plane, before)
            after = jnp.where((lane >= wide + 3 * p) & (lane < wide + 3 * p + 3), plane, after)
        if level == 1:
            after = pltpu.roll(after, HALF, 1)
        else:
            before = pltpu.roll(before, HALF, 1)
            after = pltpu.roll(after, HALF - wide, 1)
        before = jnp.where(col == 0, 0.0, before)
        after = jnp.where(col == cols - 1, 0.0, after)
        for k, strip in enumerate((jnp.where(odd, before, after), jnp.where(odd, after, before))):
            if level == 1:
                first_part[k] = strip
            else:
                other_part[k, pl.ds(STRIP_AT[level], count), :] = strip
    for k, strip in enumerate((strip_a, strip_b)):
        strip[0:5] = (first_part[k] + other_part[k, 0:40, :]).reshape(5, 8, LANES)
        strip[5] = other_part[k, 40:48, :]

    low[...] = jnp.zeros((RIMS, 8, LANES), f32)
    high[...] = jnp.zeros((RIMS, 8, LANES), f32)
    for rim, at in ((low, (0,) * 5), (high, SIDE)):
        slots = [None] * SLOTS
        for level, line, slot, lane in MOVES:
            values = levels[level][line_of(level, at[level] + line), :]
            values = pltpu.roll(values, lane, 1) if lane else values
            slots[slot] = values if slots[slot] is None else slots[slot] + values
        for k in range(SLOTS):
            rim[2 * k : 2 * k + 2] = slots[k].reshape(2, 8, LANES)
    for k in range(2):
        at = 2 * SLOTS + 3 * k
        low[at, 0:3, :] = other_part[k, 0:3, :]
        low[at + 1, 0:3, :] = other_part[k, 24:27, :]
        low[at + 1, 0:2, :] += first_part[k, 0:2, :]
        low[at + 2, 4:7, :] = other_part[k, 40:43, :]
        high[at, 0:3, :] = other_part[k, 16:19, :]
        high[at, 0:2, :] += first_part[k, 32:34, :]
        high[at + 1, 0:3, :] = other_part[k, 32:35, :]
        high[at + 2, 0:3, :] = other_part[k, 44:47, :]
    odd = jnp.bitwise_and(row, 1) == 1
    downward = jnp.where(row == 0, 0.0, low[...])
    upward = jnp.where(row == rows - 1, 0.0, high[...])
    send_a[...] = jnp.where(odd, downward, upward)
    send_b[...] = jnp.where(odd, upward, downward)
    for copy in sends:
        copy.wait()


def tables_kernel(rims, inner, tile, top, send):
    send[...] = rims[...]
    inner[...] = expand_weights(1)
    tile[...] = expand_weights(0)
    _, (is_6, row_6, col_6) = patch_places((LANES, LANES), 0)
    (is_5, row_5, col_5), _ = patch_places((LANES, LANES), 1)
    low = (iota((LANES, LANES), 0) < HALF) & (iota((LANES, LANES), 1) < HALF)
    taps = expand_taps(row_6 - 1, row_5 - 1) * expand_taps(col_6 - 1, col_5 - 1)
    weights = jnp.where(is_5 & is_6 & low, taps, 0.0).astype(bf16)
    top[...] = jnp.concatenate([weights, weights], 0)


def add_side(totals, parts, strip, on_left, held):
    held[...] = strip[...].reshape(STRIP, LANES)
    for level in range(1, 5):
        count, wide, at = ROWS[level], WIDE[level], STRIP_AT[level]
        lane = iota((count, LANES), 1)
        start = 0 if level == 1 else HALF
        rim = held[at : at + count, :]
        rim = jnp.where((lane >= start) & (lane < start + 3 * PLANES), rim, 0.0)
        rim = jnp.where(on_left, rim, pltpu.roll(rim, wide, 1))
        first = jnp.where(on_left, 0, wide)
        inside = (lane >= first) & (lane < first + 3)
        for p in range(PLANES):
            away = -(start + 3 * p) % LANES
            place = plane_of(level, p)
            part = jnp.where(inside, pltpu.roll(rim, away, 1) if away else rim, 0.0)
            totals[level][place, :] = parts[level][place, :] + part


def rims_kernel(
    cols, x1, x2, x3, x4, got_a, got_b, side, inner, tile, s0, scale,
    t1, t2, t3, t4, wide_2, wide_3, wide_4, chosen, held,
):
    col = lax.axis_index("tx")
    step = inner[0:LANES, :].astype(f32)

    def masked(level):
        across = iota((LANES, LANES), 1)
        first, last = 1 - WIDE[level] * col, 1 + WIDE[level] * (cols - col)
        return jnp.where((across >= first) & (across < last), step, 0.0).astype(bf16)

    def halved(weights):
        high = weights.astype(bf16)
        return high, (weights - high.astype(f32)).astype(bf16)

    weights = jnp.dot(masked(1), tile[0:LANES, :], preferred_element_type=f32).astype(bf16)
    wide_2[...] = jnp.concatenate([weights, weights], 0)
    high, low = halved(jnp.dot(masked(2), weights, preferred_element_type=f32))
    wide_3[...] = jnp.concatenate([high, high, low], 0)
    both = jnp.concatenate([masked(3), masked(3)], 1)
    weights = jnp.dot(both, jnp.concatenate([high, low], 0), preferred_element_type=f32)
    high, low = halved(weights)
    wide_4[...] = jnp.concatenate([high, high, low], 0)
    for b in range(BANDS):
        total = jnp.zeros((ROWS[0], LANES), f32)
        for e in range(EXPOSURES):
            p = e * BANDS + b
            total = total + s0[INNER + e, 8:72, :] * (s0[p, 8:72, :] * scale[p, 0:1, :])
        chosen[b] = total

    row_odd = lax.axis_index("core") == 1
    col_odd = jnp.bitwise_and(lax.axis_index("tx"), 1) == 1
    totals = (None, t1, t2, t3, t4)
    add_side(totals, (None, x1, x2, x3, x4), side, col_odd, held)
    rims_a, rims_b = got_a[0 : 2 * SLOTS], got_b[0 : 2 * SLOTS]
    below = jnp.where(row_odd, rims_a, rims_b).reshape(SLOTS, PLANES, LANES)
    above = jnp.where(row_odd, rims_b, rims_a).reshape(SLOTS, PLANES, LANES)
    for rim, at in ((below, (0,) * 5), (above, SIDE)):
        for level, line, slot, lane in MOVES:
            values = rim[slot]
            values = pltpu.roll(values, LANES - lane, 1) if lane else values
            totals[level][line_of(level, at[level] + line), :] += values


def fine_kernel(
    s0, chosen, x1, x2, x3, x4, side, inner, tile, wide_2, wide_3,
    b0, b1, b2, b3, t4,
    t1, t2, t3, held, across, spread,
):
    col_odd = jnp.bitwise_and(lax.axis_index("tx"), 1) == 1
    totals = (None, t1, t2, t3, t4)
    add_side(totals, (None, x1, x2, x3, x4), side, jnp.logical_not(col_odd), held)

    for level in (3, 2, 1):
        source, count, out = totals[level + 1], ROWS[level + 1], (None, b1, b2, b3)[level]
        wide = split_dot(source[0 : INNER * count, :], inner[...])
        across[:, 0:count, :] = wide.reshape(INNER, count, LANES)
        if level == 3:
            spread[:, 0 : ROWS[3], :] = jnp.zeros((INNER, ROWS[3], LANES), f32)
        expand_rows(across, spread, PAIRS[level])
        here = totals[level]
        bands = []
        for b in range(BANDS):
            total = jnp.zeros((ROWS[level], LANES), f32)
            for e in range(EXPOSURES):
                p = e * BANDS + b
                laplace = here[plane_of(level, p), :] - spread[p, 0 : ROWS[level], :]
                total = total + here[plane_of(level, INNER + e), :] * laplace
            bands.append(total)
        bands = jnp.concatenate(bands + [jnp.zeros((ROWS[level], LANES), f32)], 0)
        if level == 3:
            bands = split_dot_2(bands, wide_3[...])
        else:
            bands = split_dot(bands, wide_2[...] if level == 2 else tile[...])
        out[...] = bands[0 : BANDS * ROWS[level]].reshape(BANDS, ROWS[level], LANES)
    across[...] = split_dot(t1[0 : INNER * ROWS[1], :], tile[...]).reshape(INNER, ROWS[1], LANES)
    expand_rows_tile(across, spread, PAIRS[0])
    for b in range(BANDS):
        total = chosen[b]
        for e in range(EXPOSURES):
            total = total - s0[INNER + e, 8:72, :] * spread[e * BANDS + b]
        b0[b] = total


def collapse_kernel(
    rows, cols, patches, b0, b1, b2, b3, t4, inner, wide_4, top_weights, out,
    v5, window, c4, c3, c2, c1, across, spread,
):
    row, col = place_of(CORES)
    total = patches[0]
    for k in range(1, rows * cols):
        total = total + patches[k]
    lane = iota((PLANES, LANES), 1)
    total = jnp.concatenate([total, pltpu.roll(total, HALF, 1)], 0)
    v5[...] = jnp.where(lane < HALF, total, 0.0)

    def blend(less):
        total = None
        for e in range(EXPOSURES):
            part = v5[e * BANDS : (e + 1) * BANDS, :]
            if less is not None:
                part = part - less[e * BANDS : (e + 1) * BANDS, :]
            part = part * v5[INNER + e : INNER + e + 1, :]
            total = part if total is None else total + part
        return total

    window[0:PLANES, :] = v5[...]
    window[INNER : INNER + BANDS, :] = blend(None)
    less = split_dot(window[0:PLANES, :], top_weights[...])
    (is_5, row_5, col_5), _ = patch_places((BANDS, LANES), 1)
    along, aside = row_5 + (SIDE[5] * row - 1), col_5 + (WIDE[5] * col - 1)
    held = is_5 & (along >= 0) & (along < SIDE[5] * rows) & (aside >= 0) & (aside < WIDE[5] * cols)
    v5[INNER : INNER + BANDS, :] = jnp.where(held, blend(less) + less[INNER : INNER + BANDS, :], 0.0)

    window[...] = jnp.zeros((PLANES * 8, LANES), f32)
    for k in range(SIDE[5] + 3):
        line = v5[...]
        line = pltpu.roll(line, LANES - PITCH_5 * k, 1) if k else line
        window[line_of(5, k), :] = jnp.where(lane < WIDE[5] + 3, line, 0.0)

    across[:, 0:8, :] = split_dot(window[...], inner[...]).reshape(PLANES, 8, LANES)
    expand_rows(across, spread, PAIRS[4])
    inside = in_slab(4, row, col, rows, cols)
    for b in range(BANDS):
        total = spread[INNER + b, 0:8, :]
        for e in range(EXPOSURES):
            p = e * BANDS + b
            laplace = t4[plane_of(4, p), :] - spread[p, 0:8, :]
            total = total + t4[plane_of(4, INNER + e), :] * laplace
        c4[b] = jnp.where(inside, total, 0.0)
    c4[BANDS] = jnp.zeros((8, LANES), f32)

    wide = split_dot_2(c4[...].reshape(EXPOSURES * ROWS[4], LANES), wide_4[...])
    c4[...] = wide.reshape(EXPOSURES, ROWS[4], LANES)
    spread[0:BANDS, 0 : ROWS[3], :] = jnp.zeros((BANDS, ROWS[3], LANES), f32)
    for level, source, target, band in ((3, c4, c3, b3), (2, c3, c2, b2), (1, c2, c1, b1)):
        depth = ROWS[level]
        expand_rows(source.at[0:BANDS], spread.at[0:BANDS], PAIRS[level])
        along = iota((depth, LANES), 0)
        first, last = 1 - SIDE[level] * row, 1 + SIDE[level] * (rows - row)
        inside = (along >= first) & (along < last)
        for b in range(BANDS):
            target[b] = jnp.where(inside, band[b] + spread[b, 0:depth, :], 0.0)
    expand_rows_tile(c1, spread.at[0:BANDS], PAIRS[0])
    out[...] = b0[...] + spread[0:BANDS]


VMEM = pl.BlockSpec(memory_space=pltpu.VMEM)
SMEM = pl.BlockSpec(memory_space=pltpu.SMEM)
HBM = pl.BlockSpec(memory_space=pltpu.HBM)
PARAMS = pltpu.CompilerParams(vmem_limit_bytes=32 * 1024 * 1024)


def floats(*shape):
    return jax.ShapeDtypeStruct(shape, f32)


def halves(*shape):
    return jax.ShapeDtypeStruct(shape, bf16)


def scratch(*shape):
    return pltpu.VMEM(shape, f32)


def swaps(size, first):
    return [(i, ((i - first) ^ 1) + first) for i in range(first, size - first)]


def shards(images, gains, labels):
    chips, cols = lax.axis_size("chip"), lax.axis_size("tx")
    rows = CORES * chips
    images = images.reshape(INNER, ROWS[0], LANES)
    pinned = [pltpu.with_memory_space_constraint(x, pltpu.HBM) for x in (images, gains, labels)]
    levels = [floats(PLANES * ROWS[level], LANES) for level in range(1, 5)]
    s0, scale, x1, x2, x3, x4, send_a, send_b, strip_a, strip_b, patches = pl.pallas_call(
        lambda *refs: partial_kernel(rows, cols, *refs),
        out_shape=[
            floats(PLANES, 88, LANES),
            floats(INNER, 8, LANES),
            *levels,
            floats(RIMS, 8, LANES),
            floats(RIMS, 8, LANES),
            floats(6, 8, LANES),
            floats(6, 8, LANES),
            floats(rows * cols, 8, LANES),
        ],
        in_specs=[HBM] * 3,
        out_specs=[VMEM] * 10 + [HBM],
        scratch_shapes=[
            scratch(PLANES, 56, LANES),
            scratch(PLANES, 40, LANES),
            scratch(PLANES, 24, LANES),
            scratch(PLANES, 24, LANES),
            scratch(PLANES, 24, LANES),
            scratch(PLANES * 8, LANES),
            scratch(PLANES * 8, LANES),
            pltpu.VMEM((ROWS[0], LANES), jnp.int32),
            pltpu.SMEM((EXPOSURES, BANDS), f32),
            scratch(2, ROWS[1], LANES),
            scratch(2, STRIP, LANES),
            scratch(RIMS, 8, LANES),
            scratch(RIMS, 8, LANES),
            scratch((rows + 2 * REACH_ROWS) * (cols + 2 * REACH_COLS), 8, LANES),
            pltpu.SemaphoreType.DMA((EXPOSURES + 2,)),
            pltpu.SemaphoreType.DMA((rows,)),
        ],
        compiler_params=PARAMS,
        name="partial_levels",
    )(*pinned)
    got_b = lax.ppermute(send_b, ("chip", "core"), swaps(rows, 1))
    inner, tile, top, send_a = pl.pallas_call(
        tables_kernel,
        out_shape=[halves(2 * LANES, LANES)] * 3 + [floats(RIMS, 8, LANES)],
        in_specs=[VMEM],
        out_specs=[VMEM] * 4,
        compiler_params=PARAMS,
        name="expand_tables",
    )(send_a)
    got_a = lax.ppermute(send_a, "core", swaps(CORES, 0))
    odd = lax.axis_index("core") == 1
    rims_a, rims_b = got_a[2 * SLOTS :], got_b[2 * SLOTS :]
    below, above = jnp.where(odd, rims_a, rims_b), jnp.where(odd, rims_b, rims_a)
    strips = []
    for k, strip in enumerate((strip_a, strip_b)):
        low, high = below[3 * k : 3 * k + 3], above[3 * k : 3 * k + 3]
        none = jnp.zeros((1, 8, LANES), f32)
        rims = [low[0:1], none, high[0:1], low[1:2], high[1:2], low[2:3] + high[2:3]]
        strips.append(strip + jnp.concatenate(rims, 0))
    patches = lax.all_to_all(patches, ("chip", "core", "tx"), 0, 0, tiled=True)
    side_a = lax.ppermute(strips[0], "tx", swaps(cols, 0))
    side_b = lax.ppermute(strips[1], "tx", swaps(cols, 1))
    x1, x2, x3, x4, wide_2, wide_3, wide_4, chosen = pl.pallas_call(
        lambda *refs: rims_kernel(cols, *refs),
        out_shape=levels
        + [halves(2 * LANES, LANES), halves(3 * LANES, LANES), halves(3 * LANES, LANES)]
        + [floats(BANDS, ROWS[0], LANES)],
        in_specs=[VMEM] * 11,
        out_specs=[VMEM] * 8,
        scratch_shapes=[scratch(STRIP, LANES)],
        compiler_params=PARAMS,
        name="add_rims",
    )(x1, x2, x3, x4, got_a, got_b, side_a, inner, tile, s0, scale)
    b0, b1, b2, b3, t4 = pl.pallas_call(
        fine_kernel,
        out_shape=[floats(BANDS, ROWS[level], LANES) for level in range(4)] + [levels[3]],
        in_specs=[VMEM] * 11,
        out_specs=[VMEM] * 5,
        scratch_shapes=[
            scratch(PLANES * ROWS[1], LANES),
            scratch(PLANES * ROWS[2], LANES),
            scratch(PLANES * ROWS[3], LANES),
            scratch(STRIP, LANES),
            scratch(INNER, ROWS[1], LANES),
            scratch(INNER, ROWS[0], LANES),
        ],
        compiler_params=PARAMS,
        name="fine_laplacians",
    )(s0, chosen, x1, x2, x3, x4, side_b, inner, tile, wide_2, wide_3)
    return pl.pallas_call(
        lambda *refs: collapse_kernel(rows, cols, *refs),
        out_shape=floats(BANDS, ROWS[0], LANES),
        in_specs=[VMEM] * 9,
        out_specs=VMEM,
        scratch_shapes=[
            scratch(PLANES, LANES),
            scratch(PLANES * 8, LANES),
            scratch(EXPOSURES, ROWS[4], LANES),
            scratch(BANDS, ROWS[3], LANES),
            scratch(BANDS, ROWS[2], LANES),
            scratch(BANDS, ROWS[1], LANES),
            scratch(PLANES, ROWS[4], LANES),
            scratch(PLANES, ROWS[0], LANES),
        ],
        compiler_params=PARAMS,
        name="collapse",
    )(patches, b0, b1, b2, b3, t4, inner, wide_4, top)


def solution(mesh):
    groups, rows, cols = mesh.devices.shape
    devices = mesh.devices.reshape(groups, rows // CORES, CORES, cols)
    split = Mesh(devices, ("grp", "chip", "core", "tx"))
    down = ("grp", "chip", "core")
    return jax.shard_map(
        shards,
        mesh=split,
        in_specs=(P(None, None, down, "tx"), P(), P(down, "tx")),
        out_specs=P(None, down, "tx"),
        check_vma=False,
    )
```

```python
import jax
import jax.numpy as jnp
from jax import lax
from jax.experimental import pallas as pl
from jax.experimental.pallas import tpu as pltpu
from jax.sharding import Mesh, PartitionSpec as P

EXPOSURES = 4
BANDS = 3
INNER = EXPOSURES * BANDS
PLANES = INNER + EXPOSURES
LANES = 128
HALF = LANES // 2

SIDE = (64, 32, 16, 8, 4, 2, 1)
WIDE = (128, 64, 32, 16, 8, 4, 2)
ROWS = (64, 40, 24, 16, 8, 8, 8)
PAIRS = (32, 20, 12, 6, 4)
SLOTS = 3
MOVES = (
    (1, 0, 0, 0), (1, 1, 1, 0),
    (2, 0, 0, 66), (2, 1, 1, 66), (2, 2, 2, 0),
    (3, 0, 2, 35), (3, 1, 2, 54), (3, 2, 2, 73),
    (4, 0, 2, 92), (4, 1, 2, 103), (4, 2, 2, 114),
)
STRIP_AT = (0, 0, 0, 24, 40)
STRIP = 48
PITCH_5 = 8
PITCH_6 = 6
AT_6 = 40
RIMS = 2 * SLOTS + 6
CORES = 2
REACH_ROWS = 3
REACH_COLS = 2

f32 = jnp.float32
bf16 = jnp.bfloat16


def iota(shape, dim):
    return lax.broadcasted_iota(jnp.int32, shape, dim)


def reduce_weights(first):
    tap = iota((LANES, LANES), 0) - 2 * iota((LANES, LANES), 1) + first
    near = jnp.where((tap == 1) | (tap == 3), 0.25, 0.0)
    ends = jnp.where((tap == 0) | (tap == 4), 0.0625, 0.0)
    weights = jnp.where(tap == 2, 0.375, near + ends).astype(bf16)
    return jnp.concatenate([weights, weights], 0)


def expand_taps(source, target):
    away = 2 * source - target
    even = jnp.where(away == 0, 0.75, 0.0) + jnp.where((away == 2) | (away == -2), 0.125, 0.0)
    odd = jnp.where((away == 1) | (away == -1), 0.5, 0.0)
    return jnp.where(jnp.bitwise_and(target, 1) == 1, odd, even)


def expand_weights(first):
    shape = (LANES, LANES)
    weights = expand_taps(iota(shape, 0) - 1, iota(shape, 1) - first).astype(bf16)
    return jnp.concatenate([weights, weights], 0)


def split_dot(values, weights):
    high = values.astype(bf16)
    low = (values - high.astype(f32)).astype(bf16)
    return jnp.dot(jnp.concatenate([high, low], 1), weights, preferred_element_type=f32)


def split_dot_2(values, weights):
    high = values.astype(bf16)
    low = (values - high.astype(f32)).astype(bf16)
    return jnp.dot(jnp.concatenate([high, low, high], 1), weights, preferred_element_type=f32)


def in_slab(level, row, col, rows, cols):
    shape = (ROWS[level], LANES)
    along, across = iota(shape, 0), iota(shape, 1)
    first, last = 1 - SIDE[level] * row, 1 + SIDE[level] * (rows - row)
    left, right = 1 - WIDE[level] * col, 1 + WIDE[level] * (cols - col)
    return (along >= first) & (along < last) & (across >= left) & (across < right)


def expand_rows(source, target, count):
    before = source[:, 0:count, :]
    centre = source[:, 1 : count + 1, :]
    after = source[:, 2 : count + 2, :]
    target[:, pl.ds(0, count, stride=2), :] = (before + centre) * 0.5
    target[:, pl.ds(1, count, stride=2), :] = centre * 0.75 + (before + after) * 0.125


def expand_rows_tile(source, target, count):
    before = source[:, 0:count, :]
    centre = source[:, 1 : count + 1, :]
    after = source[:, 2 : count + 2, :]
    target[:, pl.ds(0, count, stride=2), :] = centre * 0.75 + (before + after) * 0.125
    target[:, pl.ds(1, count, stride=2), :] = (centre + after) * 0.5


def plane_of(level, p):
    return pl.ds(p * ROWS[level], ROWS[level])


def line_of(level, line):
    return pl.ds(line, PLANES, stride=ROWS[level])


def patch_places(shape, dim):
    lane = jnp.bitwise_and(iota(shape, dim), HALF - 1)
    row_5, col_5 = lax.shift_right_logical(lane, 3), jnp.bitwise_and(lane, PITCH_5 - 1)
    past = lane - AT_6
    row_6 = lax.shift_right_arithmetic(past * 43, 8)
    col_6 = past - PITCH_6 * row_6
    is_5 = (lane < AT_6) & (col_5 < WIDE[5] + 3)
    is_6 = (lane >= AT_6) & (col_6 < WIDE[6] + 3)
    return (is_5, row_5, col_5), (is_6, row_6, col_6)


def place_of(cores):
    return lax.axis_index("chip") * cores + lax.axis_index("core"), lax.axis_index("tx")


def partial_kernel(
    rows, cols, images, gains, labels,
    s0, scale, x1, x2, x3, x4, send_a, send_b, strip_a, strip_b, patches,
    s1, s2, s3, s4, s5, y5, y6, across, label, gain, first_part, other_part, low, high, slots, done, sent,
):
    row, col = place_of(CORES)
    copies = [
        pltpu.make_async_copy(labels, label, done.at[EXPOSURES]),
        pltpu.make_async_copy(gains, gain, done.at[EXPOSURES + 1]),
    ]
    for e in range(EXPOSURES):
        planes = pl.ds(e * BANDS, BANDS)
        copies.append(pltpu.make_async_copy(images.at[planes], s0.at[planes, pl.ds(8, 64)], done.at[e]))
    for copy in copies:
        copy.start()
    s0[:, 0:8, :] = jnp.zeros((PLANES, 8, LANES), f32)
    s0[:, 72:88, :] = jnp.zeros((PLANES, 16, LANES), f32)
    slots[...] = jnp.zeros(slots.shape, f32)
    for store in (s1, s2, s3, s4, s5):
        depth = store.shape[1]
        store[:, 0:8, :] = jnp.zeros((PLANES, 8, LANES), f32)
        store[:, depth - 8 : depth, :] = jnp.zeros((PLANES, 8, LANES), f32)
    edge_weights, weights = reduce_weights(4), reduce_weights(3)

    def reduce_rows(source, level, first, p, scale=None):
        count = ROWS[level]
        tap = [source[p, pl.ds(first + k, count, stride=2), :] for k in range(5)]
        total = tap[2] * 0.375 + (tap[1] + tap[3]) * 0.25 + (tap[0] + tap[4]) * 0.0625
        across[plane_of(level, p), :] = total if scale is None else total * scale

    def reduce_columns(level, weights, store, out):
        count = ROWS[level]
        result = split_dot(across[0 : PLANES * count, :], weights).reshape(PLANES, count, LANES)
        result = jnp.where(in_slab(level, row, col, rows, cols)[None], result, 0.0)
        out[...] = result.reshape(PLANES * count, LANES)
        if store is not None:
            store[:, 8 : 8 + count, :] = result

    copies[0].wait()
    for e in range(EXPOSURES):
        s0[INNER + e, 8:72, :] = jnp.where(label[...] == e, 1.0, 0.0)
        reduce_rows(s0, 1, 4, INNER + e)
    copies[1].wait()
    for p in range(INNER):
        scale[p] = jnp.full((8, LANES), gain[p // BANDS, p % BANDS], f32)
    for e in range(EXPOSURES):
        copies[2 + e].wait()
        for b in range(BANDS):
            reduce_rows(s0, 1, 4, e * BANDS + b, gain[e, b])
    reduce_columns(1, edge_weights, s1, x1)
    stores = ((2, s1, s2, x2), (3, s2, s3, x3), (4, s3, s4, x4), (5, s4, s5, y5), (6, s5, None, y6))
    for level, source, store, out in stores:
        for p in range(PLANES):
            reduce_rows(source, level, 5, p)
        reduce_columns(level, weights, store, out)

    patch = jnp.zeros((PLANES, LANES), f32)
    for k in range(SIDE[5] + 3):
        line = y5[line_of(5, k), :]
        patch = patch + (pltpu.roll(line, PITCH_5 * k, 1) if k else line)
    for k in range(SIDE[6] + 3):
        patch = patch + pltpu.roll(y6[line_of(6, k), :], AT_6 + PITCH_6 * k, 1)
    patch = patch[0:8, :] + pltpu.roll(patch[8:16, :], HALF, 1)
    width = cols + 2 * REACH_COLS
    (is_5, row_5, col_5), (is_6, row_6, col_6) = patch_places((8, LANES), 1)
    for down in range(-REACH_ROWS, REACH_ROWS + 1):
        for over in range(-REACH_COLS, REACH_COLS + 1):
            along, aside = row_6 + down, col_6 + 2 * over
            held = is_6 & (along >= 0) & (along < SIDE[6] + 3) & (aside >= 0) & (aside < WIDE[6] + 3)
            away = -(PITCH_6 * down + 2 * over) % LANES
            block = jnp.where(held, pltpu.roll(patch, away, 1) if away else patch, 0.0)
            if abs(down) < REACH_ROWS and abs(over) < REACH_COLS:
                along, aside = row_5 + 2 * down, col_5 + 4 * over
                held = is_5 & (along >= 0) & (along < SIDE[5] + 3) & (aside >= 0) & (aside < WIDE[5] + 3)
                away = -(2 * PITCH_5 * down + 4 * over) % LANES
                block = jnp.where(held, pltpu.roll(patch, away, 1) if away else patch, block)
            slots[(row + (down + REACH_ROWS)) * width + col + (over + REACH_COLS)] = block
    sends = []
    for r in range(rows):
        source = slots.at[pl.ds((r + REACH_ROWS) * width + REACH_COLS, cols)]
        sends.append(pltpu.make_async_copy(source, patches.at[pl.ds(r * cols, cols)], sent.at[r]))
        sends[r].start()

    levels = (None, x1, x2, x3, x4)
    odd = jnp.bitwise_and(col, 1) == 1
    for level in range(1, 5):
        count, wide = ROWS[level], WIDE[level]
        lane = iota((count, LANES), 1)
        before = jnp.zeros((count, LANES), f32)
        after = jnp.zeros((count, LANES), f32)
        for p in range(PLANES):
            plane = levels[level][plane_of(level, p), :]
            plane = pltpu.roll(plane, 3 * p, 1) if p else plane
            before = jnp.where((lane >= 3 * p) & (lane < 3 * p + 3), plane, before)
            after = jnp.where((lane >= wide + 3 * p) & (lane < wide + 3 * p + 3), plane, after)
        if level == 1:
            after = pltpu.roll(after, HALF, 1)
        else:
            before = pltpu.roll(before, HALF, 1)
            after = pltpu.roll(after, HALF - wide, 1)
        before = jnp.where(col == 0, 0.0, before)
        after = jnp.where(col == cols - 1, 0.0, after)
        for k, strip in enumerate((jnp.where(odd, before, after), jnp.where(odd, after, before))):
            if level == 1:
                first_part[k] = strip
            else:
                other_part[k, pl.ds(STRIP_AT[level], count), :] = strip
    for k, strip in enumerate((strip_a, strip_b)):
        strip[0:5] = (first_part[k] + other_part[k, 0:40, :]).reshape(5, 8, LANES)
        strip[5] = other_part[k, 40:48, :]

    low[...] = jnp.zeros((RIMS, 8, LANES), f32)
    high[...] = jnp.zeros((RIMS, 8, LANES), f32)
    for rim, at in ((low, (0,) * 5), (high, SIDE)):
        slots = [None] * SLOTS
        for level, line, slot, lane in MOVES:
            values = levels[level][line_of(level, at[level] + line), :]
            values = pltpu.roll(values, lane, 1) if lane else values
            slots[slot] = values if slots[slot] is None else slots[slot] + values
        for k in range(SLOTS):
            rim[2 * k : 2 * k + 2] = slots[k].reshape(2, 8, LANES)
    for k in range(2):
        at = 2 * SLOTS + 3 * k
        low[at, 0:3, :] = other_part[k, 0:3, :]
        low[at + 1, 0:3, :] = other_part[k, 24:27, :]
        low[at + 1, 0:2, :] += first_part[k, 0:2, :]
        low[at + 2, 4:7, :] = other_part[k, 40:43, :]
        high[at, 0:3, :] = other_part[k, 16:19, :]
        high[at, 0:2, :] += first_part[k, 32:34, :]
        high[at + 1, 0:3, :] = other_part[k, 32:35, :]
        high[at + 2, 0:3, :] = other_part[k, 44:47, :]
    odd = jnp.bitwise_and(row, 1) == 1
    downward = jnp.where(row == 0, 0.0, low[...])
    upward = jnp.where(row == rows - 1, 0.0, high[...])
    send_a[...] = jnp.where(odd, downward, upward)
    send_b[...] = jnp.where(odd, upward, downward)
    for copy in sends:
        copy.wait()


def tables_kernel(rims, inner, tile, top, send):
    send[...] = rims[...]
    inner[...] = expand_weights(1)
    tile[...] = expand_weights(0)
    _, (is_6, row_6, col_6) = patch_places((LANES, LANES), 0)
    (is_5, row_5, col_5), _ = patch_places((LANES, LANES), 1)
    low = (iota((LANES, LANES), 0) < HALF) & (iota((LANES, LANES), 1) < HALF)
    taps = expand_taps(row_6 - 1, row_5 - 1) * expand_taps(col_6 - 1, col_5 - 1)
    weights = jnp.where(is_5 & is_6 & low, taps, 0.0).astype(bf16)
    top[...] = jnp.concatenate([weights, weights], 0)


def add_side(totals, parts, strip, on_left, held):
    held[...] = strip[...].reshape(STRIP, LANES)
    for level in range(1, 5):
        count, wide, at = ROWS[level], WIDE[level], STRIP_AT[level]
        lane = iota((count, LANES), 1)
        start = 0 if level == 1 else HALF
        rim = held[at : at + count, :]
        rim = jnp.where((lane >= start) & (lane < start + 3 * PLANES), rim, 0.0)
        rim = jnp.where(on_left, rim, pltpu.roll(rim, wide, 1))
        first = jnp.where(on_left, 0, wide)
        inside = (lane >= first) & (lane < first + 3)
        for p in range(PLANES):
            away = -(start + 3 * p) % LANES
            place = plane_of(level, p)
            part = jnp.where(inside, pltpu.roll(rim, away, 1) if away else rim, 0.0)
            totals[level][place, :] = parts[level][place, :] + part


def rims_kernel(
    cols, x1, x2, x3, x4, got_a, got_b, side, inner, tile, s0, scale,
    t1, t2, t3, t4, wide, wide_4, chosen, held,
):
    col = lax.axis_index("tx")
    step = inner[0:LANES, :].astype(f32)

    def masked(level):
        across = iota((LANES, LANES), 1)
        first, last = 1 - WIDE[level] * col, 1 + WIDE[level] * (cols - col)
        return jnp.where((across >= first) & (across < last), step, 0.0).astype(bf16)

    def halved(weights):
        high = weights.astype(bf16)
        return high, (weights - high.astype(f32)).astype(bf16)

    second = jnp.dot(masked(1), tile[0:LANES, :], preferred_element_type=f32).astype(bf16)
    high, low = halved(jnp.dot(masked(2), second, preferred_element_type=f32))
    weights = jnp.concatenate([high, second, tile[0:LANES, :], low], 1)
    wide[...] = jnp.concatenate([weights, weights], 0)
    both = jnp.concatenate([masked(3), masked(3)], 1)
    weights = jnp.dot(both, jnp.concatenate([high, low], 0), preferred_element_type=f32)
    high, low = halved(weights)
    wide_4[...] = jnp.concatenate([high, high, low], 0)
    for b in range(BANDS):
        total = jnp.zeros((ROWS[0], LANES), f32)
        for e in range(EXPOSURES):
            p = e * BANDS + b
            total = total + s0[INNER + e, 8:72, :] * (s0[p, 8:72, :] * scale[p, 0:1, :])
        chosen[b] = total

    row_odd = lax.axis_index("core") == 1
    col_odd = jnp.bitwise_and(lax.axis_index("tx"), 1) == 1
    totals = (None, t1, t2, t3, t4)
    add_side(totals, (None, x1, x2, x3, x4), side, col_odd, held)
    rims_a, rims_b = got_a[0 : 2 * SLOTS], got_b[0 : 2 * SLOTS]
    below = jnp.where(row_odd, rims_a, rims_b).reshape(SLOTS, PLANES, LANES)
    above = jnp.where(row_odd, rims_b, rims_a).reshape(SLOTS, PLANES, LANES)
    for rim, at in ((below, (0,) * 5), (above, SIDE)):
        for level, line, slot, lane in MOVES:
            values = rim[slot]
            values = pltpu.roll(values, LANES - lane, 1) if lane else values
            totals[level][line_of(level, at[level] + line), :] += values


def fine_kernel(
    s0, chosen, x1, x2, x3, x4, side, inner, tile, wide,
    b0, b1, b2, b3, t4,
    t1, t2, t3, held, u1, u2, u3, u4, d0, d1, d2, d3, bands,
):
    col_odd = jnp.bitwise_and(lax.axis_index("tx"), 1) == 1
    totals = (None, t1, t2, t3, t4)
    add_side(totals, (None, x1, x2, x3, x4), side, jnp.logical_not(col_odd), held)

    values = [totals[level][0 : INNER * ROWS[level], :] for level in (4, 3, 2)]
    values = split_dot(jnp.concatenate(values, 0), inner[...])
    at = 0
    for level, store in ((4, u4), (3, u3), (2, u2)):
        count = INNER * ROWS[level]
        store[...] = values[at : at + count, :].reshape(INNER, ROWS[level], LANES)
        at += count
    values = split_dot(t1[0 : INNER * ROWS[1], :], tile[...])
    u1[...] = values.reshape(INNER, ROWS[1], LANES)
    d3[...] = jnp.zeros((INNER, ROWS[3], LANES), f32)
    at = 0
    for level, source, spread in ((3, u4, d3), (2, u3, d2), (1, u2, d1)):
        expand_rows(source, spread, PAIRS[level])
        here = totals[level]
        for b in range(BANDS):
            total = jnp.zeros((ROWS[level], LANES), f32)
            for e in range(EXPOSURES):
                p = e * BANDS + b
                laplace = here[plane_of(level, p), :] - spread[p]
                total = total + here[plane_of(level, INNER + e), :] * laplace
            bands[at : at + ROWS[level], :] = total
            at += ROWS[level]
    values = split_dot(bands[...], wide[...])
    at = 0
    for k, level, out in ((0, 3, b3), (1, 2, b2), (2, 1, b1)):
        count = BANDS * ROWS[level]
        part = values[at : at + count, k * LANES : (k + 1) * LANES]
        if level == 3:
            part = part + values[at : at + count, 3 * LANES :]
        out[...] = part.reshape(BANDS, ROWS[level], LANES)
        at += count
    expand_rows_tile(u1, d0, PAIRS[0])
    for b in range(BANDS):
        total = chosen[b]
        for e in range(EXPOSURES):
            total = total - s0[INNER + e, 8:72, :] * d0[e * BANDS + b]
        b0[b] = total


def collapse_kernel(
    rows, cols, patches, b0, b1, b2, b3, t4, inner, wide_4, top_weights, out,
    v5, window, c4, c3, c2, c1, across, spread,
):
    row, col = place_of(CORES)
    total = patches[0]
    for k in range(1, rows * cols):
        total = total + patches[k]
    lane = iota((PLANES, LANES), 1)
    total = jnp.concatenate([total, pltpu.roll(total, HALF, 1)], 0)
    v5[...] = jnp.where(lane < HALF, total, 0.0)

    def blend(less):
        total = None
        for e in range(EXPOSURES):
            part = v5[e * BANDS : (e + 1) * BANDS, :]
            if less is not None:
                part = part - less[e * BANDS : (e + 1) * BANDS, :]
            part = part * v5[INNER + e : INNER + e + 1, :]
            total = part if total is None else total + part
        return total

    window[0:PLANES, :] = v5[...]
    window[INNER : INNER + BANDS, :] = blend(None)
    less = split_dot(window[0:PLANES, :], top_weights[...])
    (is_5, row_5, col_5), _ = patch_places((BANDS, LANES), 1)
    along, aside = row_5 + (SIDE[5] * row - 1), col_5 + (WIDE[5] * col - 1)
    held = is_5 & (along >= 0) & (along < SIDE[5] * rows) & (aside >= 0) & (aside < WIDE[5] * cols)
    v5[INNER : INNER + BANDS, :] = jnp.where(held, blend(less) + less[INNER : INNER + BANDS, :], 0.0)

    window[...] = jnp.zeros((PLANES * 8, LANES), f32)
    for k in range(SIDE[5] + 3):
        line = v5[...]
        line = pltpu.roll(line, LANES - PITCH_5 * k, 1) if k else line
        window[line_of(5, k), :] = jnp.where(lane < WIDE[5] + 3, line, 0.0)

    across[:, 0:8, :] = split_dot(window[...], inner[...]).reshape(PLANES, 8, LANES)
    expand_rows(across, spread, PAIRS[4])
    inside = in_slab(4, row, col, rows, cols)
    for b in range(BANDS):
        total = spread[INNER + b, 0:8, :]
        for e in range(EXPOSURES):
            p = e * BANDS + b
            laplace = t4[plane_of(4, p), :] - spread[p, 0:8, :]
            total = total + t4[plane_of(4, INNER + e), :] * laplace
        c4[b] = jnp.where(inside, total, 0.0)
    c4[BANDS] = jnp.zeros((8, LANES), f32)

    wide = split_dot_2(c4[...].reshape(EXPOSURES * ROWS[4], LANES), wide_4[...])
    c4[...] = wide.reshape(EXPOSURES, ROWS[4], LANES)
    spread[0:BANDS, 0 : ROWS[3], :] = jnp.zeros((BANDS, ROWS[3], LANES), f32)
    for level, source, target, band in ((3, c4, c3, b3), (2, c3, c2, b2), (1, c2, c1, b1)):
        depth = ROWS[level]
        expand_rows(source.at[0:BANDS], spread.at[0:BANDS], PAIRS[level])
        along = iota((depth, LANES), 0)
        first, last = 1 - SIDE[level] * row, 1 + SIDE[level] * (rows - row)
        inside = (along >= first) & (along < last)
        for b in range(BANDS):
            target[b] = jnp.where(inside, band[b] + spread[b, 0:depth, :], 0.0)
    expand_rows_tile(c1, spread.at[0:BANDS], PAIRS[0])
    out[...] = b0[...] + spread[0:BANDS]


VMEM = pl.BlockSpec(memory_space=pltpu.VMEM)
SMEM = pl.BlockSpec(memory_space=pltpu.SMEM)
HBM = pl.BlockSpec(memory_space=pltpu.HBM)
PARAMS = pltpu.CompilerParams(vmem_limit_bytes=32 * 1024 * 1024)


def floats(*shape):
    return jax.ShapeDtypeStruct(shape, f32)


def halves(*shape):
    return jax.ShapeDtypeStruct(shape, bf16)


def scratch(*shape):
    return pltpu.VMEM(shape, f32)


def swaps(size, first):
    return [(i, ((i - first) ^ 1) + first) for i in range(first, size - first)]


def shards(images, gains, labels):
    chips, cols = lax.axis_size("chip"), lax.axis_size("tx")
    rows = CORES * chips
    images = images.reshape(INNER, ROWS[0], LANES)
    pinned = [pltpu.with_memory_space_constraint(x, pltpu.HBM) for x in (images, gains, labels)]
    levels = [floats(PLANES * ROWS[level], LANES) for level in range(1, 5)]
    s0, scale, x1, x2, x3, x4, send_a, send_b, strip_a, strip_b, patches = pl.pallas_call(
        lambda *refs: partial_kernel(rows, cols, *refs),
        out_shape=[
            floats(PLANES, 88, LANES),
            floats(INNER, 8, LANES),
            *levels,
            floats(RIMS, 8, LANES),
            floats(RIMS, 8, LANES),
            floats(6, 8, LANES),
            floats(6, 8, LANES),
            floats(rows * cols, 8, LANES),
        ],
        in_specs=[HBM] * 3,
        out_specs=[VMEM] * 10 + [HBM],
        scratch_shapes=[
            scratch(PLANES, 56, LANES),
            scratch(PLANES, 40, LANES),
            scratch(PLANES, 24, LANES),
            scratch(PLANES, 24, LANES),
            scratch(PLANES, 24, LANES),
            scratch(PLANES * 8, LANES),
            scratch(PLANES * 8, LANES),
            scratch(PLANES * ROWS[1], LANES),
            pltpu.VMEM((ROWS[0], LANES), jnp.int32),
            pltpu.SMEM((EXPOSURES, BANDS), f32),
            scratch(2, ROWS[1], LANES),
            scratch(2, STRIP, LANES),
            scratch(RIMS, 8, LANES),
            scratch(RIMS, 8, LANES),
            scratch((rows + 2 * REACH_ROWS) * (cols + 2 * REACH_COLS), 8, LANES),
            pltpu.SemaphoreType.DMA((EXPOSURES + 2,)),
            pltpu.SemaphoreType.DMA((rows,)),
        ],
        compiler_params=PARAMS,
        name="partial_levels",
    )(*pinned)
    got_b = lax.ppermute(send_b, ("chip", "core"), swaps(rows, 1))
    inner, tile, top, send_a = pl.pallas_call(
        tables_kernel,
        out_shape=[halves(2 * LANES, LANES)] * 3 + [floats(RIMS, 8, LANES)],
        in_specs=[VMEM],
        out_specs=[VMEM] * 4,
        compiler_params=PARAMS,
        name="expand_tables",
    )(send_a)
    got_a = lax.ppermute(send_a, "core", swaps(CORES, 0))
    odd = lax.axis_index("core") == 1
    rims_a, rims_b = got_a[2 * SLOTS :], got_b[2 * SLOTS :]
    below, above = jnp.where(odd, rims_a, rims_b), jnp.where(odd, rims_b, rims_a)
    strips = []
    for k, strip in enumerate((strip_a, strip_b)):
        low, high = below[3 * k : 3 * k + 3], above[3 * k : 3 * k + 3]
        none = jnp.zeros((1, 8, LANES), f32)
        rims = [low[0:1], none, high[0:1], low[1:2], high[1:2], low[2:3] + high[2:3]]
        strips.append(strip + jnp.concatenate(rims, 0))
    patches = lax.all_to_all(patches, ("chip", "core", "tx"), 0, 0, tiled=True)
    side_a = lax.ppermute(strips[0], "tx", swaps(cols, 0))
    side_b = lax.ppermute(strips[1], "tx", swaps(cols, 1))
    x1, x2, x3, x4, wide, wide_4, chosen = pl.pallas_call(
        lambda *refs: rims_kernel(cols, *refs),
        out_shape=levels
        + [halves(2 * LANES, 4 * LANES), halves(3 * LANES, LANES)]
        + [floats(BANDS, ROWS[0], LANES)],
        in_specs=[VMEM] * 11,
        out_specs=[VMEM] * 7,
        scratch_shapes=[scratch(STRIP, LANES)],
        compiler_params=PARAMS,
        name="add_rims",
    )(x1, x2, x3, x4, got_a, got_b, side_a, inner, tile, s0, scale)
    b0, b1, b2, b3, t4 = pl.pallas_call(
        fine_kernel,
        out_shape=[floats(BANDS, ROWS[level], LANES) for level in range(4)] + [levels[3]],
        in_specs=[VMEM] * 10,
        out_specs=[VMEM] * 5,
        scratch_shapes=[
            scratch(PLANES * ROWS[1], LANES),
            scratch(PLANES * ROWS[2], LANES),
            scratch(PLANES * ROWS[3], LANES),
            scratch(STRIP, LANES),
            *[scratch(INNER, ROWS[level], LANES) for level in (1, 2, 3, 4, 0, 1, 2, 3)],
            scratch(BANDS * (ROWS[1] + ROWS[2] + ROWS[3]), LANES),
        ],
        compiler_params=PARAMS,
        name="fine_laplacians",
    )(s0, chosen, x1, x2, x3, x4, side_b, inner, tile, wide)
    return pl.pallas_call(
        lambda *refs: collapse_kernel(rows, cols, *refs),
        out_shape=floats(BANDS, ROWS[0], LANES),
        in_specs=[VMEM] * 9,
        out_specs=VMEM,
        scratch_shapes=[
            scratch(PLANES, LANES),
            scratch(PLANES * 8, LANES),
            scratch(EXPOSURES, ROWS[4], LANES),
            scratch(BANDS, ROWS[3], LANES),
            scratch(BANDS, ROWS[2], LANES),
            scratch(BANDS, ROWS[1], LANES),
            scratch(PLANES, ROWS[4], LANES),
            scratch(PLANES, ROWS[0], LANES),
        ],
        compiler_params=PARAMS,
        name="collapse",
    )(patches, b0, b1, b2, b3, t4, inner, wide_4, top)


def solution(mesh):
    groups, rows, cols = mesh.devices.shape
    devices = mesh.devices.reshape(groups, rows // CORES, CORES, cols)
    split = Mesh(devices, ("grp", "chip", "core", "tx"))
    down = ("grp", "chip", "core")
    return jax.shard_map(
        shards,
        mesh=split,
        in_specs=(P(None, None, down, "tx"), P(), P(down, "tx")),
        out_specs=P(None, down, "tx"),
        check_vma=False,
    )
```

```python
import jax
import jax.numpy as jnp
from jax import lax
from jax.experimental import pallas as pl
from jax.experimental.pallas import tpu as pltpu
from jax.sharding import Mesh, PartitionSpec as P

EXPOSURES = 4
BANDS = 3
INNER = EXPOSURES * BANDS
PLANES = INNER + EXPOSURES
LANES = 128
HALF = LANES // 2

SIDE = (64, 32, 16, 8, 4, 2, 1)
WIDE = (128, 64, 32, 16, 8, 4, 2)
ROWS = (64, 40, 24, 16, 8, 8, 8)
PAIRS = (32, 20, 12, 6, 4)
SLOTS = 3
MOVES = (
    (1, 0, 0, 0), (1, 1, 1, 0),
    (2, 0, 0, 66), (2, 1, 1, 66), (2, 2, 2, 0),
    (3, 0, 2, 35), (3, 1, 2, 54), (3, 2, 2, 73),
    (4, 0, 2, 92), (4, 1, 2, 103), (4, 2, 2, 114),
)
STRIP_AT = (0, 0, 0, 24, 40)
STRIP = 48
PITCH_5 = 8
PITCH_6 = 6
AT_6 = 40
RIMS = 2 * SLOTS + 6
CORES = 2
REACH_ROWS = 3
REACH_COLS = 2

f32 = jnp.float32
bf16 = jnp.bfloat16


def iota(shape, dim):
    return lax.broadcasted_iota(jnp.int32, shape, dim)


def reduce_weights(first):
    tap = iota((LANES, LANES), 0) - 2 * iota((LANES, LANES), 1) + first
    near = jnp.where((tap == 1) | (tap == 3), 0.25, 0.0)
    ends = jnp.where((tap == 0) | (tap == 4), 0.0625, 0.0)
    weights = jnp.where(tap == 2, 0.375, near + ends).astype(bf16)
    return jnp.concatenate([weights, weights], 0)


def expand_taps(source, target):
    away = 2 * source - target
    even = jnp.where(away == 0, 0.75, 0.0) + jnp.where((away == 2) | (away == -2), 0.125, 0.0)
    odd = jnp.where((away == 1) | (away == -1), 0.5, 0.0)
    return jnp.where(jnp.bitwise_and(target, 1) == 1, odd, even)


def expand_weights(first):
    shape = (LANES, LANES)
    weights = expand_taps(iota(shape, 0) - 1, iota(shape, 1) - first).astype(bf16)
    return jnp.concatenate([weights, weights], 0)


def split_dot(values, weights):
    high = values.astype(bf16)
    low = (values - high.astype(f32)).astype(bf16)
    return jnp.dot(jnp.concatenate([high, low], 1), weights, preferred_element_type=f32)


def in_slab(level, row, col, rows, cols):
    shape = (ROWS[level], LANES)
    along, across = iota(shape, 0), iota(shape, 1)
    first, last = 1 - SIDE[level] * row, 1 + SIDE[level] * (rows - row)
    left, right = 1 - WIDE[level] * col, 1 + WIDE[level] * (cols - col)
    return (along >= first) & (along < last) & (across >= left) & (across < right)


def expand_rows(source, target, count):
    before = source[:, 0:count, :]
    centre = source[:, 1 : count + 1, :]
    after = source[:, 2 : count + 2, :]
    target[:, pl.ds(0, count, stride=2), :] = (before + centre) * 0.5
    target[:, pl.ds(1, count, stride=2), :] = centre * 0.75 + (before + after) * 0.125


def expand_rows_tile(source, target, count):
    before = source[:, 0:count, :]
    centre = source[:, 1 : count + 1, :]
    after = source[:, 2 : count + 2, :]
    target[:, pl.ds(0, count, stride=2), :] = centre * 0.75 + (before + after) * 0.125
    target[:, pl.ds(1, count, stride=2), :] = (centre + after) * 0.5


def plane_of(level, p):
    return pl.ds(p * ROWS[level], ROWS[level])


def line_of(level, line):
    return pl.ds(line, PLANES, stride=ROWS[level])


def patch_places(shape, dim):
    lane = jnp.bitwise_and(iota(shape, dim), HALF - 1)
    row_5, col_5 = lax.shift_right_logical(lane, 3), jnp.bitwise_and(lane, PITCH_5 - 1)
    past = lane - AT_6
    row_6 = lax.shift_right_arithmetic(past * 43, 8)
    col_6 = past - PITCH_6 * row_6
    is_5 = (lane < AT_6) & (col_5 < WIDE[5] + 3)
    is_6 = (lane >= AT_6) & (col_6 < WIDE[6] + 3)
    return (is_5, row_5, col_5), (is_6, row_6, col_6)


def place_of(cores):
    return lax.axis_index("chip") * cores + lax.axis_index("core"), lax.axis_index("tx")


def partial_kernel(
    rows, cols, images, gains, labels,
    s0, scale, x1, x2, x3, x4, send_a, send_b, strip_a, strip_b, patches,
    s1, s2, s3, s4, s5, y5, y6, across, label, gain, first_part, other_part, low, high, slots, done, sent,
):
    row, col = place_of(CORES)
    copies = [
        pltpu.make_async_copy(labels, label, done.at[EXPOSURES]),
        pltpu.make_async_copy(gains, gain, done.at[EXPOSURES + 1]),
    ]
    for e in range(EXPOSURES):
        planes = pl.ds(e * BANDS, BANDS)
        copies.append(pltpu.make_async_copy(images.at[planes], s0.at[planes, pl.ds(8, 64)], done.at[e]))
    for copy in copies:
        copy.start()
    s0[:, 0:8, :] = jnp.zeros((PLANES, 8, LANES), f32)
    s0[:, 72:88, :] = jnp.zeros((PLANES, 16, LANES), f32)
    slots[...] = jnp.zeros(slots.shape, f32)
    for store in (s1, s2, s3, s4, s5):
        depth = store.shape[1]
        store[:, 0:8, :] = jnp.zeros((PLANES, 8, LANES), f32)
        store[:, depth - 8 : depth, :] = jnp.zeros((PLANES, 8, LANES), f32)
    edge_weights, weights = reduce_weights(4), reduce_weights(3)

    def reduce_rows(source, level, first, p, scale=None):
        count = ROWS[level]
        tap = [source[p, pl.ds(first + k, count, stride=2), :] for k in range(5)]
        total = tap[2] * 0.375 + (tap[1] + tap[3]) * 0.25 + (tap[0] + tap[4]) * 0.0625
        across[plane_of(level, p), :] = total if scale is None else total * scale

    def reduce_columns(level, weights, store, out):
        count = ROWS[level]
        result = split_dot(across[0 : PLANES * count, :], weights).reshape(PLANES, count, LANES)
        result = jnp.where(in_slab(level, row, col, rows, cols)[None], result, 0.0)
        out[...] = result.reshape(PLANES * count, LANES)
        if store is not None:
            store[:, 8 : 8 + count, :] = result

    copies[0].wait()
    for e in range(EXPOSURES):
        s0[INNER + e, 8:72, :] = jnp.where(label[...] == e, 1.0, 0.0)
        reduce_rows(s0, 1, 4, INNER + e)
    copies[1].wait()
    for p in range(INNER):
        scale[p] = jnp.full((8, LANES), gain[p // BANDS, p % BANDS], f32)
    for e in range(EXPOSURES):
        copies[2 + e].wait()
        for b in range(BANDS):
            reduce_rows(s0, 1, 4, e * BANDS + b, gain[e, b])
    reduce_columns(1, edge_weights, s1, x1)
    stores = ((2, s1, s2, x2), (3, s2, s3, x3), (4, s3, s4, x4), (5, s4, s5, y5), (6, s5, None, y6))
    for level, source, store, out in stores:
        for p in range(PLANES):
            reduce_rows(source, level, 5, p)
        reduce_columns(level, weights, store, out)

    patch = jnp.zeros((PLANES, LANES), f32)
    for k in range(SIDE[5] + 3):
        line = y5[line_of(5, k), :]
        patch = patch + (pltpu.roll(line, PITCH_5 * k, 1) if k else line)
    for k in range(SIDE[6] + 3):
        patch = patch + pltpu.roll(y6[line_of(6, k), :], AT_6 + PITCH_6 * k, 1)
    patch = patch[0:8, :] + pltpu.roll(patch[8:16, :], HALF, 1)
    width = cols + 2 * REACH_COLS
    (is_5, row_5, col_5), (is_6, row_6, col_6) = patch_places((8, LANES), 1)
    for down in range(-REACH_ROWS, REACH_ROWS + 1):
        for over in range(-REACH_COLS, REACH_COLS + 1):
            along, aside = row_6 + down, col_6 + 2 * over
            held = is_6 & (along >= 0) & (along < SIDE[6] + 3) & (aside >= 0) & (aside < WIDE[6] + 3)
            away = -(PITCH_6 * down + 2 * over) % LANES
            block = jnp.where(held, pltpu.roll(patch, away, 1) if away else patch, 0.0)
            if abs(down) < REACH_ROWS and abs(over) < REACH_COLS:
                along, aside = row_5 + 2 * down, col_5 + 4 * over
                held = is_5 & (along >= 0) & (along < SIDE[5] + 3) & (aside >= 0) & (aside < WIDE[5] + 3)
                away = -(2 * PITCH_5 * down + 4 * over) % LANES
                block = jnp.where(held, pltpu.roll(patch, away, 1) if away else patch, block)
            slots[(row + (down + REACH_ROWS)) * width + col + (over + REACH_COLS)] = block
    sends = []
    for r in range(rows):
        source = slots.at[pl.ds((r + REACH_ROWS) * width + REACH_COLS, cols)]
        sends.append(pltpu.make_async_copy(source, patches.at[pl.ds(r * cols, cols)], sent.at[r]))
        sends[r].start()

    levels = (None, x1, x2, x3, x4)
    odd = jnp.bitwise_and(col, 1) == 1
    for level in range(1, 5):
        count, wide = ROWS[level], WIDE[level]
        lane = iota((count, LANES), 1)
        before = jnp.zeros((count, LANES), f32)
        after = jnp.zeros((count, LANES), f32)
        for p in range(PLANES):
            plane = levels[level][plane_of(level, p), :]
            plane = pltpu.roll(plane, 3 * p, 1) if p else plane
            before = jnp.where((lane >= 3 * p) & (lane < 3 * p + 3), plane, before)
            after = jnp.where((lane >= wide + 3 * p) & (lane < wide + 3 * p + 3), plane, after)
        if level == 1:
            after = pltpu.roll(after, HALF, 1)
        else:
            before = pltpu.roll(before, HALF, 1)
            after = pltpu.roll(after, HALF - wide, 1)
        before = jnp.where(col == 0, 0.0, before)
        after = jnp.where(col == cols - 1, 0.0, after)
        for k, strip in enumerate((jnp.where(odd, before, after), jnp.where(odd, after, before))):
            if level == 1:
                first_part[k] = strip
            else:
                other_part[k, pl.ds(STRIP_AT[level], count), :] = strip
    for k, strip in enumerate((strip_a, strip_b)):
        strip[0:5] = (first_part[k] + other_part[k, 0:40, :]).reshape(5, 8, LANES)
        strip[5] = other_part[k, 40:48, :]

    low[...] = jnp.zeros((RIMS, 8, LANES), f32)
    high[...] = jnp.zeros((RIMS, 8, LANES), f32)
    for rim, at in ((low, (0,) * 5), (high, SIDE)):
        slots = [None] * SLOTS
        for level, line, slot, lane in MOVES:
            values = levels[level][line_of(level, at[level] + line), :]
            values = pltpu.roll(values, lane, 1) if lane else values
            slots[slot] = values if slots[slot] is None else slots[slot] + values
        for k in range(SLOTS):
            rim[2 * k : 2 * k + 2] = slots[k].reshape(2, 8, LANES)
    for k in range(2):
        at = 2 * SLOTS + 3 * k
        low[at, 0:3, :] = other_part[k, 0:3, :]
        low[at + 1, 0:3, :] = other_part[k, 24:27, :]
        low[at + 1, 0:2, :] += first_part[k, 0:2, :]
        low[at + 2, 4:7, :] = other_part[k, 40:43, :]
        high[at, 0:3, :] = other_part[k, 16:19, :]
        high[at, 0:2, :] += first_part[k, 32:34, :]
        high[at + 1, 0:3, :] = other_part[k, 32:35, :]
        high[at + 2, 0:3, :] = other_part[k, 44:47, :]
    odd = jnp.bitwise_and(row, 1) == 1
    downward = jnp.where(row == 0, 0.0, low[...])
    upward = jnp.where(row == rows - 1, 0.0, high[...])
    send_a[...] = jnp.where(odd, downward, upward)
    send_b[...] = jnp.where(odd, upward, downward)
    for copy in sends:
        copy.wait()


def tables_kernel(rims, inner, tile, top, send):
    send[...] = rims[...]
    inner[...] = expand_weights(1)
    tile[...] = expand_weights(0)
    _, (is_6, row_6, col_6) = patch_places((LANES, LANES), 0)
    (is_5, row_5, col_5), _ = patch_places((LANES, LANES), 1)
    low = (iota((LANES, LANES), 0) < HALF) & (iota((LANES, LANES), 1) < HALF)
    taps = expand_taps(row_6 - 1, row_5 - 1) * expand_taps(col_6 - 1, col_5 - 1)
    weights = jnp.where(is_5 & is_6 & low, taps, 0.0).astype(bf16)
    top[...] = jnp.concatenate([weights, weights], 0)


def add_side(totals, parts, strip, on_left, held):
    held[...] = strip[...].reshape(STRIP, LANES)
    for level in range(1, 5):
        count, wide, at = ROWS[level], WIDE[level], STRIP_AT[level]
        lane = iota((count, LANES), 1)
        start = 0 if level == 1 else HALF
        rim = held[at : at + count, :]
        rim = jnp.where((lane >= start) & (lane < start + 3 * PLANES), rim, 0.0)
        rim = jnp.where(on_left, rim, pltpu.roll(rim, wide, 1))
        first = jnp.where(on_left, 0, wide)
        inside = (lane >= first) & (lane < first + 3)
        for p in range(PLANES):
            away = -(start + 3 * p) % LANES
            place = plane_of(level, p)
            part = jnp.where(inside, pltpu.roll(rim, away, 1) if away else rim, 0.0)
            totals[level][place, :] = parts[level][place, :] + part


def rims_kernel(
    cols, x1, x2, x3, x4, got_a, got_b, side, inner, tile, s0, scale,
    t1, t2, t3, t4, wide, chosen, held,
):
    col = lax.axis_index("tx")
    step = inner[0:LANES, :].astype(f32)

    def masked(level):
        across = iota((LANES, LANES), 1)
        first, last = 1 - WIDE[level] * col, 1 + WIDE[level] * (cols - col)
        return jnp.where((across >= first) & (across < last), step, 0.0).astype(bf16)

    def halved(weights):
        high = weights.astype(bf16)
        return high, (weights - high.astype(f32)).astype(bf16)

    second = jnp.dot(masked(1), tile[0:LANES, :], preferred_element_type=f32).astype(bf16)
    high, low = halved(jnp.dot(masked(2), second, preferred_element_type=f32))
    both = jnp.concatenate([masked(3), masked(3)], 1)
    fourth = jnp.dot(both, jnp.concatenate([high, low], 0), preferred_element_type=f32)
    high_4, low_4 = halved(fourth)
    weights = jnp.concatenate([high_4, high, second, tile[0:LANES, :], low_4, low], 1)
    wide[...] = jnp.concatenate([weights, weights], 0)
    for b in range(BANDS):
        total = jnp.zeros((ROWS[0], LANES), f32)
        for e in range(EXPOSURES):
            p = e * BANDS + b
            total = total + s0[INNER + e, 8:72, :] * (s0[p, 8:72, :] * scale[p, 0:1, :])
        chosen[b] = total

    row_odd = lax.axis_index("core") == 1
    col_odd = jnp.bitwise_and(lax.axis_index("tx"), 1) == 1
    totals = (None, t1, t2, t3, t4)
    add_side(totals, (None, x1, x2, x3, x4), side, col_odd, held)
    rims_a, rims_b = got_a[0 : 2 * SLOTS], got_b[0 : 2 * SLOTS]
    below = jnp.where(row_odd, rims_a, rims_b).reshape(SLOTS, PLANES, LANES)
    above = jnp.where(row_odd, rims_b, rims_a).reshape(SLOTS, PLANES, LANES)
    for rim, at in ((below, (0,) * 5), (above, SIDE)):
        for level, line, slot, lane in MOVES:
            values = rim[slot]
            values = pltpu.roll(values, LANES - lane, 1) if lane else values
            totals[level][line_of(level, at[level] + line), :] += values


def finish_kernel(
    rows, cols, s0, chosen, x1, x2, x3, x4, side, inner, tile, wide, coarse, out,
    t1, t2, t3, t4, held, u1, u2, u3, u4, d0, d1, d2, d3, bands, c4, c3, c2, c1, spread,
):
    row, col = place_of(CORES)
    col_odd = jnp.bitwise_and(col, 1) == 1
    totals = (None, t1, t2, t3, t4)
    add_side(totals, (None, x1, x2, x3, x4), side, jnp.logical_not(col_odd), held)

    values = [totals[level][0 : INNER * ROWS[level], :] for level in (4, 3, 2)]
    values = split_dot(jnp.concatenate(values, 0), inner[...])
    at = 0
    for level, store in ((4, u4), (3, u3), (2, u2)):
        count = INNER * ROWS[level]
        store[...] = values[at : at + count, :].reshape(INNER, ROWS[level], LANES)
        at += count
    values = split_dot(t1[0 : INNER * ROWS[1], :], tile[...])
    u1[...] = values.reshape(INNER, ROWS[1], LANES)
    d3[...] = jnp.zeros((INNER, ROWS[3], LANES), f32)
    inside = in_slab(4, row, col, rows, cols)
    for b in range(BANDS):
        total = coarse[INNER + b]
        for e in range(EXPOSURES):
            p = e * BANDS + b
            laplace = t4[plane_of(4, p), :] - coarse[p]
            total = total + t4[plane_of(4, INNER + e), :] * laplace
        bands[b * ROWS[4] : (b + 1) * ROWS[4], :] = jnp.where(inside, total, 0.0)
    bands[BANDS * ROWS[4] : PLANES // 4 * ROWS[4], :] = jnp.zeros((ROWS[4], LANES), f32)
    at = PLANES // 4 * ROWS[4]
    for level, source, spread_out in ((3, u4, d3), (2, u3, d2), (1, u2, d1)):
        expand_rows(source, spread_out, PAIRS[level])
        here = totals[level]
        for b in range(BANDS):
            total = jnp.zeros((ROWS[level], LANES), f32)
            for e in range(EXPOSURES):
                p = e * BANDS + b
                laplace = here[plane_of(level, p), :] - spread_out[p]
                total = total + here[plane_of(level, INNER + e), :] * laplace
            bands[at : at + ROWS[level], :] = total
            at += ROWS[level]
    values = split_dot(bands[...], wide[...])
    at, parts = 0, {}
    for k, level in enumerate((4, 3, 2, 1)):
        count = BANDS * ROWS[level]
        part = values[at : at + count, k * LANES : (k + 1) * LANES]
        if k < 2:
            part = part + values[at : at + count, (k + 4) * LANES : (k + 5) * LANES]
        parts[level] = part.reshape(BANDS, ROWS[level], LANES)
        at += PLANES // 4 * ROWS[4] if level == 4 else count
    c4[...] = parts[4]
    for level, store in ((3, c3), (2, c2), (1, c1)):
        store[...] = parts[level]
    expand_rows_tile(u1, d0, PAIRS[0])
    for b in range(BANDS):
        total = chosen[b]
        for e in range(EXPOSURES):
            total = total - s0[INNER + e, 8:72, :] * d0[e * BANDS + b]
        out[b] = total
    spread[:, 0 : ROWS[3], :] = jnp.zeros((BANDS, ROWS[3], LANES), f32)
    for level, source, target in ((3, c4, c3), (2, c3, c2), (1, c2, c1)):
        depth = ROWS[level]
        expand_rows(source, spread, PAIRS[level])
        along = iota((depth, LANES), 0)
        first, last = 1 - SIDE[level] * row, 1 + SIDE[level] * (rows - row)
        inside = (along >= first) & (along < last)
        for b in range(BANDS):
            target[b] = jnp.where(inside, target[b] + spread[b, 0:depth, :], 0.0)
    expand_rows_tile(c1, spread, PAIRS[0])
    out[...] = out[...] + spread[...]


def coarse_kernel(rows, cols, patches, inner, top_weights, spread, v5, window, across):
    row, col = place_of(CORES)
    total = patches[0]
    for k in range(1, rows * cols):
        total = total + patches[k]
    lane = iota((PLANES, LANES), 1)
    total = jnp.concatenate([total, pltpu.roll(total, HALF, 1)], 0)
    v5[...] = jnp.where(lane < HALF, total, 0.0)

    def blend(less):
        total = None
        for e in range(EXPOSURES):
            part = v5[e * BANDS : (e + 1) * BANDS, :]
            if less is not None:
                part = part - less[e * BANDS : (e + 1) * BANDS, :]
            part = part * v5[INNER + e : INNER + e + 1, :]
            total = part if total is None else total + part
        return total

    window[0:PLANES, :] = v5[...]
    window[INNER : INNER + BANDS, :] = blend(None)
    less = split_dot(window[0:PLANES, :], top_weights[...])
    (is_5, row_5, col_5), _ = patch_places((BANDS, LANES), 1)
    along, aside = row_5 + (SIDE[5] * row - 1), col_5 + (WIDE[5] * col - 1)
    held = is_5 & (along >= 0) & (along < SIDE[5] * rows) & (aside >= 0) & (aside < WIDE[5] * cols)
    v5[INNER : INNER + BANDS, :] = jnp.where(held, blend(less) + less[INNER : INNER + BANDS, :], 0.0)

    window[...] = jnp.zeros((PLANES * 8, LANES), f32)
    for k in range(SIDE[5] + 3):
        line = v5[...]
        line = pltpu.roll(line, LANES - PITCH_5 * k, 1) if k else line
        window[line_of(5, k), :] = jnp.where(lane < WIDE[5] + 3, line, 0.0)

    across[:, 0:8, :] = split_dot(window[...], inner[...]).reshape(PLANES, 8, LANES)
    expand_rows(across, spread, PAIRS[4])


VMEM = pl.BlockSpec(memory_space=pltpu.VMEM)
SMEM = pl.BlockSpec(memory_space=pltpu.SMEM)
HBM = pl.BlockSpec(memory_space=pltpu.HBM)
PARAMS = pltpu.CompilerParams(vmem_limit_bytes=32 * 1024 * 1024)


def floats(*shape):
    return jax.ShapeDtypeStruct(shape, f32)


def halves(*shape):
    return jax.ShapeDtypeStruct(shape, bf16)


def scratch(*shape):
    return pltpu.VMEM(shape, f32)


def swaps(size, first):
    return [(i, ((i - first) ^ 1) + first) for i in range(first, size - first)]


def shards(images, gains, labels):
    chips, cols = lax.axis_size("chip"), lax.axis_size("tx")
    rows = CORES * chips
    images = images.reshape(INNER, ROWS[0], LANES)
    pinned = [pltpu.with_memory_space_constraint(x, pltpu.HBM) for x in (images, gains, labels)]
    levels = [floats(PLANES * ROWS[level], LANES) for level in range(1, 5)]
    s0, scale, x1, x2, x3, x4, send_a, send_b, strip_a, strip_b, patches = pl.pallas_call(
        lambda *refs: partial_kernel(rows, cols, *refs),
        out_shape=[
            floats(PLANES, 88, LANES),
            floats(INNER, 8, LANES),
            *levels,
            floats(RIMS, 8, LANES),
            floats(RIMS, 8, LANES),
            floats(6, 8, LANES),
            floats(6, 8, LANES),
            floats(rows * cols, 8, LANES),
        ],
        in_specs=[HBM] * 3,
        out_specs=[VMEM] * 10 + [HBM],
        scratch_shapes=[
            scratch(PLANES, 56, LANES),
            scratch(PLANES, 40, LANES),
            scratch(PLANES, 24, LANES),
            scratch(PLANES, 24, LANES),
            scratch(PLANES, 24, LANES),
            scratch(PLANES * 8, LANES),
            scratch(PLANES * 8, LANES),
            scratch(PLANES * ROWS[1], LANES),
            pltpu.VMEM((ROWS[0], LANES), jnp.int32),
            pltpu.SMEM((EXPOSURES, BANDS), f32),
            scratch(2, ROWS[1], LANES),
            scratch(2, STRIP, LANES),
            scratch(RIMS, 8, LANES),
            scratch(RIMS, 8, LANES),
            scratch((rows + 2 * REACH_ROWS) * (cols + 2 * REACH_COLS), 8, LANES),
            pltpu.SemaphoreType.DMA((EXPOSURES + 2,)),
            pltpu.SemaphoreType.DMA((rows,)),
        ],
        compiler_params=PARAMS,
        name="partial_levels",
    )(*pinned)
    got_b = lax.ppermute(send_b, ("chip", "core"), swaps(rows, 1))
    inner, tile, top, send_a = pl.pallas_call(
        tables_kernel,
        out_shape=[halves(2 * LANES, LANES)] * 3 + [floats(RIMS, 8, LANES)],
        in_specs=[VMEM],
        out_specs=[VMEM] * 4,
        compiler_params=PARAMS,
        name="expand_tables",
    )(send_a)
    got_a = lax.ppermute(send_a, "core", swaps(CORES, 0))
    odd = lax.axis_index("core") == 1
    rims_a, rims_b = got_a[2 * SLOTS :], got_b[2 * SLOTS :]
    below, above = jnp.where(odd, rims_a, rims_b), jnp.where(odd, rims_b, rims_a)
    strips = []
    for k, strip in enumerate((strip_a, strip_b)):
        low, high = below[3 * k : 3 * k + 3], above[3 * k : 3 * k + 3]
        none = jnp.zeros((1, 8, LANES), f32)
        rims = [low[0:1], none, high[0:1], low[1:2], high[1:2], low[2:3] + high[2:3]]
        strips.append(strip + jnp.concatenate(rims, 0))
    patches = lax.all_to_all(patches, ("chip", "core", "tx"), 0, 0, tiled=True)
    side_a = lax.ppermute(strips[0], "tx", swaps(cols, 0))
    side_b = lax.ppermute(strips[1], "tx", swaps(cols, 1))
    x1, x2, x3, x4, wide, chosen = pl.pallas_call(
        lambda *refs: rims_kernel(cols, *refs),
        out_shape=levels
        + [halves(2 * LANES, 6 * LANES)]
        + [floats(BANDS, ROWS[0], LANES)],
        in_specs=[VMEM] * 11,
        out_specs=[VMEM] * 6,
        scratch_shapes=[scratch(STRIP, LANES)],
        compiler_params=PARAMS,
        name="add_rims",
    )(x1, x2, x3, x4, got_a, got_b, side_a, inner, tile, s0, scale)
    coarse = pl.pallas_call(
        lambda *refs: coarse_kernel(rows, cols, *refs),
        out_shape=floats(PLANES, ROWS[4], LANES),
        in_specs=[VMEM] * 3,
        out_specs=VMEM,
        scratch_shapes=[
            scratch(PLANES, LANES),
            scratch(PLANES * 8, LANES),
            scratch(PLANES, 8, LANES),
        ],
        compiler_params=PARAMS,
        name="coarse_levels",
    )(patches, inner, top)
    return pl.pallas_call(
        lambda *refs: finish_kernel(rows, cols, *refs),
        out_shape=floats(BANDS, ROWS[0], LANES),
        in_specs=[VMEM] * 11,
        out_specs=VMEM,
        scratch_shapes=[
            *[scratch(PLANES * ROWS[level], LANES) for level in (1, 2, 3, 4)],
            scratch(STRIP, LANES),
            *[scratch(INNER, ROWS[level], LANES) for level in (1, 2, 3, 4, 0, 1, 2, 3)],
            scratch(PLANES // 4 * ROWS[4] + BANDS * (ROWS[1] + ROWS[2] + ROWS[3]), LANES),
            *[scratch(BANDS, ROWS[level], LANES) for level in (4, 3, 2, 1)],
            scratch(BANDS, ROWS[0], LANES),
        ],
        compiler_params=PARAMS,
        name="finish",
    )(s0, chosen, x1, x2, x3, x4, side_b, inner, tile, wide, coarse)


def solution(mesh):
    groups, rows, cols = mesh.devices.shape
    devices = mesh.devices.reshape(groups, rows // CORES, CORES, cols)
    split = Mesh(devices, ("grp", "chip", "core", "tx"))
    down = ("grp", "chip", "core")
    return jax.shard_map(
        shards,
        mesh=split,
        in_specs=(P(None, None, down, "tx"), P(), P(down, "tx")),
        out_specs=P(None, down, "tx"),
        check_vma=False,
    )
```

```python
import jax
import jax.numpy as jnp
from jax import lax
from jax.experimental import pallas as pl
from jax.experimental.pallas import tpu as pltpu
from jax.sharding import Mesh, PartitionSpec as P

EXPOSURES = 4
BANDS = 3
INNER = EXPOSURES * BANDS
PLANES = INNER + EXPOSURES
LANES = 128
HALF = LANES // 2

SIDE = (64, 32, 16, 8, 4, 2, 1)
WIDE = (128, 64, 32, 16, 8, 4, 2)
ROWS = (64, 40, 24, 16, 8, 8, 8)
PAIRS = (32, 20, 12, 6, 4)
SLOTS = 3
MOVES = (
    (1, 0, 0, 0), (1, 1, 1, 0),
    (2, 0, 0, 66), (2, 1, 1, 66), (2, 2, 2, 0),
    (3, 0, 2, 35), (3, 1, 2, 54), (3, 2, 2, 73),
    (4, 0, 2, 92), (4, 1, 2, 103), (4, 2, 2, 114),
)
STRIP_AT = (0, 0, 0, 24, 40)
STRIP = 48
PITCH_5 = 8
PITCH_6 = 6
AT_6 = 40
RIMS = 2 * SLOTS + 6
CORES = 2
REACH_ROWS = 3
REACH_COLS = 2

f32 = jnp.float32
bf16 = jnp.bfloat16


def iota(shape, dim):
    return lax.broadcasted_iota(jnp.int32, shape, dim)


def reduce_weights(first):
    tap = iota((LANES, LANES), 0) - 2 * iota((LANES, LANES), 1) + first
    near = jnp.where((tap == 1) | (tap == 3), 0.25, 0.0)
    ends = jnp.where((tap == 0) | (tap == 4), 0.0625, 0.0)
    weights = jnp.where(tap == 2, 0.375, near + ends).astype(bf16)
    return jnp.concatenate([weights, weights], 0)


def expand_taps(source, target):
    away = 2 * source - target
    even = jnp.where(away == 0, 0.75, 0.0) + jnp.where((away == 2) | (away == -2), 0.125, 0.0)
    odd = jnp.where((away == 1) | (away == -1), 0.5, 0.0)
    return jnp.where(jnp.bitwise_and(target, 1) == 1, odd, even)


def expand_weights(first):
    shape = (LANES, LANES)
    weights = expand_taps(iota(shape, 0) - 1, iota(shape, 1) - first).astype(bf16)
    return jnp.concatenate([weights, weights], 0)


def split_dot(values, weights):
    high = values.astype(bf16)
    low = (values - high.astype(f32)).astype(bf16)
    return jnp.dot(jnp.concatenate([high, low], 1), weights, preferred_element_type=f32)


def in_slab(level, row, col, rows, cols):
    shape = (ROWS[level], LANES)
    along, across = iota(shape, 0), iota(shape, 1)
    first, last = 1 - SIDE[level] * row, 1 + SIDE[level] * (rows - row)
    left, right = 1 - WIDE[level] * col, 1 + WIDE[level] * (cols - col)
    return (along >= first) & (along < last) & (across >= left) & (across < right)


def expand_rows(source, target, count):
    before = source[:, 0:count, :]
    centre = source[:, 1 : count + 1, :]
    after = source[:, 2 : count + 2, :]
    target[:, pl.ds(0, count, stride=2), :] = (before + centre) * 0.5
    target[:, pl.ds(1, count, stride=2), :] = centre * 0.75 + (before + after) * 0.125


def expand_rows_tile(source, target, count):
    before = source[:, 0:count, :]
    centre = source[:, 1 : count + 1, :]
    after = source[:, 2 : count + 2, :]
    target[:, pl.ds(0, count, stride=2), :] = centre * 0.75 + (before + after) * 0.125
    target[:, pl.ds(1, count, stride=2), :] = (centre + after) * 0.5


def plane_of(level, p):
    return pl.ds(p * ROWS[level], ROWS[level])


def line_of(level, line):
    return pl.ds(line, PLANES, stride=ROWS[level])


def patch_places(shape, dim):
    lane = jnp.bitwise_and(iota(shape, dim), HALF - 1)
    row_5, col_5 = lax.shift_right_logical(lane, 3), jnp.bitwise_and(lane, PITCH_5 - 1)
    past = lane - AT_6
    row_6 = lax.shift_right_arithmetic(past * 43, 8)
    col_6 = past - PITCH_6 * row_6
    is_5 = (lane < AT_6) & (col_5 < WIDE[5] + 3)
    is_6 = (lane >= AT_6) & (col_6 < WIDE[6] + 3)
    return (is_5, row_5, col_5), (is_6, row_6, col_6)


def place_of(cores):
    return lax.axis_index("chip") * cores + lax.axis_index("core"), lax.axis_index("tx")


def partial_kernel(
    rows, cols, images, gains, labels,
    s0, scale, x1, x2, x3, x4, send_a, send_b, strip_a, strip_b, patches,
    s1, s2, s3, s4, s5, y5, y6, across, label, gain, first_part, other_part, low, high, slots, done, sent,
):
    row, col = place_of(CORES)
    copies = [
        pltpu.make_async_copy(labels, label, done.at[EXPOSURES]),
        pltpu.make_async_copy(gains, gain, done.at[EXPOSURES + 1]),
    ]
    for e in range(EXPOSURES):
        planes = pl.ds(e * BANDS, BANDS)
        copies.append(pltpu.make_async_copy(images.at[planes], s0.at[planes, pl.ds(8, 64)], done.at[e]))
    for copy in copies:
        copy.start()
    s0[:, 0:8, :] = jnp.zeros((PLANES, 8, LANES), f32)
    s0[:, 72:88, :] = jnp.zeros((PLANES, 16, LANES), f32)
    slots[...] = jnp.zeros(slots.shape, f32)
    for store in (s1, s2, s3, s4, s5):
        depth = store.shape[1]
        store[:, 0:8, :] = jnp.zeros((PLANES, 8, LANES), f32)
        store[:, depth - 8 : depth, :] = jnp.zeros((PLANES, 8, LANES), f32)
    edge_weights, weights = reduce_weights(4), reduce_weights(3)

    def reduce_rows(source, level, first, p, scale=None):
        count = ROWS[level]
        tap = [source[p, pl.ds(first + k, count, stride=2), :] for k in range(5)]
        total = tap[2] * 0.375 + (tap[1] + tap[3]) * 0.25 + (tap[0] + tap[4]) * 0.0625
        across[plane_of(level, p), :] = total if scale is None else total * scale

    def reduce_columns(level, weights, store, out):
        count = ROWS[level]
        result = split_dot(across[0 : PLANES * count, :], weights).reshape(PLANES, count, LANES)
        result = jnp.where(in_slab(level, row, col, rows, cols)[None], result, 0.0)
        out[...] = result.reshape(PLANES * count, LANES)
        if store is not None:
            store[:, 8 : 8 + count, :] = result

    copies[0].wait()
    for e in range(EXPOSURES):
        s0[INNER + e, 8:72, :] = jnp.where(label[...] == e, 1.0, 0.0)
        reduce_rows(s0, 1, 4, INNER + e)
    copies[1].wait()
    for p in range(INNER):
        scale[p] = jnp.full((8, LANES), gain[p // BANDS, p % BANDS], f32)
    for e in range(EXPOSURES):
        copies[2 + e].wait()
        for b in range(BANDS):
            reduce_rows(s0, 1, 4, e * BANDS + b, gain[e, b])
    reduce_columns(1, edge_weights, s1, x1)
    stores = ((2, s1, s2, x2), (3, s2, s3, x3), (4, s3, s4, x4), (5, s4, s5, y5), (6, s5, None, y6))
    for level, source, store, out in stores:
        for p in range(PLANES):
            reduce_rows(source, level, 5, p)
        reduce_columns(level, weights, store, out)

    patch = jnp.zeros((PLANES, LANES), f32)
    for k in range(SIDE[5] + 3):
        line = y5[line_of(5, k), :]
        patch = patch + (pltpu.roll(line, PITCH_5 * k, 1) if k else line)
    for k in range(SIDE[6] + 3):
        patch = patch + pltpu.roll(y6[line_of(6, k), :], AT_6 + PITCH_6 * k, 1)
    patch = patch[0:8, :] + pltpu.roll(patch[8:16, :], HALF, 1)
    width = cols + 2 * REACH_COLS
    (is_5, row_5, col_5), (is_6, row_6, col_6) = patch_places((8, LANES), 1)
    downs = range(-REACH_ROWS, REACH_ROWS + 1)
    overs = range(-REACH_COLS, REACH_COLS + 1)
    rows_5 = {k: is_5 & (row_5 >= -2 * k) & (row_5 < SIDE[5] + 3 - 2 * k) for k in downs}
    rows_6 = {k: is_6 & (row_6 >= -k) & (row_6 < SIDE[6] + 3 - k) for k in downs}
    cols_5 = {k: (col_5 >= -4 * k) & (col_5 < WIDE[5] + 3 - 4 * k) for k in overs}
    cols_6 = {k: (col_6 >= -2 * k) & (col_6 < WIDE[6] + 3 - 2 * k) for k in overs}
    for down in range(-REACH_ROWS, REACH_ROWS + 1):
        for over in range(-REACH_COLS, REACH_COLS + 1):
            held = rows_6[down] & cols_6[over]
            away = -(PITCH_6 * down + 2 * over) % LANES
            block = jnp.where(held, pltpu.roll(patch, away, 1) if away else patch, 0.0)
            if abs(down) < REACH_ROWS and abs(over) < REACH_COLS:
                held = rows_5[down] & cols_5[over]
                away = -(2 * PITCH_5 * down + 4 * over) % LANES
                block = jnp.where(held, pltpu.roll(patch, away, 1) if away else patch, block)
            slots[(row + (down + REACH_ROWS)) * width + col + (over + REACH_COLS)] = block
    sends = []
    for r in range(rows):
        source = slots.at[pl.ds((r + REACH_ROWS) * width + REACH_COLS, cols)]
        sends.append(pltpu.make_async_copy(source, patches.at[pl.ds(r * cols, cols)], sent.at[r]))
        sends[r].start()

    levels = (None, x1, x2, x3, x4)
    odd = jnp.bitwise_and(col, 1) == 1
    for level in range(1, 5):
        count, wide = ROWS[level], WIDE[level]
        lane = iota((count, LANES), 1)
        before = jnp.zeros((count, LANES), f32)
        after = jnp.zeros((count, LANES), f32)
        for p in range(PLANES):
            plane = levels[level][plane_of(level, p), :]
            plane = pltpu.roll(plane, 3 * p, 1) if p else plane
            before = jnp.where((lane >= 3 * p) & (lane < 3 * p + 3), plane, before)
            after = jnp.where((lane >= wide + 3 * p) & (lane < wide + 3 * p + 3), plane, after)
        if level == 1:
            after = pltpu.roll(after, HALF, 1)
        else:
            before = pltpu.roll(before, HALF, 1)
            after = pltpu.roll(after, HALF - wide, 1)
        before = jnp.where(col == 0, 0.0, before)
        after = jnp.where(col == cols - 1, 0.0, after)
        for k, strip in enumerate((jnp.where(odd, before, after), jnp.where(odd, after, before))):
            if level == 1:
                first_part[k] = strip
            else:
                other_part[k, pl.ds(STRIP_AT[level], count), :] = strip
    for k, strip in enumerate((strip_a, strip_b)):
        strip[0:5] = (first_part[k] + other_part[k, 0:40, :]).reshape(5, 8, LANES)
        strip[5] = other_part[k, 40:48, :]

    low[...] = jnp.zeros((RIMS, 8, LANES), f32)
    high[...] = jnp.zeros((RIMS, 8, LANES), f32)
    for rim, at in ((low, (0,) * 5), (high, SIDE)):
        slots = [None] * SLOTS
        for level, line, slot, lane in MOVES:
            values = levels[level][line_of(level, at[level] + line), :]
            values = pltpu.roll(values, lane, 1) if lane else values
            slots[slot] = values if slots[slot] is None else slots[slot] + values
        for k in range(SLOTS):
            rim[2 * k : 2 * k + 2] = slots[k].reshape(2, 8, LANES)
    for k in range(2):
        at = 2 * SLOTS + 3 * k
        low[at, 0:3, :] = other_part[k, 0:3, :]
        low[at + 1, 0:3, :] = other_part[k, 24:27, :]
        low[at + 1, 0:2, :] += first_part[k, 0:2, :]
        low[at + 2, 4:7, :] = other_part[k, 40:43, :]
        high[at, 0:3, :] = other_part[k, 16:19, :]
        high[at, 0:2, :] += first_part[k, 32:34, :]
        high[at + 1, 0:3, :] = other_part[k, 32:35, :]
        high[at + 2, 0:3, :] = other_part[k, 44:47, :]
    odd = jnp.bitwise_and(row, 1) == 1
    downward = jnp.where(row == 0, 0.0, low[...])
    upward = jnp.where(row == rows - 1, 0.0, high[...])
    send_a[...] = jnp.where(odd, downward, upward)
    send_b[...] = jnp.where(odd, upward, downward)
    for copy in sends:
        copy.wait()


def tables_kernel(rims, inner, tile, top, send):
    send[...] = rims[...]
    inner[...] = expand_weights(1)
    tile[...] = expand_weights(0)
    _, (is_6, row_6, col_6) = patch_places((LANES, LANES), 0)
    (is_5, row_5, col_5), _ = patch_places((LANES, LANES), 1)
    low = (iota((LANES, LANES), 0) < HALF) & (iota((LANES, LANES), 1) < HALF)
    taps = expand_taps(row_6 - 1, row_5 - 1) * expand_taps(col_6 - 1, col_5 - 1)
    weights = jnp.where(is_5 & is_6 & low, taps, 0.0).astype(bf16)
    top[...] = jnp.concatenate([weights, weights], 0)


def add_side(totals, parts, strip, on_left, held):
    held[...] = strip[...].reshape(STRIP, LANES)
    for level in range(1, 5):
        count, wide, at = ROWS[level], WIDE[level], STRIP_AT[level]
        lane = iota((count, LANES), 1)
        start = 0 if level == 1 else HALF
        rim = held[at : at + count, :]
        rim = jnp.where((lane >= start) & (lane < start + 3 * PLANES), rim, 0.0)
        rim = jnp.where(on_left, rim, pltpu.roll(rim, wide, 1))
        first = jnp.where(on_left, 0, wide)
        inside = (lane >= first) & (lane < first + 3)
        for p in range(PLANES):
            away = -(start + 3 * p) % LANES
            place = plane_of(level, p)
            part = jnp.where(inside, pltpu.roll(rim, away, 1) if away else rim, 0.0)
            totals[level][place, :] = parts[level][place, :] + part


def rims_kernel(
    cols, x1, x2, x3, x4, got_a, got_b, side, inner, tile, s0, scale,
    t1, t2, t3, t4, wide, chosen, held,
):
    col = lax.axis_index("tx")
    step = inner[0:LANES, :].astype(f32)

    def masked(level):
        across = iota((LANES, LANES), 1)
        first, last = 1 - WIDE[level] * col, 1 + WIDE[level] * (cols - col)
        return jnp.where((across >= first) & (across < last), step, 0.0).astype(bf16)

    def halved(weights):
        high = weights.astype(bf16)
        return high, (weights - high.astype(f32)).astype(bf16)

    second = jnp.dot(masked(1), tile[0:LANES, :], preferred_element_type=f32).astype(bf16)
    high, low = halved(jnp.dot(masked(2), second, preferred_element_type=f32))
    both = jnp.concatenate([masked(3), masked(3)], 1)
    fourth = jnp.dot(both, jnp.concatenate([high, low], 0), preferred_element_type=f32)
    high_4, low_4 = halved(fourth)
    weights = jnp.concatenate([high_4, high, second, tile[0:LANES, :], low_4, low], 1)
    wide[...] = jnp.concatenate([weights, weights], 0)
    for b in range(BANDS):
        total = jnp.zeros((ROWS[0], LANES), f32)
        for e in range(EXPOSURES):
            p = e * BANDS + b
            total = total + s0[INNER + e, 8:72, :] * (s0[p, 8:72, :] * scale[p, 0:1, :])
        chosen[b] = total

    row_odd = lax.axis_index("core") == 1
    col_odd = jnp.bitwise_and(lax.axis_index("tx"), 1) == 1
    totals = (None, t1, t2, t3, t4)
    add_side(totals, (None, x1, x2, x3, x4), side, col_odd, held)
    rims_a, rims_b = got_a[0 : 2 * SLOTS], got_b[0 : 2 * SLOTS]
    below = jnp.where(row_odd, rims_a, rims_b).reshape(SLOTS, PLANES, LANES)
    above = jnp.where(row_odd, rims_b, rims_a).reshape(SLOTS, PLANES, LANES)
    for rim, at in ((below, (0,) * 5), (above, SIDE)):
        for level, line, slot, lane in MOVES:
            values = rim[slot]
            values = pltpu.roll(values, LANES - lane, 1) if lane else values
            totals[level][line_of(level, at[level] + line), :] += values


def finish_kernel(
    rows, cols, s0, chosen, x1, x2, x3, x4, side, inner, tile, wide, coarse, out,
    t1, t2, t3, t4, held, u1, u2, u3, u4, d0, d1, d2, d3, bands, c4, c3, c2, c1, spread,
):
    row, col = place_of(CORES)
    col_odd = jnp.bitwise_and(col, 1) == 1
    totals = (None, t1, t2, t3, t4)
    add_side(totals, (None, x1, x2, x3, x4), side, jnp.logical_not(col_odd), held)

    values = [totals[level][0 : INNER * ROWS[level], :] for level in (4, 3, 2)]
    values = split_dot(jnp.concatenate(values, 0), inner[...])
    at = 0
    for level, store in ((4, u4), (3, u3), (2, u2)):
        count = INNER * ROWS[level]
        store[...] = values[at : at + count, :].reshape(INNER, ROWS[level], LANES)
        at += count
    values = split_dot(t1[0 : INNER * ROWS[1], :], tile[...])
    u1[...] = values.reshape(INNER, ROWS[1], LANES)
    d3[...] = jnp.zeros((INNER, ROWS[3], LANES), f32)
    inside = in_slab(4, row, col, rows, cols)
    for b in range(BANDS):
        total = coarse[INNER + b]
        for e in range(EXPOSURES):
            p = e * BANDS + b
            laplace = t4[plane_of(4, p), :] - coarse[p]
            total = total + t4[plane_of(4, INNER + e), :] * laplace
        bands[b * ROWS[4] : (b + 1) * ROWS[4], :] = jnp.where(inside, total, 0.0)
    bands[BANDS * ROWS[4] : PLANES // 4 * ROWS[4], :] = jnp.zeros((ROWS[4], LANES), f32)
    at = PLANES // 4 * ROWS[4]
    for level, source, spread_out in ((3, u4, d3), (2, u3, d2), (1, u2, d1)):
        expand_rows(source, spread_out, PAIRS[level])
        here = totals[level]
        for b in range(BANDS):
            total = jnp.zeros((ROWS[level], LANES), f32)
            for e in range(EXPOSURES):
                p = e * BANDS + b
                laplace = here[plane_of(level, p), :] - spread_out[p]
                total = total + here[plane_of(level, INNER + e), :] * laplace
            bands[at : at + ROWS[level], :] = total
            at += ROWS[level]
    values = split_dot(bands[...], wide[...])
    at, parts = 0, {}
    for k, level in enumerate((4, 3, 2, 1)):
        count = BANDS * ROWS[level]
        part = values[at : at + count, k * LANES : (k + 1) * LANES]
        if k < 2:
            part = part + values[at : at + count, (k + 4) * LANES : (k + 5) * LANES]
        parts[level] = part.reshape(BANDS, ROWS[level], LANES)
        at += PLANES // 4 * ROWS[4] if level == 4 else count
    c4[...] = parts[4]
    for level, store in ((3, c3), (2, c2), (1, c1)):
        store[...] = parts[level]
    expand_rows_tile(u1, d0, PAIRS[0])
    for b in range(BANDS):
        total = chosen[b]
        for e in range(EXPOSURES):
            total = total - s0[INNER + e, 8:72, :] * d0[e * BANDS + b]
        out[b] = total
    spread[:, 0 : ROWS[3], :] = jnp.zeros((BANDS, ROWS[3], LANES), f32)
    for level, source, target in ((3, c4, c3), (2, c3, c2), (1, c2, c1)):
        depth = ROWS[level]
        expand_rows(source, spread, PAIRS[level])
        along = iota((depth, LANES), 0)
        first, last = 1 - SIDE[level] * row, 1 + SIDE[level] * (rows - row)
        inside = (along >= first) & (along < last)
        for b in range(BANDS):
            target[b] = jnp.where(inside, target[b] + spread[b, 0:depth, :], 0.0)
    expand_rows_tile(c1, spread, PAIRS[0])
    out[...] = out[...] + spread[...]


def coarse_kernel(rows, cols, patches, inner, top_weights, spread, v5, window, across):
    row, col = place_of(CORES)
    total = patches[0]
    for k in range(1, rows * cols):
        total = total + patches[k]
    lane = iota((PLANES, LANES), 1)
    total = jnp.concatenate([total, pltpu.roll(total, HALF, 1)], 0)
    v5[...] = jnp.where(lane < HALF, total, 0.0)

    def blend(less):
        total = None
        for e in range(EXPOSURES):
            part = v5[e * BANDS : (e + 1) * BANDS, :]
            if less is not None:
                part = part - less[e * BANDS : (e + 1) * BANDS, :]
            part = part * v5[INNER + e : INNER + e + 1, :]
            total = part if total is None else total + part
        return total

    window[0:PLANES, :] = v5[...]
    window[INNER : INNER + BANDS, :] = blend(None)
    less = split_dot(window[0:PLANES, :], top_weights[...])
    (is_5, row_5, col_5), _ = patch_places((BANDS, LANES), 1)
    along, aside = row_5 + (SIDE[5] * row - 1), col_5 + (WIDE[5] * col - 1)
    held = is_5 & (along >= 0) & (along < SIDE[5] * rows) & (aside >= 0) & (aside < WIDE[5] * cols)
    v5[INNER : INNER + BANDS, :] = jnp.where(held, blend(less) + less[INNER : INNER + BANDS, :], 0.0)

    window[...] = jnp.zeros((PLANES * 8, LANES), f32)
    for k in range(SIDE[5] + 3):
        line = v5[...]
        line = pltpu.roll(line, LANES - PITCH_5 * k, 1) if k else line
        window[line_of(5, k), :] = jnp.where(lane < WIDE[5] + 3, line, 0.0)

    across[:, 0:8, :] = split_dot(window[...], inner[...]).reshape(PLANES, 8, LANES)
    expand_rows(across, spread, PAIRS[4])


VMEM = pl.BlockSpec(memory_space=pltpu.VMEM)
SMEM = pl.BlockSpec(memory_space=pltpu.SMEM)
HBM = pl.BlockSpec(memory_space=pltpu.HBM)
PARAMS = pltpu.CompilerParams(vmem_limit_bytes=32 * 1024 * 1024)


def floats(*shape):
    return jax.ShapeDtypeStruct(shape, f32)


def halves(*shape):
    return jax.ShapeDtypeStruct(shape, bf16)


def scratch(*shape):
    return pltpu.VMEM(shape, f32)


def swaps(size, first):
    return [(i, ((i - first) ^ 1) + first) for i in range(first, size - first)]


def shards(images, gains, labels):
    chips, cols = lax.axis_size("chip"), lax.axis_size("tx")
    rows = CORES * chips
    images = images.reshape(INNER, ROWS[0], LANES)
    pinned = [pltpu.with_memory_space_constraint(x, pltpu.HBM) for x in (images, gains, labels)]
    levels = [floats(PLANES * ROWS[level], LANES) for level in range(1, 5)]
    s0, scale, x1, x2, x3, x4, send_a, send_b, strip_a, strip_b, patches = pl.pallas_call(
        lambda *refs: partial_kernel(rows, cols, *refs),
        out_shape=[
            floats(PLANES, 88, LANES),
            floats(INNER, 8, LANES),
            *levels,
            floats(RIMS, 8, LANES),
            floats(RIMS, 8, LANES),
            floats(6, 8, LANES),
            floats(6, 8, LANES),
            floats(rows * cols, 8, LANES),
        ],
        in_specs=[HBM] * 3,
        out_specs=[VMEM] * 10 + [HBM],
        scratch_shapes=[
            scratch(PLANES, 56, LANES),
            scratch(PLANES, 40, LANES),
            scratch(PLANES, 24, LANES),
            scratch(PLANES, 24, LANES),
            scratch(PLANES, 24, LANES),
            scratch(PLANES * 8, LANES),
            scratch(PLANES * 8, LANES),
            scratch(PLANES * ROWS[1], LANES),
            pltpu.VMEM((ROWS[0], LANES), jnp.int32),
            pltpu.SMEM((EXPOSURES, BANDS), f32),
            scratch(2, ROWS[1], LANES),
            scratch(2, STRIP, LANES),
            scratch(RIMS, 8, LANES),
            scratch(RIMS, 8, LANES),
            scratch((rows + 2 * REACH_ROWS) * (cols + 2 * REACH_COLS), 8, LANES),
            pltpu.SemaphoreType.DMA((EXPOSURES + 2,)),
            pltpu.SemaphoreType.DMA((rows,)),
        ],
        compiler_params=PARAMS,
        name="partial_levels",
    )(*pinned)
    got_b = lax.ppermute(send_b, ("chip", "core"), swaps(rows, 1))
    inner, tile, top, send_a = pl.pallas_call(
        tables_kernel,
        out_shape=[halves(2 * LANES, LANES)] * 3 + [floats(RIMS, 8, LANES)],
        in_specs=[VMEM],
        out_specs=[VMEM] * 4,
        compiler_params=PARAMS,
        name="expand_tables",
    )(send_a)
    got_a = lax.ppermute(send_a, "core", swaps(CORES, 0))
    odd = lax.axis_index("core") == 1
    rims_a, rims_b = got_a[2 * SLOTS :], got_b[2 * SLOTS :]
    below, above = jnp.where(odd, rims_a, rims_b), jnp.where(odd, rims_b, rims_a)
    strips = []
    for k, strip in enumerate((strip_a, strip_b)):
        low, high = below[3 * k : 3 * k + 3], above[3 * k : 3 * k + 3]
        none = jnp.zeros((1, 8, LANES), f32)
        rims = [low[0:1], none, high[0:1], low[1:2], high[1:2], low[2:3] + high[2:3]]
        strips.append(strip + jnp.concatenate(rims, 0))
    patches = lax.all_to_all(patches, ("chip", "core", "tx"), 0, 0, tiled=True)
    side_a = lax.ppermute(strips[0], "tx", swaps(cols, 0))
    side_b = lax.ppermute(strips[1], "tx", swaps(cols, 1))
    x1, x2, x3, x4, wide, chosen = pl.pallas_call(
        lambda *refs: rims_kernel(cols, *refs),
        out_shape=levels
        + [halves(2 * LANES, 6 * LANES)]
        + [floats(BANDS, ROWS[0], LANES)],
        in_specs=[VMEM] * 11,
        out_specs=[VMEM] * 6,
        scratch_shapes=[scratch(STRIP, LANES)],
        compiler_params=PARAMS,
        name="add_rims",
    )(x1, x2, x3, x4, got_a, got_b, side_a, inner, tile, s0, scale)
    coarse = pl.pallas_call(
        lambda *refs: coarse_kernel(rows, cols, *refs),
        out_shape=floats(PLANES, ROWS[4], LANES),
        in_specs=[VMEM] * 3,
        out_specs=VMEM,
        scratch_shapes=[
            scratch(PLANES, LANES),
            scratch(PLANES * 8, LANES),
            scratch(PLANES, 8, LANES),
        ],
        compiler_params=PARAMS,
        name="coarse_levels",
    )(patches, inner, top)
    return pl.pallas_call(
        lambda *refs: finish_kernel(rows, cols, *refs),
        out_shape=floats(BANDS, ROWS[0], LANES),
        in_specs=[VMEM] * 11,
        out_specs=VMEM,
        scratch_shapes=[
            *[scratch(PLANES * ROWS[level], LANES) for level in (1, 2, 3, 4)],
            scratch(STRIP, LANES),
            *[scratch(INNER, ROWS[level], LANES) for level in (1, 2, 3, 4, 0, 1, 2, 3)],
            scratch(PLANES // 4 * ROWS[4] + BANDS * (ROWS[1] + ROWS[2] + ROWS[3]), LANES),
            *[scratch(BANDS, ROWS[level], LANES) for level in (4, 3, 2, 1)],
            scratch(BANDS, ROWS[0], LANES),
        ],
        compiler_params=PARAMS,
        name="finish",
    )(s0, chosen, x1, x2, x3, x4, side_b, inner, tile, wide, coarse)


def solution(mesh):
    groups, rows, cols = mesh.devices.shape
    devices = mesh.devices.reshape(groups, rows // CORES, CORES, cols)
    split = Mesh(devices, ("grp", "chip", "core", "tx"))
    down = ("grp", "chip", "core")
    return jax.shard_map(
        shards,
        mesh=split,
        in_specs=(P(None, None, down, "tx"), P(), P(down, "tx")),
        out_specs=P(None, down, "tx"),
        check_vma=False,
    )
```
